32 devices in a mesh: dp: 8 (over z, y), tensor: 4 (over x, core).
Axes of the slice: x: 2, y: 2, z: 4, core: 2. Of those that a mesh axis runs over, the one named last changes fastest.
Arguments:
- tokens: bfloat16 [8192, 2048], P(('dp', 'tensor')), may hold values from -6 to 6
- cotangent: bfloat16 [8192, 2048], P(('dp', 'tensor')), may hold values from -6 to 6
- doc_lengths: int32 [8, 4], P('dp'), may hold values from 1 to 512, 1024 in all within a row
- key_weights: float32 [2, 2048, 2048], P(None, 'dp', 'tensor'), may hold values from -0.125 to 0.125
- value_weights: float32 [2, 2048, 3456], P(None, 'dp', 'tensor'), may hold values from -0.125 to 0.125
- out_weights: float32 [3456, 2048], P('tensor', 'dp'), may hold values from -0.109375 to 0.109375
- up_weights: float32 [2, 2048, 3456], P(None, 'dp', 'tensor'), may hold values from -0.125 to 0.125
- down_weights: float32 [3456, 2048], P('tensor', 'dp'), may hold values from -0.109375 to 0.109375
- key_momentum: float32 [2, 2048, 2048], P(None, 'dp', 'tensor'), as said below
- value_momentum: float32 [2, 2048, 3456], P(None, 'dp', 'tensor'), as said below
- out_momentum: float32 [3456, 2048], P('tensor', 'dp'), as said below
- up_momentum: float32 [2, 2048, 3456], P(None, 'dp', 'tensor'), as said below
- down_momentum: float32 [3456, 2048], P('tensor', 'dp'), as said below
- norm_params: float32 [11008], P(('dp', 'tensor')), may hold values from -2 to 2, as said below
- norm_first: float32 [11008], P(('dp', 'tensor')), as said below
- norm_second: float32 [11008], P(('dp', 'tensor')), may hold values from 204 to 1638
Outputs:
- result: bfloat16 [8192, 2048], P(('dp', 'tensor'))
- token_grad: float32 [8192, 2048], P(('dp', 'tensor'))
- new_key_momentum: float32 [2, 2048, 2048], P(None, 'dp', 'tensor')
- new_value_momentum: float32 [2, 2048, 3456], P(None, 'dp', 'tensor')
- new_out_momentum: float32 [3456, 2048], P('tensor', 'dp')
- new_up_momentum: float32 [2, 2048, 3456], P(None, 'dp', 'tensor')
- new_down_momentum: float32 [3456, 2048], P('tensor', 'dp')
- new_key_weights: float32 [2, 2048, 2048], P(None, 'dp', 'tensor')
- new_value_weights: float32 [2, 2048, 3456], P(None, 'dp', 'tensor')
- new_out_weights: float32 [3456, 2048], P('tensor', 'dp')
- new_up_weights: float32 [2, 2048, 3456], P(None, 'dp', 'tensor')
- new_down_weights: float32 [3456, 2048], P('tensor', 'dp')
- new_norm_first: float32 [11008], P(('dp', 'tensor'))
- new_norm_second: float32 [11008], P(('dp', 'tensor'))
- new_norm_params: float32 [11008], P(('dp', 'tensor'))
The draws below stay inside these ranges and needn't reach their ends.
Inputs may be any that keep to these rules, and one draw needn't show every extreme that they name: `doc_lengths`: each row holds the lengths of the documents packed in order into one sequence; they sum to 1024, and the longest of each row is exactly 512. `key_momentum`: independent entries of zero mean, within six times their scale. `value_momentum`: independent entries of zero mean, within six times their scale. `out_momentum`: independent entries of zero mean, within six times their scale. `up_momentum`: independent entries of zero mean, within six times their scale. `down_momentum`: independent entries of zero mean, within six times their scale. `norm_first`: independent entries of zero mean, within six times their scale. `norm_params`: gains lie in 0.75 to 1.25; the bias entries are independent and of zero mean.
All inputs are finite; a program needn't handle non-finite values.
Results may differ from the reference program's by a relative error of at most 0.02.
Values may be sent and summed in bfloat16 or wider, within the bound.
No kernel may reach another device: no remote copies, remote signals or barrier semaphores. Data moves between devices by JAX's collectives and lax.ppermute only.
A program may use at most 256 MiB of HBM per device.

```python
import math
import jax
import jax.numpy as jnp
import numpy as np
from jax import lax

D = 2048
H = 8
KEY_HEAD_SIZE = 256
DV = 432
FF = 3456
LEN = 1024
DOCS = 4
NS_ITERS = 5
STEP = 10
SEQS = 8
TOKENS = 8192
KEYS = 2048
VAL = 3456
NORMS = 11008
SPLITS = 4


def scaled_normal(key, shape, factor):
    sample = jnp.clip(jax.random.normal(key, shape, jnp.float32), -6.0, 6.0)
    return factor * jnp.sqrt(jnp.float32(TOKENS)) * sample


def draw_key_momentum(key, part):
    key = jax.random.fold_in(key, 11)
    return scaled_normal(key, (2, D, KEYS), 0.5)


def draw_value_momentum(key, part):
    key = jax.random.fold_in(key, 13)
    return scaled_normal(key, (2, D, VAL), 0.5)


def draw_out_momentum(key, part):
    key = jax.random.fold_in(key, 17)
    return scaled_normal(key, (VAL, D), 0.5)


def draw_up_momentum(key, part):
    key = jax.random.fold_in(key, 19)
    return scaled_normal(key, (2, D, FF), 0.5)


def draw_down_momentum(key, part):
    key = jax.random.fold_in(key, 23)
    return scaled_normal(key, (FF, D), 0.5)


def draw_norm_first(key, part):
    key = jax.random.fold_in(key, 29)
    return scaled_normal(key, (NORMS,), 0.1)


def draw_norm_params(key, part):
    key = jax.random.fold_in(key, 31)
    gain_part = jax.random.uniform(key, (2 * D + VAL,), jnp.float32, 0.75, 1.25)
    biases = 0.3 * jnp.clip(jax.random.normal(jax.random.fold_in(key, 1), (VAL,), jnp.float32), -6.0, 6.0)
    return jnp.concatenate([gain_part, biases])


def levels(stream_key, extent, cuts, least, top_value):
    factor_of = 1.0
    for dim, blocks in cuts:
        heights = jax.random.uniform(jax.random.fold_in(jax.random.fold_in(stream_key, 6), dim), (blocks,), jnp.float32, least / len(cuts), top_value / len(cuts))
        factor_of = factor_of * jnp.repeat(jnp.exp(heights), extent[dim] // blocks).reshape((-1,) + (1,) * (len(extent) - 1 - dim))
    return factor_of


def length_profile(number_of, total, bound, skew):
    portions = [(1 << 20) // math.isqrt(grade ** skew) + 1 for grade in range(2, number_of + 1)]
    surplus, given = total - bound - (number_of - 1), [1] * (number_of - 1)
    while surplus > 0:
        candidates = [i for i in range(number_of - 1) if given[i] < bound]
        whole, left = sum([portions[i] for i in candidates]), surplus
        for i in candidates:
            addition = min(bound - given[i], max(1, left * portions[i] // whole), surplus)
            given[i] = given[i] + addition
            surplus = surplus - addition
    return np.array([bound] + given)


def uneven_parts(stream_key, amount, total, limit, slope):
    if amount == 2:
        one = jax.random.randint(stream_key, (), max(1, total - limit), min(limit, total - 1) + 1)
        return jnp.stack([one, total - one])
    lengths = jnp.asarray(length_profile(amount, total, limit, slope), jnp.int32)
    twos = (amount - 1) // 2
    donor, receiver = lengths[1:1 + 2 * twos:2], lengths[2:2 + 2 * twos:2]
    slack = jnp.minimum(donor - 1, limit - receiver)
    passed = jax.random.randint(jax.random.fold_in(stream_key, 1), (twos,), 0, 1 << 20) % (slack + 1)
    lengths = lengths.at[1:1 + 2 * twos:2].set(donor - passed).at[2:2 + 2 * twos:2].set(receiver + passed)
    return lengths[jax.random.permutation(jax.random.fold_in(stream_key, 2), amount)]


def normal_values(stream_key, shape, width, bound, shards=(), kind=jnp.bfloat16):
    level = levels(stream_key, shape, shards, -0.22, 0.18) if shards else 1.0
    values = jax.random.normal(stream_key, shape, jnp.float32) * width * level
    return jnp.minimum(jnp.maximum(values, -bound), bound).astype(kind)


def setup_inputs(seed: int = 0) -> dict:
    splits = jax.random.split(jax.random.key(seed), 17)
    return {
        "tokens": normal_values(splits[0], (TOKENS, D), 1.0, 6.0, ((0, 32),)),
        "cotangent": normal_values(splits[1], (TOKENS, D), 1.0, 6.0, ((0, 32),)),
        "doc_lengths": jax.vmap(lambda own: uneven_parts(own, DOCS, LEN, LEN // 2, 1))(jax.random.split(splits[2], SEQS)).reshape((SEQS, DOCS)).astype(jnp.int32),
        "key_weights": normal_values(splits[3], (2, D, KEYS), D ** -0.5, 0.125, ((1, 8), (2, 4)), jnp.float32),
        "value_weights": normal_values(splits[4], (2, D, VAL), D ** -0.5, 0.125, ((1, 8), (2, 4)), jnp.float32),
        "out_weights": normal_values(splits[5], (VAL, D), VAL ** -0.5, 0.109375, ((0, 4), (1, 8)), jnp.float32),
        "up_weights": normal_values(splits[6], (2, D, FF), D ** -0.5, 0.125, ((1, 8), (2, 4)), jnp.float32),
        "down_weights": normal_values(splits[7], (FF, D), FF ** -0.5, 0.109375, ((0, 4), (1, 8)), jnp.float32),
        "key_momentum": draw_key_momentum(jax.random.fold_in(splits[16], 71), 0),
        "value_momentum": draw_value_momentum(jax.random.fold_in(splits[16], 71), 0),
        "out_momentum": draw_out_momentum(jax.random.fold_in(splits[16], 71), 0),
        "up_momentum": draw_up_momentum(jax.random.fold_in(splits[16], 71), 0),
        "down_momentum": draw_down_momentum(jax.random.fold_in(splits[16], 71), 0),
        "norm_params": draw_norm_params(jax.random.fold_in(splits[16], 71), 0),
        "norm_first": draw_norm_first(jax.random.fold_in(splits[16], 71), 0),
        "norm_second": jnp.clip(jnp.exp(math.log(1638.0) - 2.0831113 * jax.random.uniform(splits[15], (NORMS,), jnp.float32) ** levels(splits[15], (NORMS,), ((0, 32),), -0.2, 0.2)), 204.0, 1638.0),
    }


@jax.custom_vjp
def low(v):
    return lax.optimization_barrier(v.astype(jnp.bfloat16)).astype(jnp.float32)

@jax.custom_vjp
def low_back(v):
    return v

def low_keep(v):
    return (low(v), None)

def low_pass(kept, grad):
    return (grad,)

def back_keep(v):
    return (v, None)

def back_low(kept, grad):
    return (low(grad),)
low.defvjp(low_keep, low_pass)
low_back.defvjp(back_keep, back_low)
highest_precision = lax.Precision.HIGHEST
eps_norm = 1e-05
group_floor = 1.0
ns_first = 3.4445
ns_second = -4.775
ns_third = 2.0315
momentum_decay = 0.95
muon_rate = 0.5
weight_decay = 0.1
beta_first = 0.9
beta_second = 0.95
adam_rate = 0.8
adam_eps = 1e-08

def matmul(left, right):
    return jnp.dot(left, right, precision=highest_precision, preferred_element_type=jnp.float32)

def root_norm(values):
    return values * lax.rsqrt(lax.optimization_barrier(jnp.mean(values * values, axis=-1, keepdims=True)) + eps_norm)

def decay_table(doc_ids):
    positions = jnp.arange(LEN)
    distance = positions[:, None] - positions[None, :]
    allowed = (doc_ids[:, None] == doc_ids[None, :]) & (distance >= 0)
    head_ids = jnp.arange(H).astype(jnp.float32)
    log_gamma = jnp.log(1.0 - jnp.exp2(-5.0 - head_ids))
    steps_back = jnp.maximum(distance, 0).astype(jnp.float32)
    return jnp.where(allowed[None], jnp.exp(log_gamma[:, None, None] * steps_back[None]), 0.0)

def layer_sequence(inputs, doc_ids, matrices, norms):
    w_query, w_key, w_value, w_gate, w_out, w_hidden, w_upper, w_down = matrices
    gain_one = norms[:D]
    gain_two = norms[D:2 * D]
    group_gain = norms[2 * D:2 * D + VAL]
    group_bias = norms[2 * D + VAL:]
    normed = low(root_norm(inputs) * gain_one)
    query_rows = low_back(low(matmul(normed, w_query))).reshape(LEN, H, KEY_HEAD_SIZE)
    key_matrix_rows = low_back(low(matmul(normed, w_key))).reshape(LEN, H, KEY_HEAD_SIZE)
    value_matrix_rows = low_back(low(matmul(normed, w_value))).reshape(LEN, H, DV)
    gate_pre = low_back(matmul(normed, w_gate))
    retention_scores = jnp.einsum('gzx,bzx->zgb', query_rows, key_matrix_rows, precision=highest_precision) * KEY_HEAD_SIZE ** (-0.5)
    reduced_weights = low(low_back(retention_scores) * decay_table(doc_ids))
    head_outputs = low_back(jnp.einsum('fsl,lfa->sfa', reduced_weights, value_matrix_rows, precision=highest_precision))
    centred = head_outputs - lax.optimization_barrier(jnp.mean(head_outputs, axis=-1, keepdims=True))
    group_hat = centred * lax.rsqrt(lax.optimization_barrier(jnp.mean(centred * centred, axis=-1, keepdims=True)) + group_floor)
    group_out = group_hat.reshape(LEN, VAL) * group_gain + group_bias
    mixed = low(jax.nn.silu(gate_pre) * group_out)
    middle = inputs + low_back(matmul(mixed, w_out))
    second = low(root_norm(middle) * gain_two)
    hidden_gate = low_back(matmul(second, w_hidden))
    hidden_upper = low_back(matmul(second, w_upper))
    hidden = low(jax.nn.gelu(hidden_gate, approximate=False) * hidden_upper)
    return middle + low_back(matmul(hidden, w_down))

def orthogonal(block):
    flipped = block.shape[0] > block.shape[1]
    wide = block.T if flipped else block
    current = wide / (jnp.sqrt(jnp.sum(wide * wide)) + 1e-07)
    for turn in range(NS_ITERS):
        gram = matmul(current, current.T)
        current = ns_first * current + matmul(ns_second * gram + ns_third * matmul(gram, gram), current)
    return current.T if flipped else current

def muon_update(weight, momentum, grad, split_axis):
    fresh = momentum_decay * momentum + grad
    blocks = jnp.split(fresh, SPLITS, axis=split_axis)
    block_rows, block_cols = blocks[0].shape
    orth = jnp.concatenate([orthogonal(piece) for piece in blocks], axis=split_axis)
    factor = math.sqrt(max(1.0, block_rows / block_cols))
    return (fresh, weight * (1.0 - muon_rate * weight_decay) - muon_rate * factor * orth)

def reference(tokens, cotangent, doc_lengths, key_weights, value_weights, out_weights, up_weights, down_weights, key_momentum, value_momentum, out_momentum, up_momentum, down_momentum, norm_params, norm_first, norm_second):
    starts = jnp.cumsum(doc_lengths, axis=1) - doc_lengths
    positions = jnp.arange(LEN).astype(jnp.int32)
    doc_ids = lax.optimization_barrier(jnp.sum((positions[None, :, None] >= starts[:, None, :]).astype(jnp.int32), axis=2)) - 1
    sequences = tokens.astype(jnp.float32).reshape(SEQS, LEN, D)
    matrices = (key_weights[0], key_weights[1], value_weights[0], value_weights[1], out_weights, up_weights[0], up_weights[1], down_weights)

    def forward(inputs, weight_list, norms):
        rounded = tuple((low(matrix) for matrix in weight_list))
        checked_layer = jax.checkpoint(layer_sequence)

        def per_sequence(running, element):
            return (running, checked_layer(element[0], element[1], rounded, norms))
        unused, outputs = lax.scan(per_sequence, jnp.zeros((), jnp.float32), (inputs, doc_ids))
        return outputs
    outputs, pullback = jax.vjp(forward, sequences, matrices, norm_params)
    grad_inputs, grad_matrices, grad_norms = pullback(cotangent.astype(jnp.float32).reshape(SEQS, LEN, D))
    result = outputs.reshape(TOKENS, D).astype(jnp.bfloat16)
    token_grad = grad_inputs.reshape(TOKENS, D)
    key_pair = [muon_update(key_weights[member], key_momentum[member], grad_matrices[member], 1) for member in range(2)]
    value_pair = [muon_update(value_weights[member], value_momentum[member], grad_matrices[2 + member], 1) for member in range(2)]
    out_single = muon_update(out_weights, out_momentum, grad_matrices[4], 0)
    up_pair = [muon_update(up_weights[member], up_momentum[member], grad_matrices[5 + member], 1) for member in range(2)]
    down_single = muon_update(down_weights, down_momentum, grad_matrices[7], 0)
    new_norm_first = beta_first * norm_first + (1.0 - beta_first) * grad_norms
    new_norm_second = beta_second * norm_second + (1.0 - beta_second) * grad_norms * grad_norms
    fix_first = 1.0 - beta_first ** STEP
    fix_second = 1.0 - beta_second ** STEP
    new_norm_params = norm_params - adam_rate * (new_norm_first / fix_first) / (jnp.sqrt(new_norm_second / fix_second) + adam_eps)
    return (result, token_grad, jnp.stack([key_pair[0][0], key_pair[1][0]]), jnp.stack([value_pair[0][0], value_pair[1][0]]), out_single[0], jnp.stack([up_pair[0][0], up_pair[1][0]]), down_single[0], jnp.stack([key_pair[0][1], key_pair[1][1]]), jnp.stack([value_pair[0][1], value_pair[1][1]]), out_single[1], jnp.stack([up_pair[0][1], up_pair[1][1]]), down_single[1], new_norm_first, new_norm_second, new_norm_params)
```

```python
from functools import partial
import math

import jax
import jax.numpy as jnp
from jax import lax
from jax.sharding import PartitionSpec as P

H = 8
KEY_HEAD_SIZE = 256
DV = 432
LEN = 1024
NS_ITERS = 5
STEP = 10


eps_norm = 1e-05
group_floor = 1.0
ns_first = 3.4445
ns_second = -4.775
ns_third = 2.0315
momentum_decay = 0.95
muon_rate = 0.5
weight_decay = 0.1
beta_first = 0.9
beta_second = 0.95
adam_rate = 0.8
adam_eps = 1e-08
TILE = 1024


def root_scale(values):
    return lax.rsqrt(jnp.mean(values * values, axis=-1, keepdims=True) + eps_norm)


def norm_back(grad_normed, normed, scaling):
    return scaling * (grad_normed - normed * jnp.mean(grad_normed * normed, axis=-1, keepdims=True))


def dot(left, right, left_dim, right_dim):
    return lax.dot_general(
        left, right, (((left_dim,), (right_dim,)), ((), ())), preferred_element_type=jnp.float32
    )


def gather_tokens(values):
    return lax.all_gather(values, "tensor", axis=0, tiled=True)


def scatter_tokens(values):
    return lax.psum_scatter(
        values.astype(jnp.bfloat16), "tensor", scatter_dimension=0, tiled=True
    ).astype(jnp.float32)


def ring_order(count):
    return list(range(0, count, 2)) + list(range(count - 1, 0, -2))


def ring_place(count):
    order = ring_order(count)
    return order, [(order[i], order[(i + 1) % count]) for i in range(count)]


class Ring:
    def __init__(self):
        self.count = lax.axis_size("dp")
        order, self.right = ring_place(self.count)
        self.left = [(b, a) for a, b in self.right]
        self.half = self.count // 2
        place_of = [order.index(rank) for rank in range(self.count)]
        place = jnp.asarray(place_of, jnp.int32)[lax.axis_index("dp")]
        steps = jnp.arange(self.count, dtype=jnp.int32)
        self.rank_at = jnp.asarray(order, jnp.int32)[(place + steps) % self.count]

    def rank(self, distance):
        return self.rank_at[distance % self.count]

    def gather(self, shard):
        rows, width = shard.shape
        cut = rows // 2
        full = jnp.zeros((rows, width * self.count), shard.dtype)

        def put(full, block, distance, row):
            return lax.dynamic_update_slice(full, block, (row, self.rank(distance) * width))

        full = put(full, shard, 0, 0)
        from_left = from_right = shard
        for step in range(1, self.half):
            from_left = lax.ppermute(from_left, "dp", self.right)
            from_right = lax.ppermute(from_right, "dp", self.left)
            full = put(full, from_left, -step, 0)
            full = put(full, from_right, step, 0)
        upper = lax.ppermute(from_left[:cut], "dp", self.right)
        lower = lax.ppermute(from_right[cut:], "dp", self.left)
        full = put(full, upper, self.half, 0)
        return put(full, lower, self.half, cut)

    def scatter(self, full):
        rows = full.shape[0]
        width = full.shape[1] // self.count
        cut = rows // 2

        def piece(distance, row, size):
            return lax.dynamic_slice(full, (row, self.rank(distance) * width), (size, width))

        upper = lax.ppermute(piece(self.half, 0, cut), "dp", self.right)
        lower = lax.ppermute(piece(self.half, cut, rows - cut), "dp", self.left)
        zero_upper = jnp.pad(upper, ((0, rows - cut), (0, 0)))
        zero_lower = jnp.pad(lower, ((cut, 0), (0, 0)))
        to_right, to_left = zero_upper, zero_lower
        for step in range(self.half - 1, 0, -1):
            to_right = (piece(step, 0, rows).astype(jnp.float32) + to_right.astype(jnp.float32)).astype(jnp.bfloat16)
            to_left = (piece(-step, 0, rows).astype(jnp.float32) + to_left.astype(jnp.float32)).astype(jnp.bfloat16)
            to_right = lax.ppermute(to_right, "dp", self.right)
            to_left = lax.ppermute(to_left, "dp", self.left)
        own = piece(0, 0, rows).astype(jnp.float32)
        return own + to_right.astype(jnp.float32) + to_left.astype(jnp.float32)


def decay_rows(doc_ids, log_gamma, first, size, keys):
    query_pos = first + jnp.arange(size)
    key_pos = jnp.arange(keys)
    distance = query_pos[:, None] - key_pos[None, :]
    allowed = (doc_ids[first : first + size, None] == doc_ids[None, :keys]) & (distance >= 0)
    steps_back = jnp.maximum(distance, 0).astype(jnp.float32)
    falloff = jnp.exp(log_gamma[:, None, None] * steps_back[None])
    return jnp.where(allowed[None], falloff, 0.0)


def einsum32(spec, left, right):
    return jnp.einsum(spec, left, right, preferred_element_type=jnp.float32)


def retention_forward(query, key, value, doc_ids, log_gamma, block):
    factor = KEY_HEAD_SIZE ** (-0.5)
    pieces = []
    for first in range(0, LEN, block):
        keys = first + block
        falloff = decay_rows(doc_ids, log_gamma, first, block, keys)
        scores = einsum32("hdq,hdk->hqk", query[:, :, first:keys], key[:, :, :keys]) * factor
        weights = (scores * falloff).astype(jnp.bfloat16)
        pieces.append(einsum32("hdk,hqk->hdq", value[:, :, :keys], weights))
    return jnp.concatenate(pieces, axis=2)


def retention_backward(query, key, value, grad, doc_ids, log_gamma, block):
    factor = KEY_HEAD_SIZE ** (-0.5)
    grad_query = []
    grad_key = jnp.zeros(key.shape, jnp.float32)
    grad_value = jnp.zeros(value.shape, jnp.float32)
    for first in range(0, LEN, block):
        keys = first + block
        falloff = decay_rows(doc_ids, log_gamma, first, block, keys)
        query_now, grad_now = query[:, :, first:keys], grad[:, :, first:keys]
        scores = einsum32("hdq,hdk->hqk", query_now, key[:, :, :keys]) * factor
        weights = (scores * falloff).astype(jnp.bfloat16)
        grad_weights = einsum32("hdq,hdk->hqk", grad_now, value[:, :, :keys])
        grad_scores = (grad_weights * falloff).astype(jnp.bfloat16)
        grad_query.append(einsum32("hdk,hqk->hdq", key[:, :, :keys], grad_scores) * factor)
        grad_key = grad_key.at[:, :, :keys].add(einsum32("hdq,hqk->hdk", query_now, grad_scores) * factor)
        grad_value = grad_value.at[:, :, :keys].add(einsum32("hdq,hqk->hdk", grad_now, weights))
    return jnp.concatenate(grad_query, axis=2), grad_key, grad_value


def newton_schulz(block):
    size = block.shape[0]
    eye = (lax.broadcasted_iota(jnp.int32, (size, size), 0) == lax.broadcasted_iota(jnp.int32, (size, size), 1))
    total = jnp.sum(block * block)
    current = block / (jnp.sqrt(total) + 1e-07)
    for turn in range(NS_ITERS):
        low = current.astype(jnp.bfloat16)
        gram = dot(low, low, 1, 1)
        middle = jnp.sum(jnp.where(eye, gram, 0.0)) / size
        rest = jnp.where(eye, gram - middle, gram).astype(jnp.bfloat16)
        square = dot(rest, rest, 1, 0)
        poly = (ns_second + 2.0 * ns_third * middle) * rest.astype(jnp.float32) + ns_third * square
        outer = ns_first + middle * (ns_second + ns_third * middle)
        current = outer * current + dot(poly.astype(jnp.bfloat16), low, 1, 0)
    return current


def orthogonalize(slabs):
    ranks = lax.axis_size("dp")
    widest = max(slab.shape[0] for slab in slabs)
    cols = slabs[0].shape[1]
    padded = [jnp.pad(slab.astype(jnp.bfloat16), ((0, widest - slab.shape[0]), (0, 0))) for slab in slabs]
    each = (len(slabs) + ranks - 1) // ranks
    padded += [jnp.zeros((widest, cols), jnp.bfloat16)] * (each * ranks - len(slabs))
    stacked = jnp.stack(padded)
    owned = lax.all_to_all(stacked.reshape(ranks, each, widest, cols), "dp", 0, 0, tiled=True)
    done = []
    for index in range(each):
        mine = jnp.moveaxis(owned[:, index], 0, 1).reshape(widest, ranks * cols)
        done.append(newton_schulz(mine.astype(jnp.float32)).astype(jnp.bfloat16))
    ready = [jnp.moveaxis(item.reshape(widest, ranks, cols), 1, 0) for item in done]
    ready = jnp.stack(ready, axis=1)
    returned = lax.all_to_all(ready, "dp", 0, 0, tiled=True).reshape(each * ranks, widest, cols)
    return [returned[index, : slab.shape[0]] for index, slab in enumerate(slabs)]


def gather_norms(norm_params):
    own = norm_params.shape[0]
    filled = TILE * ((own + TILE - 1) // TILE)
    tile = jnp.pad(norm_params, (0, filled - own)).reshape(filled // 128, 128)
    whole = lax.all_gather(tile, ("dp", "tensor"), axis=0, tiled=True)
    return whole.reshape(-1, filled)[:, :own].reshape(-1)


def scatter_norms(terms, own):
    filled = TILE * ((own + TILE - 1) // TILE)
    rows = jnp.pad(terms.reshape(-1, own), ((0, 0), (0, filled - own))).reshape(-1, 128)
    return lax.psum_scatter(rows, ("dp", "tensor"), scatter_dimension=0, tiled=True).reshape(-1)[:own]


def per_device(
    tokens,
    cotangent,
    doc_lengths,
    key_weights,
    value_weights,
    out_weights,
    up_weights,
    down_weights,
    key_momentum,
    value_momentum,
    out_momentum,
    up_momentum,
    down_momentum,
    norm_params,
    norm_first,
    norm_second,
):
    tensor_count = lax.axis_size("tensor")
    tensor_index = lax.axis_index("tensor")
    heads = H // tensor_count
    width = tokens.shape[1]
    keys_local = key_weights.shape[2]
    values_local = value_weights.shape[2]
    hidden_local = up_weights.shape[2]
    value_total = values_local * tensor_count
    block = min(LEN, 512)
    ring = Ring()

    def low_t(matrix):
        return matrix.astype(jnp.bfloat16).T

    attend_full = ring.gather(
        jnp.concatenate([low_t(key_weights[0]), low_t(key_weights[1]), low_t(value_weights[0])])
    )
    gate_full = ring.gather(low_t(value_weights[1]))
    out_full = ring.gather(out_weights.astype(jnp.bfloat16))
    upper_full = ring.gather(jnp.concatenate([low_t(up_weights[0]), low_t(up_weights[1])]))
    down_full = ring.gather(down_weights.astype(jnp.bfloat16))

    gathered_norms = gather_norms(norm_params)
    gain_one = gathered_norms[:width]
    gain_two = gathered_norms[width : 2 * width]
    group_gain = lax.dynamic_slice_in_dim(
        gathered_norms, 2 * width + tensor_index * values_local, values_local
    )[:, None]
    group_bias = lax.dynamic_slice_in_dim(
        gathered_norms, 2 * width + value_total + tensor_index * values_local, values_local
    )[:, None]
    starts_all = jnp.cumsum(doc_lengths[0]) - doc_lengths[0]
    positions = jnp.arange(LEN)
    doc_ids = jnp.sum((positions[:, None] >= starts_all[None, :]).astype(jnp.int32), axis=1) - 1

    inputs = tokens.astype(jnp.float32)
    scale_one = root_scale(inputs)
    normed_one = inputs * scale_one
    normed_all = gather_tokens((normed_one * gain_one).astype(jnp.bfloat16))
    rows_total = normed_all.shape[0]
    grad_rows_two = gather_tokens(cotangent)

    attend = dot(attend_full, normed_all, 1, 1).astype(jnp.bfloat16)
    query = attend[:keys_local].reshape(heads, KEY_HEAD_SIZE, rows_total)
    key = attend[keys_local : 2 * keys_local].reshape(heads, KEY_HEAD_SIZE, rows_total)
    value = attend[2 * keys_local :].reshape(heads, DV, rows_total)
    gate_pre = dot(gate_full, normed_all, 1, 1)
    head_ids = (tensor_index * heads + jnp.arange(heads)).astype(jnp.float32)
    log_gamma = jnp.log(1.0 - jnp.exp2(-5.0 - head_ids))
    mixed_heads = retention_forward(query, key, value, doc_ids, log_gamma, block)
    centred = mixed_heads - jnp.mean(mixed_heads, axis=1, keepdims=True)
    group_scale = lax.rsqrt(jnp.mean(centred * centred, axis=1, keepdims=True) + group_floor)
    group_hat = centred * group_scale
    group_flat = group_hat.reshape(values_local, rows_total)
    group_out = group_flat * group_gain + group_bias
    gate_act, silu_pull = jax.vjp(jax.nn.silu, gate_pre)
    mixed_low = (gate_act * group_out).astype(jnp.bfloat16)
    middle = inputs + scatter_tokens(dot(mixed_low, out_full, 0, 0))
    scale_two = root_scale(middle)
    normed_two = middle * scale_two
    second_all = gather_tokens((normed_two * gain_two).astype(jnp.bfloat16))
    hidden_gate = dot(upper_full[:hidden_local], second_all, 1, 1)
    hidden_upper = dot(upper_full[hidden_local:], second_all, 1, 1)
    gelu_gate, gelu_pull = jax.vjp(partial(jax.nn.gelu, approximate=False), hidden_gate)
    hidden_low = (gelu_gate * hidden_upper).astype(jnp.bfloat16)
    result = middle + scatter_tokens(dot(hidden_low, down_full, 0, 0))

    grad_result = cotangent.astype(jnp.float32)
    grad_down = dot(hidden_low, grad_rows_two, 1, 0).astype(jnp.bfloat16)
    grad_down_w = ring.scatter(grad_down)
    grad_hidden = dot(down_full, grad_rows_two, 1, 1)
    grad_gate_mlp = gelu_pull(grad_hidden * hidden_upper)[0].astype(jnp.bfloat16)
    grad_upper_mlp = (grad_hidden * gelu_gate).astype(jnp.bfloat16)
    grad_hidden_low = jnp.concatenate([grad_gate_mlp, grad_upper_mlp])
    grad_upper_w = ring.scatter(dot(grad_hidden_low, second_all, 1, 0).astype(jnp.bfloat16))
    grad_second_local = scatter_tokens(dot(grad_hidden_low, upper_full, 0, 0))
    grad_gain_two = jnp.sum(grad_second_local * normed_two, axis=0)
    grad_middle = grad_result + norm_back(grad_second_local * gain_two, normed_two, scale_two)
    grad_rows_one = gather_tokens(grad_middle.astype(jnp.bfloat16))
    grad_out_w = ring.scatter(dot(mixed_low, grad_rows_one, 1, 0).astype(jnp.bfloat16))
    grad_mixed = dot(out_full, grad_rows_one, 1, 1)
    grad_gate_low = silu_pull(grad_mixed * group_out)[0].astype(jnp.bfloat16)
    grad_group = grad_mixed * gate_act
    grad_group_gain = jnp.sum(grad_group * group_flat, axis=1)
    grad_group_bias = jnp.sum(grad_group, axis=1)
    grad_hat = (grad_group * group_gain).reshape(heads, DV, rows_total)
    grad_heads = group_scale * (
        grad_hat
        - jnp.mean(grad_hat, axis=1, keepdims=True)
        - group_hat * jnp.mean(grad_hat * group_hat, axis=1, keepdims=True)
    )
    grad_queries, grad_keys, grad_values = retention_backward(
        query, key, value, grad_heads.astype(jnp.bfloat16), doc_ids, log_gamma, block
    )
    grad_gate_w = ring.scatter(dot(grad_gate_low, normed_all, 1, 0).astype(jnp.bfloat16))
    grad_attend_low = jnp.concatenate(
        [
            grad_queries.astype(jnp.bfloat16).reshape(keys_local, rows_total),
            grad_keys.astype(jnp.bfloat16).reshape(keys_local, rows_total),
            grad_values.astype(jnp.bfloat16).reshape(values_local, rows_total),
        ]
    )
    grad_attend_w = ring.scatter(dot(grad_attend_low, normed_all, 1, 0).astype(jnp.bfloat16))
    grad_first = dot(grad_attend_low, attend_full, 0, 0) + dot(grad_gate_low, gate_full, 0, 0)
    grad_first_local = scatter_tokens(grad_first)
    grad_gain_one = jnp.sum(grad_first_local * normed_one, axis=0)
    token_grad = grad_middle + norm_back(grad_first_local * gain_one, normed_one, scale_one)
    group_part = jnp.zeros((2, value_total), jnp.float32)
    group_part = lax.dynamic_update_slice_in_dim(
        group_part, jnp.stack([grad_group_gain, grad_group_bias]), tensor_index * values_local, 1
    )
    norm_terms = jnp.concatenate([grad_gain_one, grad_gain_two, group_part.reshape(-1)])
    norm_grad = scatter_norms(norm_terms, norm_params.shape[0])

    fresh_query = momentum_decay * key_momentum[0] + grad_attend_w[:keys_local].T
    fresh_key = momentum_decay * key_momentum[1] + grad_attend_w[keys_local : 2 * keys_local].T
    fresh_value = momentum_decay * value_momentum[0] + grad_attend_w[2 * keys_local :].T
    fresh_gate = momentum_decay * value_momentum[1] + grad_gate_w.T
    fresh_out = momentum_decay * out_momentum + grad_out_w
    fresh_hidden = momentum_decay * up_momentum[0] + grad_upper_w[:hidden_local].T
    fresh_upper = momentum_decay * up_momentum[1] + grad_upper_w[hidden_local:].T
    fresh_down = momentum_decay * down_momentum + grad_down_w
    orth = orthogonalize(
        [
            fresh_query.T,
            fresh_key.T,
            fresh_value.T,
            fresh_gate.T,
            fresh_hidden.T,
            fresh_upper.T,
            fresh_out,
            fresh_down,
        ]
    )
    orth = [item.astype(jnp.float32) for item in orth]
    keep_factor = 1.0 - muon_rate * weight_decay

    def rate(rows, cols):
        return muon_rate * math.sqrt(max(1.0, rows / cols))

    new_key_weights = key_weights * keep_factor - rate(width, keys_local) * jnp.stack([orth[0].T, orth[1].T])
    new_value_weights = value_weights * keep_factor - rate(width, values_local) * jnp.stack([orth[2].T, orth[3].T])
    new_upper_weights = up_weights * keep_factor - rate(width, hidden_local) * jnp.stack([orth[4].T, orth[5].T])
    new_out_weights = out_weights * keep_factor - rate(values_local, width) * orth[6]
    new_down_weights = down_weights * keep_factor - rate(hidden_local, width) * orth[7]
    new_norm_first = beta_first * norm_first + (1.0 - beta_first) * norm_grad
    new_norm_second = beta_second * norm_second + (1.0 - beta_second) * norm_grad * norm_grad
    fix_first = 1.0 - beta_first**STEP
    fix_second = 1.0 - beta_second**STEP
    new_norm_params = norm_params - adam_rate * (new_norm_first / fix_first) / (
        jnp.sqrt(new_norm_second / fix_second) + adam_eps
    )
    return (
        result.astype(jnp.bfloat16),
        token_grad,
        jnp.stack([fresh_query, fresh_key]),
        jnp.stack([fresh_value, fresh_gate]),
        fresh_out,
        jnp.stack([fresh_hidden, fresh_upper]),
        fresh_down,
        new_key_weights,
        new_value_weights,
        new_out_weights,
        new_upper_weights,
        new_down_weights,
        new_norm_first,
        new_norm_second,
        new_norm_params,
    )


def solution(mesh):
    tokens = P(("dp", "tensor"), None)
    wide = P(None, "dp", "tensor")
    tall = P("tensor", "dp")
    norms = P(("dp", "tensor"))
    return jax.shard_map(
        per_device,
        mesh=mesh,
        in_specs=(
            tokens, tokens, P("dp", None), wide, wide, tall, wide, tall,
            wide, wide, tall, wide, tall, norms, norms, norms,
        ),
        out_specs=(
            tokens, tokens, wide, wide, tall, wide, tall,
            wide, wide, tall, wide, tall, norms, norms, norms,
        ),
        check_vma=False,
    )
```

```python
from functools import partial
import math

import jax
import jax.numpy as jnp
from jax import lax
from jax.experimental import pallas as pl
from jax.experimental.pallas import tpu as pltpu
from jax.sharding import PartitionSpec as P

H = 8
KEY_HEAD_SIZE = 256
DV = 432
LEN = 1024
NS_ITERS = 5
STEP = 10


eps_norm = 1e-05
group_floor = 1.0
ns_first = 3.4445
ns_second = -4.775
ns_third = 2.0315
momentum_decay = 0.95
muon_rate = 0.5
weight_decay = 0.1
beta_first = 0.9
beta_second = 0.95
adam_rate = 0.8
adam_eps = 1e-08
TILE = 1024


def root_scale(values):
    return lax.rsqrt(jnp.mean(values * values, axis=-1, keepdims=True) + eps_norm)


def norm_back(grad_normed, normed, scaling):
    return scaling * (grad_normed - normed * jnp.mean(grad_normed * normed, axis=-1, keepdims=True))


def dot(left, right, left_dim, right_dim):
    return lax.dot_general(
        left, right, (((left_dim,), (right_dim,)), ((), ())), preferred_element_type=jnp.float32
    )


def gather_tokens(values):
    return lax.all_gather(values, "tensor", axis=0, tiled=True)


def scatter_tokens(values):
    return lax.psum_scatter(
        values.astype(jnp.bfloat16), "tensor", scatter_dimension=0, tiled=True
    ).astype(jnp.float32)


def ring_order(count):
    return list(range(0, count, 2)) + list(range(count - 1, 0, -2))


def ring_place(count):
    order = ring_order(count)
    return order, [(order[i], order[(i + 1) % count]) for i in range(count)]


def tie(value, *others):
    return lax.optimization_barrier((value, others))[0]


class Ring:
    def __init__(self):
        self.count = lax.axis_size("dp")
        order, self.right = ring_place(self.count)
        self.left = [(b, a) for a, b in self.right]
        self.half = self.count // 2
        place_of = [order.index(rank) for rank in range(self.count)]
        place = jnp.asarray(place_of, jnp.int32)[lax.axis_index("dp")]
        steps = jnp.arange(self.count, dtype=jnp.int32)
        self.rank_at = jnp.asarray(order, jnp.int32)[(place + steps) % self.count]
        self.sent = []
        self.added = None

    def rank(self, distance):
        return self.rank_at[distance % self.count]

    def exchange(self, to_right, to_left):
        if len(self.sent) > 2:
            to_right, to_left = tie((to_right, to_left), self.sent[-3])
        got = lax.ppermute(to_right, "dp", self.right), lax.ppermute(to_left, "dp", self.left)
        self.sent.append(got)
        return got


def cut_rows(rows):
    return (rows // 2 + 15) // 16 * 16


class Gather:
    def __init__(self, ring, shard):
        self.ring = ring
        self.shard = shard
        self.rows, self.width = shard.shape
        self.blocks = [(shard, 0, 0)]
        self.from_left = self.from_right = shard
        self.at = 0
        self.marks = []

    def step(self, after=None):
        self.at += 1
        ring = self.ring
        if after is not None:
            self.from_left, self.from_right = tie((self.from_left, self.from_right), after)
        if self.at < ring.half:
            self.from_left, self.from_right = ring.exchange(self.from_left, self.from_right)
            self.blocks += [(self.from_left, -self.at, 0), (self.from_right, self.at, 0)]
            self.marks.append((self.from_left, self.from_right))
        else:
            cut = cut_rows(self.rows)
            upper, lower = ring.exchange(self.from_left[:cut], self.from_right[cut:])
            self.blocks += [(upper, self.at, 0), (lower, self.at, cut)]
            self.marks.append((upper, lower))


def run(lanes, rounds, after=None):
    for turn in range(rounds):
        for lane in lanes:
            lane.step(after if turn == 0 else None)


def reached(lanes, rounds):
    return [lane.marks[min(rounds, len(lane.marks)) - 1] for lane in lanes]


def assemble(lanes):
    ring = lanes[0].ring
    rows = sum(lane.rows for lane in lanes)
    full = jnp.zeros((rows, lanes[0].width * ring.count), lanes[0].shard.dtype)
    base = 0
    for lane in lanes:
        for block, distance, row in lane.blocks:
            full = lax.dynamic_update_slice(full, block, (base + row, ring.rank(distance) * lane.width))
        base += lane.rows
    return full


class Scatter:
    def __init__(self, ring, full, first, rows):
        self.ring = ring
        self.full = full
        self.first = first
        self.rows = rows
        self.width = full.shape[1] // ring.count
        self.at = ring.half
        self.marks = []

    def piece(self, distance, row, size):
        column = self.ring.rank(distance) * self.width
        return lax.dynamic_slice(self.full, (self.first + row, column), (size, self.width))

    def step(self, after=None):
        ring = self.ring
        if self.at == ring.half:
            cut = cut_rows(self.rows)
            upper, lower = ring.exchange(
                self.piece(self.at, 0, cut), self.piece(self.at, cut, self.rows - cut)
            )
            self.from_left = jnp.pad(upper, ((0, self.rows - cut), (0, 0)))
            self.from_right = jnp.pad(lower, ((cut, 0), (0, 0)))
        else:
            came = self.from_left, self.from_right
            if ring.added is not None:
                came = tie(came, ring.added)
            to_right = self.add(self.at, came[0]).astype(jnp.bfloat16)
            to_left = self.add(-self.at, came[1]).astype(jnp.bfloat16)
            ring.added = to_right, to_left
            self.from_left, self.from_right = ring.exchange(to_right, to_left)
        self.marks.append((self.from_left, self.from_right))
        self.at -= 1

    def add(self, distance, passed):
        return self.piece(distance, 0, self.rows).astype(jnp.float32) + passed.astype(jnp.float32)

    def total(self):
        return self.add(0, self.from_left) + self.from_right.astype(jnp.float32)


def halves(rows):
    cut = cut_rows(rows)
    return [(0, cut), (cut, rows - cut)]


def gather_lanes(ring, shard):
    return [Gather(ring, shard[first : first + size]) for first, size in halves(shard.shape[0])]


def scatter_lanes(ring, full):
    return [Scatter(ring, full, first, size) for first, size in halves(full.shape[0])]


def totals(lanes):
    return jnp.concatenate([lane.total() for lane in lanes])


def decay_rows(doc_ids, log_gamma, first, size, keys):
    query_pos = first + jnp.arange(size)
    key_pos = jnp.arange(keys)
    distance = query_pos[:, None] - key_pos[None, :]
    allowed = (doc_ids[first : first + size, None] == doc_ids[None, :keys]) & (distance >= 0)
    steps_back = jnp.maximum(distance, 0).astype(jnp.float32)
    falloff = jnp.exp(log_gamma[:, None, None] * steps_back[None])
    return jnp.where(allowed[None], falloff, 0.0)


def einsum32(spec, left, right):
    return jnp.einsum(spec, left, right, preferred_element_type=jnp.float32)


def retention_forward(query, key, value, doc_ids, log_gamma, block):
    factor = KEY_HEAD_SIZE ** (-0.5)
    pieces = []
    for first in range(0, LEN, block):
        keys = first + block
        falloff = decay_rows(doc_ids, log_gamma, first, block, keys)
        scores = einsum32("hdq,hdk->hqk", query[:, :, first:keys], key[:, :, :keys]) * factor
        weights = (scores * falloff).astype(jnp.bfloat16)
        pieces.append(einsum32("hdk,hqk->hdq", value[:, :, :keys], weights))
    return jnp.concatenate(pieces, axis=2)


def retention_backward(query, key, value, grad, doc_ids, log_gamma, block):
    factor = KEY_HEAD_SIZE ** (-0.5)
    grad_query = []
    grad_key = jnp.zeros(key.shape, jnp.float32)
    grad_value = jnp.zeros(value.shape, jnp.float32)
    for first in range(0, LEN, block):
        keys = first + block
        falloff = decay_rows(doc_ids, log_gamma, first, block, keys)
        query_now, grad_now = query[:, :, first:keys], grad[:, :, first:keys]
        scores = einsum32("hdq,hdk->hqk", query_now, key[:, :, :keys]) * factor
        weights = (scores * falloff).astype(jnp.bfloat16)
        grad_weights = einsum32("hdq,hdk->hqk", grad_now, value[:, :, :keys])
        grad_scores = (grad_weights * falloff).astype(jnp.bfloat16)
        grad_query.append(einsum32("hdk,hqk->hdq", key[:, :, :keys], grad_scores) * factor)
        grad_key = grad_key.at[:, :, :keys].add(einsum32("hdq,hqk->hdk", query_now, grad_scores) * factor)
        grad_value = grad_value.at[:, :, :keys].add(einsum32("hdq,hqk->hdk", grad_now, weights))
    return jnp.concatenate(grad_query, axis=2), grad_key, grad_value


def newton_schulz_kernel(turns, step, in_ref, out_ref, cur_ref, low_ref, rest_ref, poly_ref, scale_ref):
    parts, size, cols = in_ref.shape
    width = parts * cols
    blocks = size // step

    def rows_of(index):
        return pl.ds(pl.multiple_of(index * step, step), step)

    def first_sum(index, total):
        rows = rows_of(index)
        for part in range(parts):
            block = in_ref[part, rows, :].astype(jnp.float32)
            total = total + jnp.sum(block * block)
        return total

    total = lax.fori_loop(0, blocks, first_sum, jnp.float32(0.0))
    scale_ref[...] = 1.0 / (jnp.sqrt(jnp.full(scale_ref.shape, total)) + 1e-07)

    @pl.loop(0, blocks)
    def _(index):
        rows = rows_of(index)
        scale = scale_ref[0, 0]
        for part in range(parts):
            block = in_ref[part, rows, :].astype(jnp.float32) * scale
            columns = pl.ds(part * cols, cols)
            cur_ref[rows, columns] = block
            low_ref[0, rows, columns] = block.astype(jnp.bfloat16)

    norm = jnp.float32(1.0)
    for turn in range(turns):
        here, there = turn % 2, (turn + 1) % 2
        last = turn == turns - 1
        middle = norm * (1.0 / size)

        @pl.loop(0, blocks)
        def _(index):
            rows = rows_of(index)
            gram = dot(low_ref[here, rows, :], low_ref[here], 1, 1)
            place = lax.broadcasted_iota(jnp.int32, gram.shape, 0) + index * step
            eye = place == lax.broadcasted_iota(jnp.int32, gram.shape, 1)
            rest_ref[rows, :] = jnp.where(eye, gram - middle, gram).astype(jnp.bfloat16)

        @pl.loop(0, blocks)
        def _(index):
            rows = rows_of(index)
            rest = rest_ref[rows, :]
            square = dot(rest, rest_ref[...], 1, 0)
            poly = (ns_second + 2.0 * ns_third * middle) * rest.astype(jnp.float32) + ns_third * square
            poly_ref[rows, :] = poly.astype(jnp.bfloat16)

        outer = ns_first + middle * (ns_second + ns_third * middle)

        def turn_rows(index, total):
            rows = rows_of(index)
            poly = poly_ref[rows, :]
            for part in range(parts):
                columns = pl.ds(part * cols, cols)
                fresh = outer * cur_ref[rows, columns] + dot(poly, low_ref[here, :, columns], 1, 0)
                if last:
                    out_ref[part, rows, :] = fresh.astype(jnp.bfloat16)
                else:
                    cur_ref[rows, columns] = fresh
                    low_ref[there, rows, columns] = fresh.astype(jnp.bfloat16)
                    total = total + jnp.sum(fresh * fresh)
            return total

        norm = lax.fori_loop(0, blocks, turn_rows, jnp.float32(0.0))


def newton_schulz(block):
    parts, size, cols = block.shape
    width = parts * cols
    step = next(step for step in range(288, 0, -16) if size % step == 0)
    products = 2 * size * size * (2 * width + size) * NS_ITERS
    return pl.pallas_call(
        partial(newton_schulz_kernel, NS_ITERS, step),
        out_shape=jax.ShapeDtypeStruct(block.shape, jnp.bfloat16),
        in_specs=[pl.BlockSpec(memory_space=pltpu.VMEM)],
        out_specs=pl.BlockSpec(memory_space=pltpu.VMEM),
        scratch_shapes=[
            pltpu.VMEM((size, width), jnp.float32),
            pltpu.VMEM((2, size, width), jnp.bfloat16),
            pltpu.VMEM((size, size), jnp.bfloat16),
            pltpu.VMEM((size, size), jnp.bfloat16),
            pltpu.VMEM((8, 128), jnp.float32),
        ],
        compiler_params=pltpu.CompilerParams(vmem_limit_bytes=48 * 1024 * 1024),
        cost_estimate=pl.CostEstimate(flops=products, bytes_accessed=4 * size * width, transcendentals=0),
    )(block)


def orthogonalize(slabs, after):
    ranks = lax.axis_size("dp")
    widest = max(slab.shape[0] for slab in slabs)
    cols = slabs[0].shape[1]
    padded = [jnp.pad(slab.astype(jnp.bfloat16), ((0, widest - slab.shape[0]), (0, 0))) for slab in slabs]
    each = (len(slabs) + ranks - 1) // ranks
    padded += [jnp.zeros((widest, cols), jnp.bfloat16)] * (each * ranks - len(slabs))
    stacked = tie(jnp.stack(padded), after)
    owned = lax.all_to_all(stacked.reshape(ranks, each, widest, cols), "dp", 0, 0, tiled=True)
    done = []
    for index in range(each):
        mine = owned[:, index]
        if cols % 128:
            mine = jnp.moveaxis(mine, 0, 1).reshape(1, widest, ranks * cols)
        item = newton_schulz(mine)
        if cols % 128:
            item = jnp.moveaxis(item.reshape(widest, ranks, cols), 1, 0)
        done.append(item)
    ready = jnp.stack(done, axis=1)
    returned = lax.all_to_all(ready, "dp", 0, 0, tiled=True).reshape(each * ranks, widest, cols)
    return [returned[index, : slab.shape[0]] for index, slab in enumerate(slabs)]


def gather_norms(ring, norm_params):
    own = norm_params.shape[0]
    filled = TILE * ((own + TILE - 1) // TILE)
    tile = jnp.pad(norm_params, (0, filled - own)).reshape(1, filled // 128, 128)
    count = lax.axis_size("tensor")
    index = lax.axis_index("tensor")
    group = lax.dynamic_update_slice(jnp.zeros((count,) + tile.shape[1:], tile.dtype), tile, (index, 0, 0))
    for turn in range(1, count):
        moved = lax.ppermute(tile, "tensor", [(i, (i + turn) % count) for i in range(count)])
        group = lax.dynamic_update_slice(group, moved, ((index - turn) % count, 0, 0))
    whole = jnp.zeros((ring.count,) + group.shape, group.dtype)
    from_left = from_right = group
    whole = lax.dynamic_update_slice(whole, group[None], (ring.rank(0), 0, 0, 0))
    for step in range(1, ring.half + 1):
        from_left = lax.ppermute(from_left, "dp", ring.right)
        whole = lax.dynamic_update_slice(whole, from_left[None], (ring.rank(-step), 0, 0, 0))
        if step < ring.half:
            from_right = lax.ppermute(from_right, "dp", ring.left)
            whole = lax.dynamic_update_slice(whole, from_right[None], (ring.rank(step), 0, 0, 0))
    return whole.reshape(-1, filled)[:, :own].reshape(-1)


def scatter_norms(terms, own):
    filled = TILE * ((own + TILE - 1) // TILE)
    rows = jnp.pad(terms.reshape(-1, own), ((0, 0), (0, filled - own))).reshape(-1, 128)
    return lax.psum_scatter(rows, ("dp", "tensor"), scatter_dimension=0, tiled=True).reshape(-1)[:own]


def per_device(
    tokens,
    cotangent,
    doc_lengths,
    key_weights,
    value_weights,
    out_weights,
    up_weights,
    down_weights,
    key_momentum,
    value_momentum,
    out_momentum,
    up_momentum,
    down_momentum,
    norm_params,
    norm_first,
    norm_second,
):
    tensor_count = lax.axis_size("tensor")
    tensor_index = lax.axis_index("tensor")
    heads = H // tensor_count
    width = tokens.shape[1]
    keys_local = key_weights.shape[2]
    values_local = value_weights.shape[2]
    hidden_local = up_weights.shape[2]
    value_total = values_local * tensor_count
    block = min(LEN, 512)
    ring = Ring()

    def low_t(matrix):
        return matrix.astype(jnp.bfloat16).T

    gathered_norms = gather_norms(ring, norm_params)
    attend_lanes = gather_lanes(
        ring,
        jnp.concatenate(
            [low_t(key_weights[0]), low_t(key_weights[1]), low_t(value_weights[0]), low_t(value_weights[1])]
        ),
    )
    out_lanes = gather_lanes(ring, out_weights.astype(jnp.bfloat16))
    upper_lanes = gather_lanes(ring, jnp.concatenate([low_t(up_weights[0]), low_t(up_weights[1])]))
    down_lanes = gather_lanes(ring, down_weights.astype(jnp.bfloat16))
    half = ring.half
    run(attend_lanes, half)
    quarter = half // 4
    run(out_lanes, quarter)
    attend_full = assemble(attend_lanes)

    gain_one = gathered_norms[:width]
    gain_two = gathered_norms[width : 2 * width]
    group_gain = lax.dynamic_slice_in_dim(
        gathered_norms, 2 * width + tensor_index * values_local, values_local
    )[:, None]
    group_bias = lax.dynamic_slice_in_dim(
        gathered_norms, 2 * width + value_total + tensor_index * values_local, values_local
    )[:, None]
    starts_all = jnp.cumsum(doc_lengths[0]) - doc_lengths[0]
    positions = jnp.arange(LEN)
    doc_ids = jnp.sum((positions[:, None] >= starts_all[None, :]).astype(jnp.int32), axis=1) - 1

    inputs = tokens.astype(jnp.float32)
    scale_one = root_scale(inputs)
    normed_one = inputs * scale_one
    normed_all = gather_tokens((normed_one * gain_one).astype(jnp.bfloat16))
    rows_total = normed_all.shape[0]
    grad_rows_two = gather_tokens(tie(cotangent, normed_all))

    gate_row = 2 * keys_local + values_local
    attend = dot(attend_full[:gate_row], normed_all, 1, 1).astype(jnp.bfloat16)
    attend = tie(attend, reached(out_lanes, quarter))
    run(out_lanes, quarter, attend)
    query = attend[:keys_local].reshape(heads, KEY_HEAD_SIZE, rows_total)
    key = attend[keys_local : 2 * keys_local].reshape(heads, KEY_HEAD_SIZE, rows_total)
    value = attend[2 * keys_local :].reshape(heads, DV, rows_total)
    head_ids = (tensor_index * heads + jnp.arange(heads)).astype(jnp.float32)
    log_gamma = jnp.log(1.0 - jnp.exp2(-5.0 - head_ids))
    mixed_heads = retention_forward(query, key, value, doc_ids, log_gamma, block)
    mixed_heads = tie(mixed_heads, reached(out_lanes, 2 * quarter))
    run(out_lanes, half - 2 * quarter, mixed_heads)
    out_full = assemble(out_lanes)
    run(upper_lanes, half)
    run(down_lanes, half // 2)
    upper_full = assemble(upper_lanes)
    gate_pre = dot(attend_full[gate_row:], tie(normed_all, mixed_heads), 1, 1)
    centred = mixed_heads - jnp.mean(mixed_heads, axis=1, keepdims=True)
    group_scale = lax.rsqrt(jnp.mean(centred * centred, axis=1, keepdims=True) + group_floor)
    group_hat = centred * group_scale
    group_flat = group_hat.reshape(values_local, rows_total)
    group_out = group_flat * group_gain + group_bias
    gate_act, silu_pull = jax.vjp(jax.nn.silu, gate_pre)
    mixed_low = (gate_act * group_out).astype(jnp.bfloat16)
    mixed_low, grad_rows_two = tie((mixed_low, grad_rows_two), reached(out_lanes, half))
    branch_one = scatter_tokens(dot(mixed_low, out_full, 0, 0))
    middle = inputs + tie(branch_one, reached(upper_lanes, half // 2))
    scale_two = root_scale(middle)
    normed_two = middle * scale_two
    second_all = gather_tokens((normed_two * gain_two).astype(jnp.bfloat16))
    second_all = tie(second_all, reached(down_lanes, half // 2))
    run(down_lanes, half - half // 2, second_all)
    down_full = assemble(down_lanes)
    hidden_gate = dot(upper_full[:hidden_local], second_all, 1, 1)
    hidden_upper = dot(upper_full[hidden_local:], second_all, 1, 1)
    gelu_gate, gelu_pull = jax.vjp(partial(jax.nn.gelu, approximate=False), hidden_gate)
    hidden_low = (gelu_gate * hidden_upper).astype(jnp.bfloat16)

    grad_result = cotangent.astype(jnp.float32)
    grad_down = dot(hidden_low, grad_rows_two, 1, 0).astype(jnp.bfloat16)
    down_back = scatter_lanes(ring, grad_down)
    run(down_back, half)
    grad_hidden = dot(down_full, tie(grad_rows_two, grad_down), 1, 1)
    grad_gate_mlp = gelu_pull(grad_hidden * hidden_upper)[0].astype(jnp.bfloat16)
    grad_upper_mlp = (grad_hidden * gelu_gate).astype(jnp.bfloat16)
    grad_hidden_low = jnp.concatenate([grad_gate_mlp, grad_upper_mlp])
    grad_hidden_low = tie(grad_hidden_low, reached(down_back, half // 2))
    grad_second = dot(grad_hidden_low, upper_full, 0, 0).astype(jnp.bfloat16)
    grad_second, grad_hidden_late = tie((grad_second, grad_hidden_low))
    grad_second_local = scatter_tokens(grad_second)
    upper_back = scatter_lanes(ring, dot(grad_hidden_late, second_all, 1, 0).astype(jnp.bfloat16))
    run(upper_back, half)
    grad_second_local = tie(grad_second_local, reached(upper_back, half // 4))
    grad_gain_two = jnp.sum(grad_second_local * normed_two, axis=0)
    grad_middle = grad_result + norm_back(grad_second_local * gain_two, normed_two, scale_two)
    grad_rows_one = gather_tokens(grad_middle.astype(jnp.bfloat16))
    grad_rows_one = tie(grad_rows_one, reached(upper_back, half * 3 // 4))
    out_back = scatter_lanes(ring, dot(mixed_low, grad_rows_one, 1, 0).astype(jnp.bfloat16))
    run(out_back, half)
    result_low = tie(hidden_low, grad_rows_one)
    branch_two = scatter_tokens(dot(result_low, down_full, 0, 0))
    result = middle + branch_two
    grad_mixed = dot(out_full, tie(grad_rows_one, reached(upper_back, half)), 1, 1)
    grad_gate_low = silu_pull(grad_mixed * group_out)[0].astype(jnp.bfloat16)
    grad_group = grad_mixed * gate_act
    grad_group_gain = jnp.sum(grad_group * group_flat, axis=1)
    grad_group_bias = jnp.sum(grad_group, axis=1)
    grad_hat = (grad_group * group_gain).reshape(heads, DV, rows_total)
    grad_heads = group_scale * (
        grad_hat
        - jnp.mean(grad_hat, axis=1, keepdims=True)
        - group_hat * jnp.mean(grad_hat * group_hat, axis=1, keepdims=True)
    )
    grad_heads = tie(grad_heads, reached(out_back, half // 4))
    grad_queries, grad_keys, grad_values = retention_backward(
        query, key, value, grad_heads.astype(jnp.bfloat16), doc_ids, log_gamma, block
    )
    grad_attend_low = jnp.concatenate(
        [
            grad_queries.astype(jnp.bfloat16).reshape(keys_local, rows_total),
            grad_keys.astype(jnp.bfloat16).reshape(keys_local, rows_total),
            grad_values.astype(jnp.bfloat16).reshape(values_local, rows_total),
            grad_gate_low,
        ]
    )
    grad_attend_low = tie(grad_attend_low, reached(out_back, half // 2))
    grad_attend = dot(grad_attend_low, normed_all, 1, 0).astype(jnp.bfloat16)
    grad_attend, grad_attend_late = tie((grad_attend, grad_attend_low))
    attend_back = scatter_lanes(ring, grad_attend)
    run(attend_back, half)
    grad_first = dot(tie(grad_attend_late, reached(attend_back, half // 4)), attend_full, 0, 0).astype(jnp.bfloat16)
    grad_first_local = scatter_tokens(tie(grad_first, branch_two))
    grad_gain_one = jnp.sum(grad_first_local * normed_one, axis=0)
    token_grad = grad_middle + norm_back(grad_first_local * gain_one, normed_one, scale_one)
    group_part = jnp.zeros((2, value_total), jnp.float32)
    group_part = lax.dynamic_update_slice_in_dim(
        group_part, jnp.stack([grad_group_gain, grad_group_bias]), tensor_index * values_local, 1
    )
    norm_terms = jnp.concatenate([grad_gain_one, grad_gain_two, group_part.reshape(-1)])
    norm_grad = scatter_norms(norm_terms, norm_params.shape[0])
    grad_down_w = totals(down_back)
    grad_upper_w = totals(upper_back)
    grad_out_w = totals(out_back)
    grad_attend_w = totals(attend_back)

    fresh_query = momentum_decay * key_momentum[0] + grad_attend_w[:keys_local].T
    fresh_key = momentum_decay * key_momentum[1] + grad_attend_w[keys_local : 2 * keys_local].T
    fresh_value = momentum_decay * value_momentum[0] + grad_attend_w[2 * keys_local : gate_row].T
    fresh_gate = momentum_decay * value_momentum[1] + grad_attend_w[gate_row:].T
    fresh_out = momentum_decay * out_momentum + grad_out_w
    fresh_hidden = momentum_decay * up_momentum[0] + grad_upper_w[:hidden_local].T
    fresh_upper = momentum_decay * up_momentum[1] + grad_upper_w[hidden_local:].T
    fresh_down = momentum_decay * down_momentum + grad_down_w
    orth = orthogonalize(
        [
            fresh_query.T,
            fresh_key.T,
            fresh_value.T,
            fresh_gate.T,
            fresh_hidden.T,
            fresh_upper.T,
            fresh_out,
            fresh_down,
        ],
        norm_terms,
    )
    orth = [item.astype(jnp.float32) for item in orth]
    keep_factor = 1.0 - muon_rate * weight_decay

    def rate(rows, cols):
        return muon_rate * math.sqrt(max(1.0, rows / cols))

    new_key_weights = key_weights * keep_factor - rate(width, keys_local) * jnp.stack([orth[0].T, orth[1].T])
    new_value_weights = value_weights * keep_factor - rate(width, values_local) * jnp.stack([orth[2].T, orth[3].T])
    new_upper_weights = up_weights * keep_factor - rate(width, hidden_local) * jnp.stack([orth[4].T, orth[5].T])
    new_out_weights = out_weights * keep_factor - rate(values_local, width) * orth[6]
    new_down_weights = down_weights * keep_factor - rate(hidden_local, width) * orth[7]
    new_norm_first = beta_first * norm_first + (1.0 - beta_first) * norm_grad
    new_norm_second = beta_second * norm_second + (1.0 - beta_second) * norm_grad * norm_grad
    fix_first = 1.0 - beta_first**STEP
    fix_second = 1.0 - beta_second**STEP
    new_norm_params = norm_params - adam_rate * (new_norm_first / fix_first) / (
        jnp.sqrt(new_norm_second / fix_second) + adam_eps
    )
    return (
        result.astype(jnp.bfloat16),
        token_grad,
        jnp.stack([fresh_query, fresh_key]),
        jnp.stack([fresh_value, fresh_gate]),
        fresh_out,
        jnp.stack([fresh_hidden, fresh_upper]),
        fresh_down,
        new_key_weights,
        new_value_weights,
        new_out_weights,
        new_upper_weights,
        new_down_weights,
        new_norm_first,
        new_norm_second,
        new_norm_params,
    )


def solution(mesh):
    tokens = P(("dp", "tensor"), None)
    wide = P(None, "dp", "tensor")
    tall = P("tensor", "dp")
    norms = P(("dp", "tensor"))
    return jax.shard_map(
        per_device,
        mesh=mesh,
        in_specs=(
            tokens, tokens, P("dp", None), wide, wide, tall, wide, tall,
            wide, wide, tall, wide, tall, norms, norms, norms,
        ),
        out_specs=(
            tokens, tokens, wide, wide, tall, wide, tall,
            wide, wide, tall, wide, tall, norms, norms, norms,
        ),
        check_vma=False,
    )
```

```python
from functools import partial
import math

import jax
import jax.numpy as jnp
from jax import lax
from jax.experimental import pallas as pl
from jax.experimental.pallas import tpu as pltpu
from jax.sharding import PartitionSpec as P

H = 8
KEY_HEAD_SIZE = 256
DV = 432
LEN = 1024
NS_ITERS = 5
STEP = 10


eps_norm = 1e-05
group_floor = 1.0
ns_first = 3.4445
ns_second = -4.775
ns_third = 2.0315
momentum_decay = 0.95
muon_rate = 0.5
weight_decay = 0.1
beta_first = 0.9
beta_second = 0.95
adam_rate = 0.8
adam_eps = 1e-08
TILE = 1024


def root_scale(values):
    return lax.rsqrt(jnp.mean(values * values, axis=-1, keepdims=True) + eps_norm)


def norm_back(grad_normed, normed, scaling):
    return scaling * (grad_normed - normed * jnp.mean(grad_normed * normed, axis=-1, keepdims=True))


def dot(left, right, left_dim, right_dim):
    return lax.dot_general(
        left, right, (((left_dim,), (right_dim,)), ((), ())), preferred_element_type=jnp.float32
    )


def gather_tokens(values):
    return lax.all_gather(values, "tensor", axis=0, tiled=True)


def scatter_tokens(values):
    return lax.psum_scatter(
        values.astype(jnp.bfloat16), "tensor", scatter_dimension=0, tiled=True
    ).astype(jnp.float32)


def ring_order(count):
    return list(range(0, count, 2)) + list(range(count - 1, 0, -2))


def ring_place(count):
    order = ring_order(count)
    return order, [(order[i], order[(i + 1) % count]) for i in range(count)]


def tie(value, *others):
    return lax.optimization_barrier((value, others))[0]


class Ring:
    def __init__(self):
        self.count = lax.axis_size("dp")
        order, self.right = ring_place(self.count)
        self.left = [(b, a) for a, b in self.right]
        self.half = self.count // 2
        place_of = [order.index(rank) for rank in range(self.count)]
        place = jnp.asarray(place_of, jnp.int32)[lax.axis_index("dp")]
        steps = jnp.arange(self.count, dtype=jnp.int32)
        self.rank_at = jnp.asarray(order, jnp.int32)[(place + steps) % self.count]
        self.sent = []
        self.added = None

    def rank(self, distance):
        return self.rank_at[distance % self.count]

    def exchange(self, blocks):
        if len(self.sent) > 2:
            blocks = tie(blocks, self.sent[-3])
        got = {}
        for side, block in blocks.items():
            got[side] = lax.ppermute(block, "dp", self.right if side > 0 else self.left)
        self.sent.append(got)
        return got


class Gather:
    def __init__(self, ring, shard, long_side):
        self.ring = ring
        self.shard = shard
        self.long_side = long_side
        self.rows, self.width = shard.shape
        self.blocks = [(shard, 0)]
        self.held = {1: shard, -1: shard}
        self.marks = []

    def step(self, after=None):
        at = len(self.marks) + 1
        sides = (1, -1) if at < self.ring.half else (self.long_side,)
        blocks = {side: self.held[side] for side in sides}
        if after is not None:
            blocks = tie(blocks, after)
        self.held = self.ring.exchange(blocks)
        self.blocks += [(self.held[side], -side * at) for side in sides]
        self.marks.append(self.held)


def run(lanes, rounds, after=None):
    for turn in range(rounds):
        for lane in lanes:
            lane.step(after if turn == 0 else None)


def reached(lanes, rounds):
    return [lane.marks[rounds - 1] for lane in lanes]


def assemble_kernel(places, rank_ref, *refs):
    out_ref, sems = refs[-2], refs[-1]
    copies = []
    for index, (row, rows, width, distance) in enumerate(places):
        column = pl.ds(pl.multiple_of(rank_ref[distance] * width, width), width)
        copies.append(
            pltpu.make_async_copy(refs[index], out_ref.at[pl.ds(row, rows), column], sems.at[index])
        )
    for copy in copies:
        copy.start()
    for copy in copies:
        copy.wait()


def assemble(lanes):
    ring = lanes[0].ring
    width = lanes[0].width
    rows = sum(lane.rows for lane in lanes)
    dtype = lanes[0].shard.dtype
    blocks, places, base = [], [], 0
    for lane in lanes:
        for block, distance in lane.blocks:
            blocks.append(block)
            places.append((base, lane.rows, width, distance % ring.count))
        base += lane.rows
    if width % 128 or any(lane.rows % 16 for lane in lanes):
        full = jnp.zeros((rows, width * ring.count), dtype)
        for block, (row, _, _, distance) in zip(blocks, places):
            full = lax.dynamic_update_slice(full, block, (row, ring.rank(distance) * width))
        return full
    return pl.pallas_call(
        partial(assemble_kernel, places),
        out_shape=jax.ShapeDtypeStruct((rows, width * ring.count), dtype),
        in_specs=[pl.BlockSpec(memory_space=pltpu.SMEM)] + [pl.BlockSpec(memory_space=pl.ANY)] * len(blocks),
        out_specs=pl.BlockSpec(memory_space=pl.ANY),
        scratch_shapes=[pltpu.SemaphoreType.DMA((len(blocks),))],
        cost_estimate=pl.CostEstimate(
            flops=0, bytes_accessed=4 * rows * width * ring.count, transcendentals=0
        ),
    )(ring.rank_at, *blocks)


class Scatter:
    def __init__(self, ring, full, first, rows, long_side):
        self.ring = ring
        self.full = full
        self.first = first
        self.rows = rows
        self.long_side = long_side
        self.width = full.shape[1] // ring.count
        self.held = {}
        self.marks = []

    def piece(self, distance):
        column = self.ring.rank(distance) * self.width
        return lax.dynamic_slice(self.full, (self.first, column), (self.rows, self.width))

    def step(self, after=None):
        ring = self.ring
        at = ring.half - len(self.marks)
        came = self.held
        if came and ring.added is not None:
            came = tie(came, ring.added)
        sides = (1, -1) if at < ring.half else (self.long_side,)
        blocks = {}
        for side in sides:
            block = self.piece(side * at)
            if side in came:
                block = (block.astype(jnp.float32) + came[side].astype(jnp.float32)).astype(jnp.bfloat16)
            blocks[side] = block
        if came:
            ring.added = blocks
        self.held = ring.exchange(blocks)
        self.marks.append(self.held)

    def total(self):
        own = self.piece(0).astype(jnp.float32)
        return own + self.held[1].astype(jnp.float32) + self.held[-1].astype(jnp.float32)


def halves(rows):
    cut = (rows // 2 + 15) // 16 * 16
    return [(0, cut, 1), (cut, rows - cut, -1)]


def gather_lanes(ring, shard):
    return [Gather(ring, shard[first : first + size], side) for first, size, side in halves(shard.shape[0])]


def scatter_lanes(ring, full):
    return [Scatter(ring, full, first, size, side) for first, size, side in halves(full.shape[0])]


def totals(lanes):
    return jnp.concatenate([lane.total() for lane in lanes])


def decay_rows(doc_ids, log_gamma, first, size, keys):
    query_pos = first + jnp.arange(size)
    key_pos = jnp.arange(keys)
    distance = query_pos[:, None] - key_pos[None, :]
    allowed = (doc_ids[first : first + size, None] == doc_ids[None, :keys]) & (distance >= 0)
    steps_back = jnp.maximum(distance, 0).astype(jnp.float32)
    falloff = jnp.exp(log_gamma[:, None, None] * steps_back[None])
    return jnp.where(allowed[None], falloff, 0.0)


def einsum32(spec, left, right):
    return jnp.einsum(spec, left, right, preferred_element_type=jnp.float32)


def retention_forward(query, key, value, doc_ids, log_gamma, block):
    factor = KEY_HEAD_SIZE ** (-0.5)
    pieces = []
    for first in range(0, LEN, block):
        keys = first + block
        falloff = decay_rows(doc_ids, log_gamma, first, block, keys)
        scores = einsum32("hdq,hdk->hqk", query[:, :, first:keys], key[:, :, :keys]) * factor
        weights = (scores * falloff).astype(jnp.bfloat16)
        pieces.append(einsum32("hdk,hqk->hdq", value[:, :, :keys], weights))
    return jnp.concatenate(pieces, axis=2)


def retention_backward(query, key, value, grad, doc_ids, log_gamma, block):
    factor = KEY_HEAD_SIZE ** (-0.5)
    grad_query = []
    grad_key = jnp.zeros(key.shape, jnp.float32)
    grad_value = jnp.zeros(value.shape, jnp.float32)
    for first in range(0, LEN, block):
        keys = first + block
        falloff = decay_rows(doc_ids, log_gamma, first, block, keys)
        query_now, grad_now = query[:, :, first:keys], grad[:, :, first:keys]
        scores = einsum32("hdq,hdk->hqk", query_now, key[:, :, :keys]) * factor
        weights = (scores * falloff).astype(jnp.bfloat16)
        grad_weights = einsum32("hdq,hdk->hqk", grad_now, value[:, :, :keys])
        grad_scores = (grad_weights * falloff).astype(jnp.bfloat16)
        grad_query.append(einsum32("hdk,hqk->hdq", key[:, :, :keys], grad_scores) * factor)
        grad_key = grad_key.at[:, :, :keys].add(einsum32("hdq,hqk->hdk", query_now, grad_scores) * factor)
        grad_value = grad_value.at[:, :, :keys].add(einsum32("hdq,hqk->hdk", grad_now, weights))
    return jnp.concatenate(grad_query, axis=2), grad_key, grad_value


def newton_schulz_kernel(turns, step, in_ref, out_ref, cur_ref, low_ref, rest_ref, poly_ref, scale_ref):
    parts, size, cols = in_ref.shape
    width = parts * cols
    band = 256
    blocks = size // step

    def rows_of(index):
        return pl.ds(pl.multiple_of(index * step, step), step)

    def first_sum(index, total):
        rows = rows_of(index)
        for part in range(parts):
            block = in_ref[part, rows, :].astype(jnp.float32)
            total = total + jnp.sum(block * block)
        return total

    total = lax.fori_loop(0, blocks, first_sum, jnp.float32(0.0))
    scale_ref[...] = 1.0 / (jnp.sqrt(jnp.full(scale_ref.shape, total)) + 1e-07)

    @pl.loop(0, blocks)
    def _(index):
        rows = rows_of(index)
        scale = scale_ref[0, 0]
        for part in range(parts):
            block = in_ref[part, rows, :].astype(jnp.float32) * scale
            columns = pl.ds(part * cols, cols)
            cur_ref[rows, columns] = block
            low_ref[0, rows, columns] = block.astype(jnp.bfloat16)

    bands = [(first, min(256, size - first)) for first in range(0, size, 256)]

    def turn_body(turn, norm, last):
        here = lax.rem(turn, 2)
        there = 1 - here
        middle = norm * (1.0 / size)
        low = low_ref.at[here]
        for first, wide in bands:
            gram = dot(low[...], low[first : first + wide, :], 1, 1)
            place = lax.broadcasted_iota(jnp.int32, gram.shape, 0)
            eye = place == lax.broadcasted_iota(jnp.int32, gram.shape, 1) + first
            rest_ref[:, first : first + wide] = jnp.where(eye, gram - middle, gram).astype(jnp.bfloat16)
        for first, wide in bands:
            rest = rest_ref[:, first : first + wide]
            square = dot(rest_ref[...], rest, 1, 0)
            poly = (ns_second + 2.0 * ns_third * middle) * rest.astype(jnp.float32) + ns_third * square
            poly_ref[:, first : first + wide] = poly.astype(jnp.bfloat16)
        outer = ns_first + middle * (ns_second + ns_third * middle)

        def part_body(part, total):
            columns = pl.ds(pl.multiple_of(part * band, band), band)
            fresh = outer * cur_ref[:, columns] + dot(poly_ref[...], low[:, columns], 1, 0)
            if last:
                out_ref[part // (cols // band), :, pl.ds(lax.rem(part, cols // band) * band, band)] = fresh.astype(jnp.bfloat16)
            else:
                cur_ref[:, columns] = fresh
                low_ref[there, :, columns] = fresh.astype(jnp.bfloat16)
                total = total + jnp.sum(fresh * fresh, axis=0, keepdims=True)
            return total

        total = lax.fori_loop(0, width // band, part_body, jnp.zeros((1, band), jnp.float32))
        return jnp.sum(total)

    norm = lax.fori_loop(0, turns - 1, lambda turn, norm: turn_body(turn, norm, False), jnp.float32(1.0))
    turn_body(turns - 1, norm, True)


def newton_schulz(block):
    parts, size, cols = block.shape
    width = parts * cols
    step = next(step for step in range(288, 0, -16) if size % step == 0)
    products = 2 * size * size * (2 * width + size) * NS_ITERS
    return pl.pallas_call(
        partial(newton_schulz_kernel, NS_ITERS, step),
        out_shape=jax.ShapeDtypeStruct(block.shape, jnp.bfloat16),
        in_specs=[pl.BlockSpec(memory_space=pltpu.VMEM)],
        out_specs=pl.BlockSpec(memory_space=pltpu.VMEM),
        scratch_shapes=[
            pltpu.VMEM((size, width), jnp.float32),
            pltpu.VMEM((2, size, width), jnp.bfloat16),
            pltpu.VMEM((size, size), jnp.bfloat16),
            pltpu.VMEM((size, size), jnp.bfloat16),
            pltpu.VMEM((8, 128), jnp.float32),
        ],
        compiler_params=pltpu.CompilerParams(vmem_limit_bytes=48 * 1024 * 1024),
        cost_estimate=pl.CostEstimate(flops=products, bytes_accessed=4 * size * width, transcendentals=0),
    )(block)


def orthogonalize(slabs, after):
    ranks = lax.axis_size("dp")
    widest = max(slab.shape[0] for slab in slabs)
    cols = slabs[0].shape[1]
    padded = [jnp.pad(slab.astype(jnp.bfloat16), ((0, widest - slab.shape[0]), (0, 0))) for slab in slabs]
    each = (len(slabs) + ranks - 1) // ranks
    padded += [jnp.zeros((widest, cols), jnp.bfloat16)] * (each * ranks - len(slabs))
    stacked = jnp.stack(padded)
    owned = lax.all_to_all(stacked.reshape(ranks, each, widest, cols), "dp", 0, 0, tiled=True)
    owned = tie(owned, after)
    done = []
    for index in range(each):
        mine = owned[:, index]
        if cols % 128:
            mine = jnp.moveaxis(mine, 0, 1).reshape(1, widest, ranks * cols)
        item = newton_schulz(mine)
        if cols % 128:
            item = jnp.moveaxis(item.reshape(widest, ranks, cols), 1, 0)
        done.append(item)
    ready = jnp.stack(done, axis=1)
    returned = lax.all_to_all(ready, "dp", 0, 0, tiled=True).reshape(each * ranks, widest, cols)
    return [returned[index, : slab.shape[0]] for index, slab in enumerate(slabs)]


def rotated(value, axis, turn):
    count = lax.axis_size(axis)
    return lax.ppermute(value, axis, [(i, (i + turn) % count) for i in range(count)])


def gather_norms(norm_params):
    own = norm_params.shape[0]
    filled = TILE * ((own + TILE - 1) // TILE)
    held = jnp.pad(norm_params, (0, filled - own)).reshape(filled // 128, 128)
    for axis in ("tensor", "dp"):
        count = lax.axis_size(axis)
        index = lax.axis_index(axis)
        held = held[None]
        start = (0,) * (held.ndim - 1)
        whole = jnp.zeros((count,) + held.shape[1:], held.dtype)
        whole = lax.dynamic_update_slice(whole, held, (index,) + start)
        for turn in range(1, count):
            whole = lax.dynamic_update_slice(whole, rotated(held, axis, turn), ((index - turn) % count,) + start)
        held = whole
    return held.reshape(-1, filled)[:, :own].reshape(-1)


def sum_norms(terms):
    for axis in ("tensor", "dp"):
        count = lax.axis_size(axis)
        bit = 1
        while bit < count:
            terms = terms + lax.ppermute(terms, axis, [(i, i ^ bit) for i in range(count)])
            bit *= 2
    return terms


def per_device(
    tokens,
    cotangent,
    doc_lengths,
    key_weights,
    value_weights,
    out_weights,
    up_weights,
    down_weights,
    key_momentum,
    value_momentum,
    out_momentum,
    up_momentum,
    down_momentum,
    norm_params,
    norm_first,
    norm_second,
):
    tensor_count = lax.axis_size("tensor")
    tensor_index = lax.axis_index("tensor")
    heads = H // tensor_count
    width = tokens.shape[1]
    keys_local = key_weights.shape[2]
    values_local = value_weights.shape[2]
    hidden_local = up_weights.shape[2]
    value_total = values_local * tensor_count
    block = min(LEN, 512)
    ring = Ring()
    half = ring.half
    quarter = half // 4

    def low_t(matrix):
        return matrix.astype(jnp.bfloat16).T

    attend_lanes = gather_lanes(
        ring,
        jnp.concatenate(
            [low_t(key_weights[0]), low_t(key_weights[1]), low_t(value_weights[0]), low_t(value_weights[1])]
        ),
    )
    out_lanes = [Gather(ring, out_weights.astype(jnp.bfloat16), 1)]
    upper_lanes = gather_lanes(ring, jnp.concatenate([low_t(up_weights[0]), low_t(up_weights[1])]))
    down_lanes = [Gather(ring, down_weights.astype(jnp.bfloat16), -1)]
    tokens_all = gather_tokens(tokens)
    gathered_norms = gather_norms(norm_params)
    run(attend_lanes, 2 * quarter)
    run(attend_lanes, quarter, gathered_norms)

    gain_one = gathered_norms[:width]
    gain_two = gathered_norms[width : 2 * width]
    group_gain = lax.dynamic_slice_in_dim(
        gathered_norms, 2 * width + tensor_index * values_local, values_local
    )[:, None]
    group_bias = lax.dynamic_slice_in_dim(
        gathered_norms, 2 * width + value_total + tensor_index * values_local, values_local
    )[:, None]
    starts_all = jnp.cumsum(doc_lengths[0]) - doc_lengths[0]
    positions = jnp.arange(LEN)
    doc_ids = jnp.sum((positions[:, None] >= starts_all[None, :]).astype(jnp.int32), axis=1) - 1

    inputs = tokens.astype(jnp.float32)
    scale_one = root_scale(inputs)
    normed_one = inputs * scale_one
    inputs_all = tokens_all.astype(jnp.float32)
    normed_all = (inputs_all * root_scale(inputs_all) * gain_one).astype(jnp.bfloat16)
    rows_total = normed_all.shape[0]
    grad_rows_two = gather_tokens(tie(cotangent, tokens_all))
    run(attend_lanes, half - 3 * quarter, normed_all)
    run(out_lanes, quarter)
    attend_full = assemble(attend_lanes)

    gate_row = 2 * keys_local + values_local
    attend = dot(attend_full[:gate_row], normed_all, 1, 1).astype(jnp.bfloat16)
    attend = tie(attend, reached(out_lanes, quarter))
    run(out_lanes, quarter, attend)
    query = attend[:keys_local].reshape(heads, KEY_HEAD_SIZE, rows_total)
    key = attend[keys_local : 2 * keys_local].reshape(heads, KEY_HEAD_SIZE, rows_total)
    value = attend[2 * keys_local :].reshape(heads, DV, rows_total)
    head_ids = (tensor_index * heads + jnp.arange(heads)).astype(jnp.float32)
    log_gamma = jnp.log(1.0 - jnp.exp2(-5.0 - head_ids))
    mixed_heads = retention_forward(query, key, value, doc_ids, log_gamma, block)
    mixed_heads = tie(mixed_heads, reached(out_lanes, 2 * quarter))
    run(out_lanes, half - 2 * quarter, mixed_heads)
    out_full = assemble(out_lanes)
    run(upper_lanes, half)
    run(down_lanes, 2 * quarter)
    upper_full = assemble(upper_lanes)
    gate_pre = dot(attend_full[gate_row:], tie(normed_all, mixed_heads), 1, 1)
    centred = mixed_heads - jnp.mean(mixed_heads, axis=1, keepdims=True)
    group_scale = lax.rsqrt(jnp.mean(centred * centred, axis=1, keepdims=True) + group_floor)
    group_hat = centred * group_scale
    group_flat = group_hat.reshape(values_local, rows_total)
    group_out = group_flat * group_gain + group_bias
    gate_act, silu_pull = jax.vjp(jax.nn.silu, gate_pre)
    mixed_low = (gate_act * group_out).astype(jnp.bfloat16)
    mixed_low, grad_rows_two = tie((mixed_low, grad_rows_two), reached(out_lanes, half))
    branch_one = scatter_tokens(dot(mixed_low, out_full, 0, 0))
    middle = inputs + tie(branch_one, reached(upper_lanes, 2 * quarter))
    scale_two = root_scale(middle)
    normed_two = middle * scale_two
    second_all = gather_tokens((normed_two * gain_two).astype(jnp.bfloat16))
    second_all = tie(second_all, reached(down_lanes, 2 * quarter))
    run(down_lanes, half - 2 * quarter, second_all)
    down_full = assemble(down_lanes)
    hidden_gate = dot(upper_full[:hidden_local], second_all, 1, 1)
    hidden_upper = dot(upper_full[hidden_local:], second_all, 1, 1)
    gelu_gate, gelu_pull = jax.vjp(partial(jax.nn.gelu, approximate=False), hidden_gate)
    hidden_low = (gelu_gate * hidden_upper).astype(jnp.bfloat16)

    grad_result = cotangent.astype(jnp.float32)
    grad_down = dot(hidden_low, grad_rows_two, 1, 0).astype(jnp.bfloat16)
    down_back = [Scatter(ring, grad_down, 0, hidden_local, -1)]
    run(down_back, half)
    grad_hidden = dot(down_full, tie(grad_rows_two, grad_down), 1, 1)
    grad_gate_mlp = gelu_pull(grad_hidden * hidden_upper)[0].astype(jnp.bfloat16)
    grad_upper_mlp = (grad_hidden * gelu_gate).astype(jnp.bfloat16)
    grad_hidden_low = jnp.concatenate([grad_gate_mlp, grad_upper_mlp])
    grad_hidden_low = tie(grad_hidden_low, reached(down_back, quarter))
    grad_second = dot(grad_hidden_low, upper_full, 0, 0).astype(jnp.bfloat16)
    grad_second, grad_hidden_late = tie((grad_second, grad_hidden_low))
    grad_second_local = scatter_tokens(grad_second)
    upper_back = scatter_lanes(ring, dot(grad_hidden_late, second_all, 1, 0).astype(jnp.bfloat16))
    run(upper_back, half)
    grad_second_local = tie(grad_second_local, reached(upper_back, 2 * quarter))
    grad_gain_two = jnp.sum(grad_second_local * normed_two, axis=0)
    grad_middle = grad_result + norm_back(grad_second_local * gain_two, normed_two, scale_two)
    grad_rows_one = gather_tokens(grad_middle.astype(jnp.bfloat16))
    grad_rows_one = tie(grad_rows_one, reached(upper_back, 3 * quarter))
    out_back = [Scatter(ring, dot(mixed_low, grad_rows_one, 1, 0).astype(jnp.bfloat16), 0, values_local, 1)]
    run(out_back, half)
    grad_mixed = dot(out_full, tie(grad_rows_one, reached(upper_back, half)), 1, 1)
    grad_gate_low = silu_pull(grad_mixed * group_out)[0].astype(jnp.bfloat16)
    gate_back = [Scatter(ring, dot(grad_gate_low, normed_all, 1, 0).astype(jnp.bfloat16), 0, values_local, -1)]
    run(gate_back, half)
    grad_group = grad_mixed * gate_act
    grad_group_gain = jnp.sum(grad_group * group_flat, axis=1)
    grad_group_bias = jnp.sum(grad_group, axis=1)
    grad_hat = (grad_group * group_gain).reshape(heads, DV, rows_total)
    grad_heads = group_scale * (
        grad_hat
        - jnp.mean(grad_hat, axis=1, keepdims=True)
        - group_hat * jnp.mean(grad_hat * group_hat, axis=1, keepdims=True)
    )
    grad_heads = tie(grad_heads, reached(out_back, quarter))
    grad_queries, grad_keys, grad_values = retention_backward(
        query, key, value, grad_heads.astype(jnp.bfloat16), doc_ids, log_gamma, block
    )
    grad_attend_low = jnp.concatenate(
        [
            grad_queries.astype(jnp.bfloat16).reshape(keys_local, rows_total),
            grad_keys.astype(jnp.bfloat16).reshape(keys_local, rows_total),
            grad_values.astype(jnp.bfloat16).reshape(values_local, rows_total),
        ]
    )
    grad_attend_low = tie(grad_attend_low, reached(out_back, 2 * quarter))
    grad_attend = dot(grad_attend_low, normed_all, 1, 0).astype(jnp.bfloat16)
    attend_back = scatter_lanes(ring, grad_attend)
    run(attend_back, half)
    grad_attend_late, grad_gate_late = tie((grad_attend_low, grad_gate_low), reached(attend_back, quarter))
    grad_first = dot(grad_attend_late, attend_full[:gate_row], 0, 0) + dot(
        grad_gate_late, attend_full[gate_row:], 0, 0
    )
    grad_first_local = scatter_tokens(grad_first)
    branch_two = scatter_tokens(dot(tie(hidden_low, grad_first), down_full, 0, 0))
    result = middle + branch_two
    grad_gain_one = jnp.sum(grad_first_local * normed_one, axis=0)
    token_grad = grad_middle + norm_back(grad_first_local * gain_one, normed_one, scale_one)
    group_part = jnp.zeros((2, value_total), jnp.float32)
    group_part = lax.dynamic_update_slice_in_dim(
        group_part, jnp.stack([grad_group_gain, grad_group_bias]), tensor_index * values_local, 1
    )
    norm_terms = jnp.concatenate([grad_gain_one, grad_gain_two, group_part.reshape(-1)])
    norm_sum = sum_norms(norm_terms)
    own_norms = norm_params.shape[0]
    norm_place = lax.axis_index("dp") * tensor_count + tensor_index
    norm_grad = lax.dynamic_slice_in_dim(norm_sum, norm_place * own_norms, own_norms)
    grad_down_w = totals(down_back)
    grad_upper_w = totals(upper_back)
    grad_out_w = totals(out_back)
    grad_gate_w = totals(gate_back)
    grad_attend_w = totals(attend_back)

    fresh_query = momentum_decay * key_momentum[0] + grad_attend_w[:keys_local].T
    fresh_key = momentum_decay * key_momentum[1] + grad_attend_w[keys_local : 2 * keys_local].T
    fresh_value = momentum_decay * value_momentum[0] + grad_attend_w[2 * keys_local :].T
    fresh_gate = momentum_decay * value_momentum[1] + grad_gate_w.T
    fresh_out = momentum_decay * out_momentum + grad_out_w
    fresh_hidden = momentum_decay * up_momentum[0] + grad_upper_w[:hidden_local].T
    fresh_upper = momentum_decay * up_momentum[1] + grad_upper_w[hidden_local:].T
    fresh_down = momentum_decay * down_momentum + grad_down_w
    orth = orthogonalize(
        [
            fresh_down,
            fresh_hidden.T,
            fresh_upper.T,
            fresh_out,
            fresh_gate.T,
            fresh_value.T,
            fresh_query.T,
            fresh_key.T,
        ],
        norm_sum,
    )
    orth = [item.astype(jnp.float32) for item in orth]
    keep_factor = 1.0 - muon_rate * weight_decay

    def rate(rows, cols):
        return muon_rate * math.sqrt(max(1.0, rows / cols))

    new_key_weights = key_weights * keep_factor - rate(width, keys_local) * jnp.stack([orth[6].T, orth[7].T])
    new_value_weights = value_weights * keep_factor - rate(width, values_local) * jnp.stack([orth[5].T, orth[4].T])
    new_upper_weights = up_weights * keep_factor - rate(width, hidden_local) * jnp.stack([orth[1].T, orth[2].T])
    new_out_weights = out_weights * keep_factor - rate(values_local, width) * orth[3]
    new_down_weights = down_weights * keep_factor - rate(hidden_local, width) * orth[0]
    new_norm_first = beta_first * norm_first + (1.0 - beta_first) * norm_grad
    new_norm_second = beta_second * norm_second + (1.0 - beta_second) * norm_grad * norm_grad
    fix_first = 1.0 - beta_first**STEP
    fix_second = 1.0 - beta_second**STEP
    new_norm_params = norm_params - adam_rate * (new_norm_first / fix_first) / (
        jnp.sqrt(new_norm_second / fix_second) + adam_eps
    )
    return (
        result.astype(jnp.bfloat16),
        token_grad,
        jnp.stack([fresh_query, fresh_key]),
        jnp.stack([fresh_value, fresh_gate]),
        fresh_out,
        jnp.stack([fresh_hidden, fresh_upper]),
        fresh_down,
        new_key_weights,
        new_value_weights,
        new_out_weights,
        new_upper_weights,
        new_down_weights,
        new_norm_first,
        new_norm_second,
        new_norm_params,
    )


def solution(mesh):
    tokens = P(("dp", "tensor"), None)
    wide = P(None, "dp", "tensor")
    tall = P("tensor", "dp")
    norms = P(("dp", "tensor"))
    return jax.shard_map(
        per_device,
        mesh=mesh,
        in_specs=(
            tokens, tokens, P("dp", None), wide, wide, tall, wide, tall,
            wide, wide, tall, wide, tall, norms, norms, norms,
        ),
        out_specs=(
            tokens, tokens, wide, wide, tall, wide, tall,
            wide, wide, tall, wide, tall, norms, norms, norms,
        ),
        check_vma=False,
    )
```

```python
from functools import partial
import math

import jax
import jax.numpy as jnp
from jax import lax
from jax.experimental import pallas as pl
from jax.experimental.pallas import tpu as pltpu
from jax.sharding import PartitionSpec as P

H = 8
KEY_HEAD_SIZE = 256
DV = 432
LEN = 1024
NS_ITERS = 5
STEP = 10


eps_norm = 1e-05
group_floor = 1.0
ns_first = 3.4445
ns_second = -4.775
ns_third = 2.0315
momentum_decay = 0.95
muon_rate = 0.5
weight_decay = 0.1
beta_first = 0.9
beta_second = 0.95
adam_rate = 0.8
adam_eps = 1e-08
TILE = 1024


def root_scale(values):
    return lax.rsqrt(jnp.mean(values * values, axis=-1, keepdims=True) + eps_norm)


def norm_back(grad_normed, normed, scaling):
    return scaling * (grad_normed - normed * jnp.mean(grad_normed * normed, axis=-1, keepdims=True))


def dot(left, right, left_dim, right_dim):
    return lax.dot_general(
        left, right, (((left_dim,), (right_dim,)), ((), ())), preferred_element_type=jnp.float32
    )


def gather_tokens(values):
    return lax.all_gather(values, "tensor", axis=0, tiled=True)


def scatter_tokens(values):
    return lax.psum_scatter(
        values.astype(jnp.bfloat16), "tensor", scatter_dimension=0, tiled=True
    ).astype(jnp.float32)


def ring_order(count):
    return list(range(0, count, 2)) + list(range(count - 1, 0, -2))


def ring_place(count):
    order = ring_order(count)
    return order, [(order[i], order[(i + 1) % count]) for i in range(count)]


def tie(value, *others):
    return lax.optimization_barrier((value, others))[0]


class Ring:
    def __init__(self):
        self.count = lax.axis_size("dp")
        order, self.right = ring_place(self.count)
        self.left = [(b, a) for a, b in self.right]
        self.half = self.count // 2
        place_of = [order.index(rank) for rank in range(self.count)]
        place = jnp.asarray(place_of, jnp.int32)[lax.axis_index("dp")]
        steps = jnp.arange(self.count, dtype=jnp.int32)
        self.rank_at = jnp.asarray(order, jnp.int32)[(place + steps) % self.count]
        self.sent = []
        self.added = None

    def rank(self, distance):
        return self.rank_at[distance % self.count]

    def exchange(self, blocks):
        if len(self.sent) > 2:
            blocks = tie(blocks, self.sent[-3])
        got = {}
        for side, block in blocks.items():
            got[side] = lax.ppermute(block, "dp", self.right if side > 0 else self.left)
        self.sent.append(got)
        return got


class Gather:
    def __init__(self, ring, shard, long_side):
        self.ring = ring
        self.shard = shard
        self.long_side = long_side
        self.rows, self.width = shard.shape
        self.blocks = [(shard, 0)]
        self.held = {1: shard, -1: shard}
        self.marks = []

    def step(self, after=None):
        at = len(self.marks) + 1
        sides = (1, -1) if at < self.ring.half else (self.long_side,)
        blocks = {side: self.held[side] for side in sides}
        if after is not None:
            blocks = tie(blocks, after)
        self.held = self.ring.exchange(blocks)
        self.blocks += [(self.held[side], -side * at) for side in sides]
        self.marks.append(self.held)


def run(lanes, rounds, after=None):
    for turn in range(rounds):
        for lane in lanes:
            lane.step(after if turn == 0 else None)


def reached(lanes, rounds):
    return [lane.marks[rounds - 1] for lane in lanes]


def loaded(lanes, rounds):
    return [lane.loads[rounds] for lane in lanes]


def assemble(lanes):
    ring = lanes[0].ring
    width = lanes[0].width
    full = jnp.zeros((sum(lane.rows for lane in lanes), width * ring.count), lanes[0].shard.dtype)
    placed, base = [], 0
    for lane in lanes:
        placed += [(index, base, block, distance) for index, (block, distance) in enumerate(lane.blocks)]
        base += lane.rows
    for _, row, block, distance in sorted(placed, key=lambda item: item[0]):
        full = lax.dynamic_update_slice(full, block, (row, ring.rank(distance) * width))
    return full


class Scatter:
    def __init__(self, ring, full, first, rows, long_side):
        self.ring = ring
        self.full = full
        self.first = first
        self.rows = rows
        self.long_side = long_side
        self.width = full.shape[1] // ring.count
        self.held = {}
        self.marks = []
        self.loads = []

    def piece(self, distance):
        column = self.ring.rank(distance) * self.width
        return lax.dynamic_slice(self.full, (self.first, column), (self.rows, self.width))

    def step(self, after=None):
        ring = self.ring
        at = ring.half - len(self.marks)
        came = self.held
        if came and ring.added is not None:
            came = tie(came, ring.added)
        sides = (1, -1) if at < ring.half else (self.long_side,)
        blocks = {}
        for side in sides:
            block = self.piece(side * at)
            if side in came:
                block = (block.astype(jnp.float32) + came[side].astype(jnp.float32)).astype(jnp.bfloat16)
            blocks[side] = block
        if came:
            ring.added = blocks
        self.loads.append(blocks)
        self.held = ring.exchange(blocks)
        self.marks.append(self.held)

    def total(self):
        own = self.piece(0).astype(jnp.float32)
        return own + self.held[1].astype(jnp.float32) + self.held[-1].astype(jnp.float32)


def halves(rows):
    cut = (rows // 2 + 15) // 16 * 16
    return [(0, cut, 1), (cut, rows - cut, -1)]


def gather_lanes(ring, shard):
    return [Gather(ring, shard[first : first + size], side) for first, size, side in halves(shard.shape[0])]


def scatter_lanes(ring, full):
    return [Scatter(ring, full, first, size, side) for first, size, side in halves(full.shape[0])]


def totals(lanes):
    return jnp.concatenate([lane.total() for lane in lanes])


def decay_rows(doc_ids, log_gamma, first, size, keys):
    query_pos = first + jnp.arange(size)
    key_pos = jnp.arange(keys)
    distance = query_pos[:, None] - key_pos[None, :]
    allowed = (doc_ids[first : first + size, None] == doc_ids[None, :keys]) & (distance >= 0)
    steps_back = jnp.maximum(distance, 0).astype(jnp.float32)
    falloff = jnp.exp(log_gamma[:, None, None] * steps_back[None])
    return jnp.where(allowed[None], falloff, 0.0)


def einsum32(spec, left, right):
    return jnp.einsum(spec, left, right, preferred_element_type=jnp.float32)


def retention_forward(query, key, value, doc_ids, log_gamma, block):
    factor = KEY_HEAD_SIZE ** (-0.5)
    pieces = []
    for first in range(0, LEN, block):
        keys = first + block
        falloff = decay_rows(doc_ids, log_gamma, first, block, keys)
        scores = einsum32("hdq,hdk->hqk", query[:, :, first:keys], key[:, :, :keys]) * factor
        weights = (scores * falloff).astype(jnp.bfloat16)
        pieces.append(einsum32("hdk,hqk->hdq", value[:, :, :keys], weights))
    return jnp.concatenate(pieces, axis=2)


def retention_backward(query, key, value, grad, doc_ids, log_gamma, block):
    factor = KEY_HEAD_SIZE ** (-0.5)
    grad_query = []
    grad_key = jnp.zeros(key.shape, jnp.float32)
    grad_value = jnp.zeros(value.shape, jnp.float32)
    for first in range(0, LEN, block):
        keys = first + block
        falloff = decay_rows(doc_ids, log_gamma, first, block, keys)
        query_now, grad_now = query[:, :, first:keys], grad[:, :, first:keys]
        scores = einsum32("hdq,hdk->hqk", query_now, key[:, :, :keys]) * factor
        weights = (scores * falloff).astype(jnp.bfloat16)
        grad_weights = einsum32("hdq,hdk->hqk", grad_now, value[:, :, :keys])
        grad_scores = (grad_weights * falloff).astype(jnp.bfloat16)
        grad_query.append(einsum32("hdk,hqk->hdq", key[:, :, :keys], grad_scores) * factor)
        grad_key = grad_key.at[:, :, :keys].add(einsum32("hdq,hqk->hdk", query_now, grad_scores) * factor)
        grad_value = grad_value.at[:, :, :keys].add(einsum32("hdq,hqk->hdk", grad_now, weights))
    return jnp.concatenate(grad_query, axis=2), grad_key, grad_value


def newton_schulz_kernel(turns, step, in_ref, out_ref, cur_ref, low_ref, rest_ref, poly_ref, scale_ref):
    parts, size, cols = in_ref.shape
    width = parts * cols
    band = 256
    blocks = size // step

    def rows_of(index):
        return pl.ds(pl.multiple_of(index * step, step), step)

    def first_sum(index, total):
        rows = rows_of(index)
        for part in range(parts):
            block = in_ref[part, rows, :].astype(jnp.float32)
            total = total + jnp.sum(block * block)
        return total

    total = lax.fori_loop(0, blocks, first_sum, jnp.float32(0.0))
    scale_ref[...] = 1.0 / (jnp.sqrt(jnp.full(scale_ref.shape, total)) + 1e-07)

    @pl.loop(0, blocks)
    def _(index):
        rows = rows_of(index)
        scale = scale_ref[0, 0]
        for part in range(parts):
            block = in_ref[part, rows, :].astype(jnp.float32) * scale
            columns = pl.ds(part * cols, cols)
            cur_ref[rows, columns] = block
            low_ref[0, rows, columns] = block.astype(jnp.bfloat16)

    bands = [(first, min(256, size - first)) for first in range(0, size, 256)]

    def turn_body(turn, norm, last):
        here = lax.rem(turn, 2)
        there = 1 - here
        middle = norm * (1.0 / size)
        low = low_ref.at[here]
        for first, wide in bands:
            gram = dot(low[...], low[first : first + wide, :], 1, 1)
            place = lax.broadcasted_iota(jnp.int32, gram.shape, 0)
            eye = place == lax.broadcasted_iota(jnp.int32, gram.shape, 1) + first
            rest_ref[:, first : first + wide] = jnp.where(eye, gram - middle, gram).astype(jnp.bfloat16)
        for first, wide in bands:
            rest = rest_ref[:, first : first + wide]
            square = dot(rest_ref[...], rest, 1, 0)
            poly = (ns_second + 2.0 * ns_third * middle) * rest.astype(jnp.float32) + ns_third * square
            poly_ref[:, first : first + wide] = poly.astype(jnp.bfloat16)
        outer = ns_first + middle * (ns_second + ns_third * middle)

        def part_body(part, total):
            columns = pl.ds(pl.multiple_of(part * band, band), band)
            fresh = outer * cur_ref[:, columns] + dot(poly_ref[...], low[:, columns], 1, 0)
            if last:
                out_ref[part // (cols // band), :, pl.ds(lax.rem(part, cols // band) * band, band)] = fresh.astype(jnp.bfloat16)
            else:
                cur_ref[:, columns] = fresh
                low_ref[there, :, columns] = fresh.astype(jnp.bfloat16)
                total = total + jnp.sum(fresh * fresh, axis=0, keepdims=True)
            return total

        total = lax.fori_loop(0, width // band, part_body, jnp.zeros((1, band), jnp.float32))
        return jnp.sum(total)

    norm = lax.fori_loop(0, turns - 1, lambda turn, norm: turn_body(turn, norm, False), jnp.float32(1.0))
    turn_body(turns - 1, norm, True)


def newton_schulz(block):
    parts, size, cols = block.shape
    width = parts * cols
    step = next(step for step in range(288, 0, -16) if size % step == 0)
    products = 2 * size * size * (2 * width + size) * NS_ITERS
    return pl.pallas_call(
        partial(newton_schulz_kernel, NS_ITERS, step),
        out_shape=jax.ShapeDtypeStruct(block.shape, jnp.bfloat16),
        in_specs=[pl.BlockSpec(memory_space=pltpu.VMEM)],
        out_specs=pl.BlockSpec(memory_space=pltpu.VMEM),
        scratch_shapes=[
            pltpu.VMEM((size, width), jnp.float32),
            pltpu.VMEM((2, size, width), jnp.bfloat16),
            pltpu.VMEM((size, size), jnp.bfloat16),
            pltpu.VMEM((size, size), jnp.bfloat16),
            pltpu.VMEM((8, 128), jnp.float32),
        ],
        compiler_params=pltpu.CompilerParams(vmem_limit_bytes=48 * 1024 * 1024),
        cost_estimate=pl.CostEstimate(flops=products, bytes_accessed=4 * size * width, transcendentals=0),
    )(block)


def orthogonalize(slabs, after):
    ranks = lax.axis_size("dp")
    widest = max(slab.shape[0] for slab in slabs)
    cols = slabs[0].shape[1]
    padded = [jnp.pad(slab.astype(jnp.bfloat16), ((0, widest - slab.shape[0]), (0, 0))) for slab in slabs]
    each = (len(slabs) + ranks - 1) // ranks
    padded += [jnp.zeros((widest, cols), jnp.bfloat16)] * (each * ranks - len(slabs))
    stacked = jnp.stack(padded)
    owned = lax.all_to_all(stacked.reshape(ranks, each, widest, cols), "dp", 0, 0, tiled=True)
    owned = tie(owned, after)
    done = []
    for index in range(each):
        mine = owned[:, index]
        if cols % 128:
            mine = jnp.moveaxis(mine, 0, 1).reshape(1, widest, ranks * cols)
        item = newton_schulz(mine)
        if cols % 128:
            item = jnp.moveaxis(item.reshape(widest, ranks, cols), 1, 0)
        done.append(item)
    ready = jnp.stack(done, axis=1)
    returned = lax.all_to_all(ready, "dp", 0, 0, tiled=True).reshape(each * ranks, widest, cols)
    return [returned[index, : slab.shape[0]] for index, slab in enumerate(slabs)]


def rotated(value, axis, turn):
    count = lax.axis_size(axis)
    return lax.ppermute(value, axis, [(i, (i + turn) % count) for i in range(count)])


def gather_norms(norm_params):
    own = norm_params.shape[0]
    filled = TILE * ((own + TILE - 1) // TILE)
    held = jnp.pad(norm_params, (0, filled - own)).reshape(filled // 128, 128)
    for axis in ("tensor", "dp"):
        count = lax.axis_size(axis)
        index = lax.axis_index(axis)
        held = held[None]
        start = (0,) * (held.ndim - 1)
        whole = jnp.zeros((count,) + held.shape[1:], held.dtype)
        whole = lax.dynamic_update_slice(whole, held, (index,) + start)
        for turn in range(1, count):
            whole = lax.dynamic_update_slice(whole, rotated(held, axis, turn), ((index - turn) % count,) + start)
        held = whole
    return held.reshape(-1, filled)[:, :own].reshape(-1)


def sum_norms(terms):
    for axis in ("tensor", "dp"):
        count = lax.axis_size(axis)
        bit = 1
        while bit < count:
            terms = terms + lax.ppermute(terms, axis, [(i, i ^ bit) for i in range(count)])
            bit *= 2
    return terms


def per_device(
    tokens,
    cotangent,
    doc_lengths,
    key_weights,
    value_weights,
    out_weights,
    up_weights,
    down_weights,
    key_momentum,
    value_momentum,
    out_momentum,
    up_momentum,
    down_momentum,
    norm_params,
    norm_first,
    norm_second,
):
    tensor_count = lax.axis_size("tensor")
    tensor_index = lax.axis_index("tensor")
    heads = H // tensor_count
    width = tokens.shape[1]
    keys_local = key_weights.shape[2]
    values_local = value_weights.shape[2]
    hidden_local = up_weights.shape[2]
    value_total = values_local * tensor_count
    block = min(LEN, 512)
    ring = Ring()
    half = ring.half
    quarter = half // 4

    def low_t(matrix):
        return matrix.astype(jnp.bfloat16).T

    attend_lanes = gather_lanes(
        ring,
        jnp.concatenate(
            [low_t(key_weights[0]), low_t(key_weights[1]), low_t(value_weights[0]), low_t(value_weights[1])]
        ),
    )
    out_lanes = [Gather(ring, out_weights.astype(jnp.bfloat16), 1)]
    upper_lanes = gather_lanes(ring, jnp.concatenate([low_t(up_weights[0]), low_t(up_weights[1])]))
    down_lanes = [Gather(ring, down_weights.astype(jnp.bfloat16), -1)]
    tokens_all = gather_tokens(tokens)
    gathered_norms = gather_norms(norm_params)
    run(attend_lanes, 3 * quarter)

    gain_one = gathered_norms[:width]
    gain_two = gathered_norms[width : 2 * width]
    group_gain = lax.dynamic_slice_in_dim(
        gathered_norms, 2 * width + tensor_index * values_local, values_local
    )[:, None]
    group_bias = lax.dynamic_slice_in_dim(
        gathered_norms, 2 * width + value_total + tensor_index * values_local, values_local
    )[:, None]
    starts_all = jnp.cumsum(doc_lengths[0]) - doc_lengths[0]
    positions = jnp.arange(LEN)
    doc_ids = jnp.sum((positions[:, None] >= starts_all[None, :]).astype(jnp.int32), axis=1) - 1

    inputs = tokens.astype(jnp.float32)
    scale_one = root_scale(inputs)
    normed_one = inputs * scale_one
    inputs_all = tokens_all.astype(jnp.float32)
    normed_all = (inputs_all * root_scale(inputs_all) * gain_one).astype(jnp.bfloat16)
    rows_total = normed_all.shape[0]
    grad_rows_two = gather_tokens(tie(cotangent, tokens_all))
    run(attend_lanes, half - 3 * quarter, normed_all)
    run(out_lanes, quarter)
    attend_full = assemble(attend_lanes)

    gate_row = 2 * keys_local + values_local
    attend = dot(attend_full[:gate_row], normed_all, 1, 1).astype(jnp.bfloat16)
    attend = tie(attend, reached(out_lanes, quarter))
    run(out_lanes, quarter, attend)
    query = attend[:keys_local].reshape(heads, KEY_HEAD_SIZE, rows_total)
    key = attend[keys_local : 2 * keys_local].reshape(heads, KEY_HEAD_SIZE, rows_total)
    value = attend[2 * keys_local :].reshape(heads, DV, rows_total)
    head_ids = (tensor_index * heads + jnp.arange(heads)).astype(jnp.float32)
    log_gamma = jnp.log(1.0 - jnp.exp2(-5.0 - head_ids))
    mixed_heads = retention_forward(query, key, value, doc_ids, log_gamma, block)
    mixed_heads = tie(mixed_heads, reached(out_lanes, 2 * quarter))
    run(out_lanes, half - 2 * quarter, mixed_heads)
    out_full = assemble(out_lanes)
    run(upper_lanes, half)
    run(down_lanes, 2 * quarter)
    upper_full = assemble(upper_lanes)
    gate_pre = dot(attend_full[gate_row:], tie(normed_all, mixed_heads), 1, 1)
    centred = mixed_heads - jnp.mean(mixed_heads, axis=1, keepdims=True)
    group_scale = lax.rsqrt(jnp.mean(centred * centred, axis=1, keepdims=True) + group_floor)
    group_hat = centred * group_scale
    group_flat = group_hat.reshape(values_local, rows_total)
    group_out = group_flat * group_gain + group_bias
    gate_act, silu_pull = jax.vjp(jax.nn.silu, gate_pre)
    mixed_low = (gate_act * group_out).astype(jnp.bfloat16)
    mixed_low, grad_rows_two = tie((mixed_low, grad_rows_two), reached(out_lanes, half))
    branch_one = scatter_tokens(dot(mixed_low, out_full, 0, 0))
    middle = inputs + tie(branch_one, reached(upper_lanes, 2 * quarter))
    scale_two = root_scale(middle)
    normed_two = middle * scale_two
    second_all = gather_tokens((normed_two * gain_two).astype(jnp.bfloat16))
    second_all = tie(second_all, reached(down_lanes, 2 * quarter))
    run(down_lanes, half - 2 * quarter, second_all)
    down_full = assemble(down_lanes)
    hidden_gate = dot(upper_full[:hidden_local], second_all, 1, 1)
    hidden_upper = dot(upper_full[hidden_local:], second_all, 1, 1)
    gelu_gate, gelu_pull = jax.vjp(partial(jax.nn.gelu, approximate=False), hidden_gate)
    hidden_low = (gelu_gate * hidden_upper).astype(jnp.bfloat16)

    grad_result = cotangent.astype(jnp.float32)
    grad_down = dot(hidden_low, grad_rows_two, 1, 0).astype(jnp.bfloat16)
    down_back = [Scatter(ring, grad_down, 0, hidden_local, -1)]
    run(down_back, half)
    grad_hidden = dot(down_full, tie(grad_rows_two, grad_down), 1, 1)
    grad_gate_mlp = gelu_pull(grad_hidden * hidden_upper)[0].astype(jnp.bfloat16)
    grad_upper_mlp = (grad_hidden * gelu_gate).astype(jnp.bfloat16)
    grad_hidden_low = jnp.concatenate([grad_gate_mlp, grad_upper_mlp])
    grad_hidden_low = tie(grad_hidden_low, loaded(down_back, quarter))
    grad_second = dot(grad_hidden_low, upper_full, 0, 0).astype(jnp.bfloat16)
    grad_second, grad_hidden_late = tie((grad_second, grad_hidden_low))
    grad_second_local = scatter_tokens(grad_second)
    upper_back = scatter_lanes(ring, dot(grad_hidden_late, second_all, 1, 0).astype(jnp.bfloat16))
    run(upper_back, half)
    grad_second_local = tie(grad_second_local, loaded(upper_back, 2 * quarter))
    grad_gain_two = jnp.sum(grad_second_local * normed_two, axis=0)
    grad_middle = grad_result + norm_back(grad_second_local * gain_two, normed_two, scale_two)
    grad_rows_one = gather_tokens(grad_middle.astype(jnp.bfloat16))
    grad_rows_one = tie(grad_rows_one, loaded(upper_back, 3 * quarter))
    out_back = [Scatter(ring, dot(mixed_low, grad_rows_one, 1, 0).astype(jnp.bfloat16), 0, values_local, 1)]
    run(out_back, half)
    grad_mixed = dot(out_full, grad_rows_one, 1, 1)
    grad_gate_low = silu_pull(grad_mixed * group_out)[0].astype(jnp.bfloat16)
    gate_back = [Scatter(ring, dot(grad_gate_low, normed_all, 1, 0).astype(jnp.bfloat16), 0, values_local, -1)]
    run(gate_back, half)
    grad_group = grad_mixed * gate_act
    grad_group_gain = jnp.sum(grad_group * group_flat, axis=1)
    grad_group_bias = jnp.sum(grad_group, axis=1)
    grad_hat = (grad_group * group_gain).reshape(heads, DV, rows_total)
    grad_heads = group_scale * (
        grad_hat
        - jnp.mean(grad_hat, axis=1, keepdims=True)
        - group_hat * jnp.mean(grad_hat * group_hat, axis=1, keepdims=True)
    )
    grad_heads = tie(grad_heads, loaded(out_back, quarter))
    grad_queries, grad_keys, grad_values = retention_backward(
        query, key, value, grad_heads.astype(jnp.bfloat16), doc_ids, log_gamma, block
    )
    grad_attend_low = jnp.concatenate(
        [
            grad_queries.astype(jnp.bfloat16).reshape(keys_local, rows_total),
            grad_keys.astype(jnp.bfloat16).reshape(keys_local, rows_total),
            grad_values.astype(jnp.bfloat16).reshape(values_local, rows_total),
        ]
    )
    grad_attend_low = tie(grad_attend_low, loaded(out_back, 2 * quarter))
    grad_attend = dot(grad_attend_low, normed_all, 1, 0).astype(jnp.bfloat16)
    attend_back = scatter_lanes(ring, grad_attend)
    run(attend_back, half)
    grad_attend_late, grad_gate_late = tie((grad_attend_low, grad_gate_low), loaded(attend_back, 2 * quarter))
    grad_first = dot(grad_attend_late, attend_full[:gate_row], 0, 0) + dot(
        grad_gate_late, attend_full[gate_row:], 0, 0
    )
    grad_first_local = scatter_tokens(grad_first)
    branch_two = scatter_tokens(dot(tie(hidden_low, grad_first), down_full, 0, 0))
    result = middle + branch_two
    grad_gain_one = jnp.sum(grad_first_local * normed_one, axis=0)
    token_grad = grad_middle + norm_back(grad_first_local * gain_one, normed_one, scale_one)
    group_part = jnp.zeros((2, value_total), jnp.float32)
    group_part = lax.dynamic_update_slice_in_dim(
        group_part, jnp.stack([grad_group_gain, grad_group_bias]), tensor_index * values_local, 1
    )
    norm_terms = jnp.concatenate([grad_gain_one, grad_gain_two, group_part.reshape(-1)])
    norm_sum = sum_norms(norm_terms)
    own_norms = norm_params.shape[0]
    norm_place = lax.axis_index("dp") * tensor_count + tensor_index
    norm_grad = lax.dynamic_slice_in_dim(norm_sum, norm_place * own_norms, own_norms)
    grad_down_w = totals(down_back)
    grad_upper_w = totals(upper_back)
    grad_out_w = totals(out_back)
    grad_gate_w = totals(gate_back)
    grad_attend_w = totals(attend_back)

    fresh_query = momentum_decay * key_momentum[0] + grad_attend_w[:keys_local].T
    fresh_key = momentum_decay * key_momentum[1] + grad_attend_w[keys_local : 2 * keys_local].T
    fresh_value = momentum_decay * value_momentum[0] + grad_attend_w[2 * keys_local :].T
    fresh_gate = momentum_decay * value_momentum[1] + grad_gate_w.T
    fresh_out = momentum_decay * out_momentum + grad_out_w
    fresh_hidden = momentum_decay * up_momentum[0] + grad_upper_w[:hidden_local].T
    fresh_upper = momentum_decay * up_momentum[1] + grad_upper_w[hidden_local:].T
    fresh_down = momentum_decay * down_momentum + grad_down_w
    orth = orthogonalize(
        [
            fresh_down,
            fresh_hidden.T,
            fresh_upper.T,
            fresh_out,
            fresh_gate.T,
            fresh_value.T,
            fresh_query.T,
            fresh_key.T,
        ],
        norm_sum,
    )
    orth = [item.astype(jnp.float32) for item in orth]
    keep_factor = 1.0 - muon_rate * weight_decay

    def rate(rows, cols):
        return muon_rate * math.sqrt(max(1.0, rows / cols))

    new_key_weights = key_weights * keep_factor - rate(width, keys_local) * jnp.stack([orth[6].T, orth[7].T])
    new_value_weights = value_weights * keep_factor - rate(width, values_local) * jnp.stack([orth[5].T, orth[4].T])
    new_upper_weights = up_weights * keep_factor - rate(width, hidden_local) * jnp.stack([orth[1].T, orth[2].T])
    new_out_weights = out_weights * keep_factor - rate(values_local, width) * orth[3]
    new_down_weights = down_weights * keep_factor - rate(hidden_local, width) * orth[0]
    new_norm_first = beta_first * norm_first + (1.0 - beta_first) * norm_grad
    new_norm_second = beta_second * norm_second + (1.0 - beta_second) * norm_grad * norm_grad
    fix_first = 1.0 - beta_first**STEP
    fix_second = 1.0 - beta_second**STEP
    new_norm_params = norm_params - adam_rate * (new_norm_first / fix_first) / (
        jnp.sqrt(new_norm_second / fix_second) + adam_eps
    )
    return (
        result.astype(jnp.bfloat16),
        token_grad,
        jnp.stack([fresh_query, fresh_key]),
        jnp.stack([fresh_value, fresh_gate]),
        fresh_out,
        jnp.stack([fresh_hidden, fresh_upper]),
        fresh_down,
        new_key_weights,
        new_value_weights,
        new_out_weights,
        new_upper_weights,
        new_down_weights,
        new_norm_first,
        new_norm_second,
        new_norm_params,
    )


def solution(mesh):
    tokens = P(("dp", "tensor"), None)
    wide = P(None, "dp", "tensor")
    tall = P("tensor", "dp")
    norms = P(("dp", "tensor"))
    return jax.shard_map(
        per_device,
        mesh=mesh,
        in_specs=(
            tokens, tokens, P("dp", None), wide, wide, tall, wide, tall,
            wide, wide, tall, wide, tall, norms, norms, norms,
        ),
        out_specs=(
            tokens, tokens, wide, wide, tall, wide, tall,
            wide, wide, tall, wide, tall, norms, norms, norms,
        ),
        check_vma=False,
    )
```

```python
from functools import partial
import math

import jax
import jax.numpy as jnp
from jax import lax
from jax.experimental import pallas as pl
from jax.experimental.pallas import tpu as pltpu
from jax.sharding import PartitionSpec as P

H = 8
KEY_HEAD_SIZE = 256
DV = 432
LEN = 1024
NS_ITERS = 5
STEP = 10


eps_norm = 1e-05
group_floor = 1.0
ns_first = 3.4445
ns_second = -4.775
ns_third = 2.0315
momentum_decay = 0.95
muon_rate = 0.5
weight_decay = 0.1
beta_first = 0.9
beta_second = 0.95
adam_rate = 0.8
adam_eps = 1e-08
TILE = 1024


def root_scale(values):
    return lax.rsqrt(jnp.mean(values * values, axis=-1, keepdims=True) + eps_norm)


def norm_back(grad_normed, normed, scaling):
    return scaling * (grad_normed - normed * jnp.mean(grad_normed * normed, axis=-1, keepdims=True))


def dot(left, right, left_dim, right_dim):
    return lax.dot_general(
        left, right, (((left_dim,), (right_dim,)), ((), ())), preferred_element_type=jnp.float32
    )


def gather_tokens(values):
    return lax.all_gather(values, "tensor", axis=0, tiled=True)


def scatter_tokens(values):
    return lax.psum_scatter(
        values.astype(jnp.bfloat16), "tensor", scatter_dimension=0, tiled=True
    ).astype(jnp.float32)


def ring_order(count):
    return list(range(0, count, 2)) + list(range(count - 1, 0, -2))


def ring_place(count):
    order = ring_order(count)
    return order, [(order[i], order[(i + 1) % count]) for i in range(count)]


def tie(value, *others):
    return lax.optimization_barrier((value, others))[0]


class Ring:
    def __init__(self):
        self.count = lax.axis_size("dp")
        order, self.right = ring_place(self.count)
        self.left = [(b, a) for a, b in self.right]
        self.half = self.count // 2
        place_of = [order.index(rank) for rank in range(self.count)]
        place = jnp.asarray(place_of, jnp.int32)[lax.axis_index("dp")]
        steps = jnp.arange(self.count, dtype=jnp.int32)
        self.rank_at = jnp.asarray(order, jnp.int32)[(place + steps) % self.count]
        self.sent = []
        self.added = None

    def rank(self, distance):
        return self.rank_at[distance % self.count]

    def exchange(self, blocks):
        if len(self.sent) > 2:
            blocks = tie(blocks, self.sent[-3])
        got = {}
        for side, block in blocks.items():
            got[side] = lax.ppermute(block, "dp", self.right if side > 0 else self.left)
        self.sent.append(got)
        return got


class Gather:
    def __init__(self, ring, shard, long_side):
        self.ring = ring
        self.shard = shard
        self.long_side = long_side
        self.rows, self.width = shard.shape
        self.blocks = [(shard, 0)]
        self.held = {1: shard, -1: shard}
        self.marks = []

    def step(self, after=None):
        at = len(self.marks) + 1
        sides = (1, -1) if at < self.ring.half else (self.long_side,)
        blocks = {side: self.held[side] for side in sides}
        if after is not None:
            blocks = tie(blocks, after)
        self.held = self.ring.exchange(blocks)
        self.blocks += [(self.held[side], -side * at) for side in sides]
        self.marks.append(self.held)

    def settle(self, *others):
        block, distance = self.blocks[-1]
        self.blocks[-1] = tie(block, others), distance


def run(lanes, rounds, after=None):
    for turn in range(rounds):
        for lane in lanes:
            lane.step(after if turn == 0 else None)


def reached(lanes, rounds):
    return [lane.marks[rounds - 1] for lane in lanes]


def loaded(lanes, rounds):
    return [lane.loads[rounds] for lane in lanes]


def nothing_kernel(out_ref):
    pass


def unwritten(shape, dtype):
    return pl.pallas_call(
        nothing_kernel,
        out_shape=jax.ShapeDtypeStruct(shape, dtype),
        out_specs=pl.BlockSpec(memory_space=pl.ANY),
    )()


def assemble(lanes):
    ring = lanes[0].ring
    width = lanes[0].width
    full = unwritten((sum(lane.rows for lane in lanes), width * ring.count), lanes[0].shard.dtype)
    placed, base = [], 0
    for lane in lanes:
        placed += [(index, base, block, distance) for index, (block, distance) in enumerate(lane.blocks)]
        base += lane.rows
    for _, row, block, distance in sorted(placed, key=lambda item: item[0]):
        full = lax.dynamic_update_slice(full, block, (row, ring.rank(distance) * width))
    return full


class Scatter:
    def __init__(self, ring, full, first, rows, long_side):
        self.ring = ring
        self.full = full
        self.first = first
        self.rows = rows
        self.long_side = long_side
        self.width = full.shape[1] // ring.count
        self.held = {}
        self.marks = []
        self.loads = []

    def piece(self, distance):
        column = self.ring.rank(distance) * self.width
        return lax.dynamic_slice(self.full, (self.first, column), (self.rows, self.width))

    def step(self, after=None):
        ring = self.ring
        at = ring.half - len(self.marks)
        came = self.held
        if came and ring.added is not None:
            came = tie(came, ring.added)
        sides = (1, -1) if at < ring.half else (self.long_side,)
        blocks = {}
        for side in sides:
            block = self.piece(side * at)
            if side in came:
                block = (block.astype(jnp.float32) + came[side].astype(jnp.float32)).astype(jnp.bfloat16)
            blocks[side] = block
        if came:
            ring.added = blocks
        self.loads.append(blocks)
        self.held = ring.exchange(blocks)
        self.marks.append(self.held)

    def total(self):
        own = self.piece(0).astype(jnp.float32)
        return own + self.held[1].astype(jnp.float32) + self.held[-1].astype(jnp.float32)


def halves(rows):
    cut = (rows // 2 + 15) // 16 * 16
    return [(0, cut, 1), (cut, rows - cut, -1)]


def gather_lanes(ring, shard):
    return [Gather(ring, shard[first : first + size], side) for first, size, side in halves(shard.shape[0])]


def scatter_lanes(ring, full):
    return [Scatter(ring, full, first, size, side) for first, size, side in halves(full.shape[0])]


def totals(lanes):
    return jnp.concatenate([lane.total() for lane in lanes])


def decay_rows(doc_ids, log_gamma, first, size, keys):
    query_pos = first + jnp.arange(size)
    key_pos = jnp.arange(keys)
    distance = query_pos[:, None] - key_pos[None, :]
    allowed = (doc_ids[first : first + size, None] == doc_ids[None, :keys]) & (distance >= 0)
    steps_back = jnp.maximum(distance, 0).astype(jnp.float32)
    falloff = jnp.exp(log_gamma[:, None, None] * steps_back[None])
    return jnp.where(allowed[None], falloff, 0.0)


def einsum32(spec, left, right):
    return jnp.einsum(spec, left, right, preferred_element_type=jnp.float32)


def retention_forward(query, key, value, doc_ids, log_gamma, block):
    factor = KEY_HEAD_SIZE ** (-0.5)
    pieces = []
    for first in range(0, LEN, block):
        keys = first + block
        falloff = decay_rows(doc_ids, log_gamma, first, block, keys)
        scores = einsum32("hdq,hdk->hqk", query[:, :, first:keys], key[:, :, :keys]) * factor
        weights = (scores * falloff).astype(jnp.bfloat16)
        pieces.append(einsum32("hdk,hqk->hdq", value[:, :, :keys], weights))
    return jnp.concatenate(pieces, axis=2)


def retention_backward(query, key, value, grad, doc_ids, log_gamma, block, waits):
    factor = KEY_HEAD_SIZE ** (-0.5)
    grad_query = []
    grad_key = jnp.zeros(key.shape, jnp.float32)
    grad_value = jnp.zeros(value.shape, jnp.float32)
    for first in range(0, LEN, block):
        keys = first + block
        falloff = decay_rows(doc_ids, log_gamma, first, block, keys)
        query_now, grad_now = query[:, :, first:keys], grad[:, :, first:keys]
        if waits[first // block] is not None:
            query_now, grad_now = tie((query_now, grad_now), waits[first // block])
        scores = einsum32("hdq,hdk->hqk", query_now, key[:, :, :keys]) * factor
        weights = (scores * falloff).astype(jnp.bfloat16)
        grad_weights = einsum32("hdq,hdk->hqk", grad_now, value[:, :, :keys])
        grad_scores = (grad_weights * falloff).astype(jnp.bfloat16)
        grad_query.append(einsum32("hdk,hqk->hdq", key[:, :, :keys], grad_scores) * factor)
        grad_key = grad_key.at[:, :, :keys].add(einsum32("hdq,hqk->hdk", query_now, grad_scores) * factor)
        grad_value = grad_value.at[:, :, :keys].add(einsum32("hdq,hqk->hdk", grad_now, weights))
    return jnp.concatenate(grad_query, axis=2), grad_key, grad_value


def newton_schulz_kernel(turns, step, in_ref, out_ref, cur_ref, low_ref, rest_ref, poly_ref, scale_ref):
    parts, size, cols = in_ref.shape
    width = parts * cols
    band = 256
    blocks = size // step

    def rows_of(index):
        return pl.ds(pl.multiple_of(index * step, step), step)

    def first_sum(index, total):
        rows = rows_of(index)
        for part in range(parts):
            block = in_ref[part, rows, :].astype(jnp.float32)
            total = total + jnp.sum(block * block)
        return total

    total = lax.fori_loop(0, blocks, first_sum, jnp.float32(0.0))
    scale_ref[...] = 1.0 / (jnp.sqrt(jnp.full(scale_ref.shape, total)) + 1e-07)

    @pl.loop(0, blocks)
    def _(index):
        rows = rows_of(index)
        scale = scale_ref[0, 0]
        for part in range(parts):
            block = in_ref[part, rows, :].astype(jnp.float32) * scale
            columns = pl.ds(part * cols, cols)
            cur_ref[rows, columns] = block
            low_ref[0, rows, columns] = block.astype(jnp.bfloat16)

    bands = [(first, min(256, size - first)) for first in range(0, size, 256)]

    def turn_body(turn, norm, last):
        here = lax.rem(turn, 2)
        there = 1 - here
        middle = norm * (1.0 / size)
        low = low_ref.at[here]
        for first, wide in bands:
            gram = dot(low[...], low[first : first + wide, :], 1, 1)
            place = lax.broadcasted_iota(jnp.int32, gram.shape, 0)
            eye = place == lax.broadcasted_iota(jnp.int32, gram.shape, 1) + first
            rest_ref[:, first : first + wide] = jnp.where(eye, gram - middle, gram).astype(jnp.bfloat16)
        for first, wide in bands:
            rest = rest_ref[:, first : first + wide]
            square = dot(rest_ref[...], rest, 1, 0)
            poly = (ns_second + 2.0 * ns_third * middle) * rest.astype(jnp.float32) + ns_third * square
            poly_ref[:, first : first + wide] = poly.astype(jnp.bfloat16)
        outer = ns_first + middle * (ns_second + ns_third * middle)

        total = jnp.zeros((1, band), jnp.float32)
        for first in range(0, width, band):
            columns = slice(first, first + band)
            fresh = outer * cur_ref[:, columns] + dot(poly_ref[...], low[:, columns], 1, 0)
            if last:
                out_ref[first // cols, :, first % cols : first % cols + band] = fresh.astype(jnp.bfloat16)
            else:
                cur_ref[:, columns] = fresh
                low_ref[there, :, columns] = fresh.astype(jnp.bfloat16)
                total = total + jnp.sum(fresh * fresh, axis=0, keepdims=True)
        return jnp.sum(total)

    norm = lax.fori_loop(0, turns - 1, lambda turn, norm: turn_body(turn, norm, False), jnp.float32(1.0))
    turn_body(turns - 1, norm, True)


def newton_schulz(block):
    parts, size, cols = block.shape
    width = parts * cols
    step = next(step for step in range(288, 0, -16) if size % step == 0)
    products = 2 * size * size * (2 * width + size) * NS_ITERS
    return pl.pallas_call(
        partial(newton_schulz_kernel, NS_ITERS, step),
        out_shape=jax.ShapeDtypeStruct(block.shape, jnp.bfloat16),
        in_specs=[pl.BlockSpec(memory_space=pltpu.VMEM)],
        out_specs=pl.BlockSpec(memory_space=pltpu.VMEM),
        scratch_shapes=[
            pltpu.VMEM((size, width), jnp.float32),
            pltpu.VMEM((2, size, width), jnp.bfloat16),
            pltpu.VMEM((size, size), jnp.bfloat16),
            pltpu.VMEM((size, size), jnp.bfloat16),
            pltpu.VMEM((8, 128), jnp.float32),
        ],
        compiler_params=pltpu.CompilerParams(vmem_limit_bytes=48 * 1024 * 1024),
        cost_estimate=pl.CostEstimate(flops=products, bytes_accessed=4 * size * width, transcendentals=0),
    )(block)


def orthogonalize(slabs, after):
    ranks = lax.axis_size("dp")
    widest = max(slab.shape[0] for slab in slabs)
    cols = slabs[0].shape[1]
    padded = [jnp.pad(slab.astype(jnp.bfloat16), ((0, widest - slab.shape[0]), (0, 0))) for slab in slabs]
    each = (len(slabs) + ranks - 1) // ranks
    padded += [jnp.zeros((widest, cols), jnp.bfloat16)] * (each * ranks - len(slabs))
    stacked = jnp.stack(padded)
    owned = lax.all_to_all(stacked.reshape(ranks, each, widest, cols), "dp", 0, 0, tiled=True)
    owned = tie(owned, after)
    done = []
    for index in range(each):
        mine = owned[:, index]
        if cols % 128:
            mine = jnp.moveaxis(mine, 0, 1).reshape(1, widest, ranks * cols)
        item = newton_schulz(mine)
        if cols % 128:
            item = jnp.moveaxis(item.reshape(widest, ranks, cols), 1, 0)
        done.append(item)
    ready = jnp.stack(done, axis=1)
    returned = lax.all_to_all(ready, "dp", 0, 0, tiled=True).reshape(each * ranks, widest, cols)
    return [returned[index, : slab.shape[0]] for index, slab in enumerate(slabs)]


def rotated(value, axis, turn):
    count = lax.axis_size(axis)
    return lax.ppermute(value, axis, [(i, (i + turn) % count) for i in range(count)])


def gather_small(piece, axis):
    count = lax.axis_size(axis)
    index = lax.axis_index(axis)
    turned = tie([rotated(piece, axis, turn) for turn in range(1, count)])
    whole = jnp.zeros((count,) + piece.shape, piece.dtype)
    start = (0,) * piece.ndim
    for turn, item in enumerate([piece] + turned):
        whole = lax.dynamic_update_slice(whole, item[None], ((index - turn) % count,) + start)
    return whole


def sum_norms(terms):
    for axis in ("tensor", "dp"):
        count = lax.axis_size(axis)
        bit = 1
        while bit < count:
            terms = terms + lax.ppermute(terms, axis, [(i, i ^ bit) for i in range(count)])
            bit *= 2
    return terms


def per_device(
    tokens,
    cotangent,
    doc_lengths,
    key_weights,
    value_weights,
    out_weights,
    up_weights,
    down_weights,
    key_momentum,
    value_momentum,
    out_momentum,
    up_momentum,
    down_momentum,
    norm_params,
    norm_first,
    norm_second,
):
    tensor_count = lax.axis_size("tensor")
    tensor_index = lax.axis_index("tensor")
    heads = H // tensor_count
    width = tokens.shape[1]
    keys_local = key_weights.shape[2]
    values_local = value_weights.shape[2]
    hidden_local = up_weights.shape[2]
    value_total = values_local * tensor_count
    block = min(LEN, 512)
    ring = Ring()
    half = ring.half
    quarter = half // 4

    def low_t(matrix):
        return matrix.astype(jnp.bfloat16).T

    attend_lanes = gather_lanes(
        ring,
        jnp.concatenate(
            [low_t(key_weights[0]), low_t(key_weights[1]), low_t(value_weights[0]), low_t(value_weights[1])]
        ),
    )
    out_lanes = [Gather(ring, out_weights.astype(jnp.bfloat16), 1)]
    upper_lanes = gather_lanes(ring, jnp.concatenate([low_t(up_weights[0]), low_t(up_weights[1])]))
    down_lanes = [Gather(ring, down_weights.astype(jnp.bfloat16), -1)]
    tokens_all = gather_tokens(tokens)
    own_norms = norm_params.shape[0]
    filled_norms = TILE * ((own_norms + TILE - 1) // TILE)
    norm_piece = jnp.pad(norm_params, (0, filled_norms - own_norms)).reshape(filled_norms // 128, 128)
    norm_group = gather_small(norm_piece, "tensor")
    run(attend_lanes, quarter, norm_group)
    gathered_norms = gather_small(norm_group, "dp")
    run(attend_lanes, 2 * quarter, gathered_norms)
    gathered_norms = gathered_norms.reshape(-1, filled_norms)[:, :own_norms].reshape(-1)

    gain_one = gathered_norms[:width]
    gain_two = gathered_norms[width : 2 * width]
    group_gain = lax.dynamic_slice_in_dim(
        gathered_norms, 2 * width + tensor_index * values_local, values_local
    )[:, None]
    group_bias = lax.dynamic_slice_in_dim(
        gathered_norms, 2 * width + value_total + tensor_index * values_local, values_local
    )[:, None]
    starts_all = jnp.cumsum(doc_lengths[0]) - doc_lengths[0]
    positions = jnp.arange(LEN)
    doc_ids = jnp.sum((positions[:, None] >= starts_all[None, :]).astype(jnp.int32), axis=1) - 1

    inputs = tokens.astype(jnp.float32)
    scale_one = root_scale(inputs)
    normed_one = inputs * scale_one
    inputs_all = tokens_all.astype(jnp.float32)
    normed_all = (inputs_all * root_scale(inputs_all) * gain_one).astype(jnp.bfloat16)
    rows_total = normed_all.shape[0]
    grad_rows_two = gather_tokens(tie(cotangent, tokens_all))
    run(attend_lanes, half - 3 * quarter)
    run(out_lanes, 2 * quarter)
    for lane in attend_lanes:
        lane.settle(normed_all)
    attend_full = assemble(attend_lanes)

    gate_row = 2 * keys_local + values_local
    attend = dot(attend_full[:gate_row], normed_all, 1, 1).astype(jnp.bfloat16)
    attend = tie(attend, reached(out_lanes, 2 * quarter))
    run(out_lanes, quarter, attend)
    query = attend[:keys_local].reshape(heads, KEY_HEAD_SIZE, rows_total)
    key = attend[keys_local : 2 * keys_local].reshape(heads, KEY_HEAD_SIZE, rows_total)
    value = attend[2 * keys_local :].reshape(heads, DV, rows_total)
    head_ids = (tensor_index * heads + jnp.arange(heads)).astype(jnp.float32)
    log_gamma = jnp.log(1.0 - jnp.exp2(-5.0 - head_ids))
    mixed_heads = retention_forward(query, key, value, doc_ids, log_gamma, block)
    mixed_heads = tie(mixed_heads, reached(out_lanes, 3 * quarter))
    run(out_lanes, half - 3 * quarter, mixed_heads)
    out_full = assemble(out_lanes)
    run(upper_lanes, half)
    run(down_lanes, half)
    upper_full = assemble(upper_lanes)
    gate_pre = dot(attend_full[gate_row:], tie(normed_all, mixed_heads), 1, 1)
    centred = mixed_heads - jnp.mean(mixed_heads, axis=1, keepdims=True)
    group_scale = lax.rsqrt(jnp.mean(centred * centred, axis=1, keepdims=True) + group_floor)
    group_hat = centred * group_scale
    group_flat = group_hat.reshape(values_local, rows_total)
    group_out = group_flat * group_gain + group_bias
    gate_act, silu_pull = jax.vjp(jax.nn.silu, gate_pre)
    mixed_low = (gate_act * group_out).astype(jnp.bfloat16)
    mixed_low, grad_rows_two = tie((mixed_low, grad_rows_two), reached(out_lanes, half))
    branch_one = scatter_tokens(dot(mixed_low, out_full, 0, 0))
    middle = inputs + tie(branch_one, reached(upper_lanes[:1], 3 * quarter), reached(upper_lanes[1:], 2 * quarter))
    scale_two = root_scale(middle)
    normed_two = middle * scale_two
    second_all = gather_tokens((normed_two * gain_two).astype(jnp.bfloat16))
    second_all = tie(second_all, reached(down_lanes, 2 * quarter))
    down_full = assemble(down_lanes)
    hidden_gate = dot(upper_full[:hidden_local], second_all, 1, 1)
    second_late = tie(second_all, hidden_gate, reached(down_lanes, 3 * quarter))
    hidden_upper = dot(upper_full[hidden_local:], second_late, 1, 1)
    gelu_gate, gelu_pull = jax.vjp(partial(jax.nn.gelu, approximate=False), hidden_gate)
    hidden_low = (gelu_gate * hidden_upper).astype(jnp.bfloat16)

    grad_result = cotangent.astype(jnp.float32)
    grad_down = dot(hidden_low, grad_rows_two, 1, 0).astype(jnp.bfloat16)
    down_back = [Scatter(ring, grad_down, 0, hidden_local, -1)]
    run(down_back, half)
    grad_hidden = dot(down_full, tie(grad_rows_two, grad_down), 1, 1)
    grad_gate_mlp = gelu_pull(grad_hidden * hidden_upper)[0].astype(jnp.bfloat16)
    grad_upper_mlp = (grad_hidden * gelu_gate).astype(jnp.bfloat16)
    grad_hidden_low = jnp.concatenate([grad_gate_mlp, grad_upper_mlp])
    grad_hidden_low = tie(grad_hidden_low, loaded(down_back, quarter))
    grad_second = dot(grad_hidden_low, upper_full, 0, 0).astype(jnp.bfloat16)
    grad_second, grad_hidden_late = tie((grad_second, grad_hidden_low))
    grad_second_local = scatter_tokens(grad_second)
    grad_hidden_late = tie(grad_hidden_late, loaded(down_back, 2 * quarter))
    grad_upper = dot(grad_hidden_late, second_all, 1, 0).astype(jnp.bfloat16)
    upper_back = scatter_lanes(ring, tie(grad_upper, reached(down_back, 3 * quarter)))
    run(upper_back, half)
    grad_second_local = tie(grad_second_local, loaded(upper_back, 2 * quarter))
    grad_gain_two = jnp.sum(grad_second_local * normed_two, axis=0)
    grad_middle = grad_result + norm_back(grad_second_local * gain_two, normed_two, scale_two)
    grad_rows_one = gather_tokens(grad_middle.astype(jnp.bfloat16))
    grad_rows_one = tie(grad_rows_one, loaded(upper_back, 3 * quarter))
    out_back = [Scatter(ring, dot(mixed_low, grad_rows_one, 1, 0).astype(jnp.bfloat16), 0, values_local, 1)]
    run(out_back, quarter)
    grad_mixed = dot(out_full, tie(grad_rows_one, loaded(out_back, 0)), 1, 1)
    grad_gate_low = silu_pull(grad_mixed * group_out)[0].astype(jnp.bfloat16)
    gate_back = [Scatter(ring, dot(grad_gate_low, normed_all, 1, 0).astype(jnp.bfloat16), 0, values_local, -1)]
    run(gate_back, quarter)
    run(out_back + gate_back, half - quarter)
    grad_group = grad_mixed * gate_act
    grad_group_gain = jnp.sum(grad_group * group_flat, axis=1)
    grad_group_bias = jnp.sum(grad_group, axis=1)
    grad_hat = (grad_group * group_gain).reshape(heads, DV, rows_total)
    grad_heads = group_scale * (
        grad_hat
        - jnp.mean(grad_hat, axis=1, keepdims=True)
        - group_hat * jnp.mean(grad_hat * group_hat, axis=1, keepdims=True)
    )
    grad_heads = tie(grad_heads, loaded(out_back, quarter), loaded(gate_back, 0))
    waits = [None, (loaded(out_back, 2 * quarter), loaded(gate_back, quarter))]
    grad_queries, grad_keys, grad_values = retention_backward(
        query, key, value, grad_heads.astype(jnp.bfloat16), doc_ids, log_gamma, block, waits
    )
    grad_attend_low = jnp.concatenate(
        [
            grad_queries.astype(jnp.bfloat16).reshape(keys_local, rows_total),
            grad_keys.astype(jnp.bfloat16).reshape(keys_local, rows_total),
            grad_values.astype(jnp.bfloat16).reshape(values_local, rows_total),
        ]
    )
    grad_attend_low = tie(grad_attend_low, loaded(out_back, 3 * quarter), loaded(gate_back, 2 * quarter))
    grad_attend = dot(grad_attend_low, normed_all, 1, 0).astype(jnp.bfloat16)
    attend_back = scatter_lanes(ring, grad_attend)
    run(attend_back, half)
    pieces = []
    for index in range(4):
        lane = attend_back[index % 2]
        rows = slice(index * rows_total // 4, (index + 1) * rows_total // 4)
        late, gate_late = tie((grad_attend_low[:, rows], grad_gate_low[:, rows]), loaded([lane], (1 + index // 2) * quarter))
        piece = dot(late, attend_full[:gate_row], 0, 0) + dot(gate_late, attend_full[gate_row:], 0, 0)
        pieces.append(piece.astype(jnp.bfloat16))
    grad_first = jnp.concatenate(pieces)
    grad_first_local = scatter_tokens(grad_first)
    branch_two = scatter_tokens(dot(tie(hidden_low, grad_first), down_full, 0, 0))
    result = middle + branch_two
    grad_gain_one = jnp.sum(grad_first_local * normed_one, axis=0)
    token_grad = grad_middle + norm_back(grad_first_local * gain_one, normed_one, scale_one)
    group_part = jnp.zeros((2, value_total), jnp.float32)
    group_part = lax.dynamic_update_slice_in_dim(
        group_part, jnp.stack([grad_group_gain, grad_group_bias]), tensor_index * values_local, 1
    )
    norm_terms = jnp.concatenate([grad_gain_one, grad_gain_two, group_part.reshape(-1)])
    norm_sum = sum_norms(norm_terms)
    norm_place = lax.axis_index("dp") * tensor_count + tensor_index
    norm_grad = lax.dynamic_slice_in_dim(norm_sum, norm_place * own_norms, own_norms)
    grad_down_w = totals(down_back)
    grad_upper_w = totals(upper_back)
    grad_out_w = totals(out_back)
    grad_gate_w = totals(gate_back)
    grad_attend_w = totals(attend_back)

    fresh_query = momentum_decay * key_momentum[0] + grad_attend_w[:keys_local].T
    fresh_key = momentum_decay * key_momentum[1] + grad_attend_w[keys_local : 2 * keys_local].T
    fresh_value = momentum_decay * value_momentum[0] + grad_attend_w[2 * keys_local :].T
    fresh_gate = momentum_decay * value_momentum[1] + grad_gate_w.T
    fresh_out = momentum_decay * out_momentum + grad_out_w
    fresh_hidden = momentum_decay * up_momentum[0] + grad_upper_w[:hidden_local].T
    fresh_upper = momentum_decay * up_momentum[1] + grad_upper_w[hidden_local:].T
    fresh_down = momentum_decay * down_momentum + grad_down_w
    orth = orthogonalize(
        [
            fresh_down,
            fresh_hidden.T,
            fresh_upper.T,
            fresh_out,
            fresh_gate.T,
            fresh_value.T,
            fresh_query.T,
            fresh_key.T,
        ],
        norm_sum,
    )
    orth = [item.astype(jnp.float32) for item in orth]
    keep_factor = 1.0 - muon_rate * weight_decay

    def rate(rows, cols):
        return muon_rate * math.sqrt(max(1.0, rows / cols))

    new_key_weights = key_weights * keep_factor - rate(width, keys_local) * jnp.stack([orth[6].T, orth[7].T])
    new_value_weights = value_weights * keep_factor - rate(width, values_local) * jnp.stack([orth[5].T, orth[4].T])
    new_upper_weights = up_weights * keep_factor - rate(width, hidden_local) * jnp.stack([orth[1].T, orth[2].T])
    new_out_weights = out_weights * keep_factor - rate(values_local, width) * orth[3]
    new_down_weights = down_weights * keep_factor - rate(hidden_local, width) * orth[0]
    new_norm_first = beta_first * norm_first + (1.0 - beta_first) * norm_grad
    new_norm_second = beta_second * norm_second + (1.0 - beta_second) * norm_grad * norm_grad
    fix_first = 1.0 - beta_first**STEP
    fix_second = 1.0 - beta_second**STEP
    new_norm_params = norm_params - adam_rate * (new_norm_first / fix_first) / (
        jnp.sqrt(new_norm_second / fix_second) + adam_eps
    )
    return (
        result.astype(jnp.bfloat16),
        token_grad,
        jnp.stack([fresh_query, fresh_key]),
        jnp.stack([fresh_value, fresh_gate]),
        fresh_out,
        jnp.stack([fresh_hidden, fresh_upper]),
        fresh_down,
        new_key_weights,
        new_value_weights,
        new_out_weights,
        new_upper_weights,
        new_down_weights,
        new_norm_first,
        new_norm_second,
        new_norm_params,
    )


def solution(mesh):
    tokens = P(("dp", "tensor"), None)
    wide = P(None, "dp", "tensor")
    tall = P("tensor", "dp")
    norms = P(("dp", "tensor"))
    return jax.shard_map(
        per_device,
        mesh=mesh,
        in_specs=(
            tokens, tokens, P("dp", None), wide, wide, tall, wide, tall,
            wide, wide, tall, wide, tall, norms, norms, norms,
        ),
        out_specs=(
            tokens, tokens, wide, wide, tall, wide, tall,
            wide, wide, tall, wide, tall, norms, norms, norms,
        ),
        check_vma=False,
    )
```

```python
from functools import partial
import math

import jax
import jax.numpy as jnp
from jax import lax
from jax.experimental import pallas as pl
from jax.experimental.pallas import tpu as pltpu
from jax.sharding import PartitionSpec as P

H = 8
KEY_HEAD_SIZE = 256
DV = 432
LEN = 1024
NS_ITERS = 5
STEP = 10


eps_norm = 1e-05
group_floor = 1.0
ns_first = 3.4445
ns_second = -4.775
ns_third = 2.0315
momentum_decay = 0.95
muon_rate = 0.5
weight_decay = 0.1
beta_first = 0.9
beta_second = 0.95
adam_rate = 0.8
adam_eps = 1e-08
TILE = 1024


def root_scale(values):
    return lax.rsqrt(jnp.mean(values * values, axis=-1, keepdims=True) + eps_norm)


def norm_back(grad_normed, normed, scaling):
    return scaling * (grad_normed - normed * jnp.mean(grad_normed * normed, axis=-1, keepdims=True))


def dot(left, right, left_dim, right_dim):
    return lax.dot_general(
        left, right, (((left_dim,), (right_dim,)), ((), ())), preferred_element_type=jnp.float32
    )


def gather_tokens(values):
    return lax.all_gather(values, "tensor", axis=0, tiled=True)


def scatter_tokens(values):
    return lax.psum_scatter(
        values.astype(jnp.bfloat16), "tensor", scatter_dimension=0, tiled=True
    ).astype(jnp.float32)


def ring_order(count):
    return list(range(0, count, 2)) + list(range(count - 1, 0, -2))


def ring_place(count):
    order = ring_order(count)
    return order, [(order[i], order[(i + 1) % count]) for i in range(count)]


def tie(value, *others):
    return lax.optimization_barrier((value, others))[0]


class Ring:
    def __init__(self):
        self.count = lax.axis_size("dp")
        order, self.right = ring_place(self.count)
        self.left = [(b, a) for a, b in self.right]
        self.half = self.count // 2
        place_of = [order.index(rank) for rank in range(self.count)]
        place = jnp.asarray(place_of, jnp.int32)[lax.axis_index("dp")]
        steps = jnp.arange(self.count, dtype=jnp.int32)
        self.rank_at = jnp.asarray(order, jnp.int32)[(place + steps) % self.count]
        self.sent = []
        self.added = None

    def rank(self, distance):
        return self.rank_at[distance % self.count]

    def exchange(self, blocks):
        if len(self.sent) > 2:
            blocks = tie(blocks, self.sent[-3])
        got = {}
        for side, block in blocks.items():
            got[side] = lax.ppermute(block, "dp", self.right if side > 0 else self.left)
        self.sent.append(got)
        return got


class Gather:
    def __init__(self, ring, shard, long_side):
        self.ring = ring
        self.shard = shard
        self.long_side = long_side
        self.rows, self.width = shard.shape
        self.blocks = [(shard, 0)]
        self.held = {1: shard, -1: shard}
        self.marks = []

    def step(self, after=None):
        at = len(self.marks) + 1
        sides = (1, -1) if at < self.ring.half else (self.long_side,)
        blocks = {side: self.held[side] for side in sides}
        if after is not None:
            blocks = tie(blocks, after)
        self.held = self.ring.exchange(blocks)
        self.blocks += [(self.held[side], -side * at) for side in sides]
        self.marks.append(self.held)


def run(lanes, rounds, after=None):
    for turn in range(rounds):
        for lane in lanes:
            lane.step(after if turn == 0 else None)


def reached(lanes, rounds):
    return [lane.marks[rounds - 1] for lane in lanes]


def loaded(lanes, rounds):
    return [lane.loads[rounds] for lane in lanes]


def nothing_kernel(out_ref):
    pass


def unwritten(shape, dtype):
    return pl.pallas_call(
        nothing_kernel,
        out_shape=jax.ShapeDtypeStruct(shape, dtype),
        out_specs=pl.BlockSpec(memory_space=pl.ANY),
    )()


def assemble(lanes):
    ring = lanes[0].ring
    width = lanes[0].width
    full = unwritten((sum(lane.rows for lane in lanes), width * ring.count), lanes[0].shard.dtype)
    placed, base = [], 0
    for lane in lanes:
        lane.blocks[0] = tie(lane.shard, lane.marks[0]), 0
        placed += [(index, base, block, distance) for index, (block, distance) in enumerate(lane.blocks)]
        base += lane.rows
    for _, row, block, distance in sorted(placed, key=lambda item: item[0]):
        full = lax.dynamic_update_slice(full, block, (row, ring.rank(distance) * width))
    return full


class Scatter:
    def __init__(self, ring, full, first, rows, long_side):
        self.ring = ring
        self.full = full
        self.first = first
        self.rows = rows
        self.long_side = long_side
        self.width = full.shape[1] // ring.count
        self.held = {}
        self.marks = []
        self.loads = []

    def piece(self, distance):
        column = self.ring.rank(distance) * self.width
        return lax.dynamic_slice(self.full, (self.first, column), (self.rows, self.width))

    def step(self, after=None):
        ring = self.ring
        at = ring.half - len(self.marks)
        came = self.held
        if came and ring.added is not None:
            came = tie(came, ring.added)
        sides = (1, -1) if at < ring.half else (self.long_side,)
        blocks = {}
        for side in sides:
            block = self.piece(side * at)
            if side in came:
                block = (block.astype(jnp.float32) + came[side].astype(jnp.float32)).astype(jnp.bfloat16)
            blocks[side] = block
        if came:
            ring.added = blocks
        self.loads.append(blocks)
        self.held = ring.exchange(blocks)
        self.marks.append(self.held)

    def total(self):
        own = self.piece(0).astype(jnp.float32)
        return own + self.held[1].astype(jnp.float32) + self.held[-1].astype(jnp.float32)


def halves(rows):
    cut = (rows // 2 + 15) // 16 * 16
    return [(0, cut, 1), (cut, rows - cut, -1)]


def gather_lanes(ring, shard):
    return [Gather(ring, shard[first : first + size], side) for first, size, side in halves(shard.shape[0])]


def scatter_lanes(ring, full):
    return [Scatter(ring, full, first, size, side) for first, size, side in halves(full.shape[0])]


def totals(lanes):
    return jnp.concatenate([lane.total() for lane in lanes])


def decay_rows(doc_ids, log_gamma, first, size, keys):
    query_pos = first + jnp.arange(size)
    key_pos = jnp.arange(keys)
    distance = query_pos[:, None] - key_pos[None, :]
    allowed = (doc_ids[first : first + size, None] == doc_ids[None, :keys]) & (distance >= 0)
    steps_back = jnp.maximum(distance, 0).astype(jnp.float32)
    falloff = jnp.exp(log_gamma[:, None, None] * steps_back[None])
    return jnp.where(allowed[None], falloff, 0.0)


def einsum32(spec, left, right):
    return jnp.einsum(spec, left, right, preferred_element_type=jnp.float32)


def retention_forward(query, key, value, doc_ids, log_gamma, block):
    factor = KEY_HEAD_SIZE ** (-0.5)
    pieces = []
    for first in range(0, LEN, block):
        keys = first + block
        falloff = decay_rows(doc_ids, log_gamma, first, block, keys)
        scores = einsum32("hdq,hdk->hqk", query[:, :, first:keys], key[:, :, :keys]) * factor
        weights = (scores * falloff).astype(jnp.bfloat16)
        pieces.append(einsum32("hdk,hqk->hdq", value[:, :, :keys], weights))
    return jnp.concatenate(pieces, axis=2)


def retention_backward(query, key, value, grad, doc_ids, log_gamma, block, waits):
    factor = KEY_HEAD_SIZE ** (-0.5)
    grad_query = []
    grad_key = jnp.zeros(key.shape, jnp.float32)
    grad_value = jnp.zeros(value.shape, jnp.float32)
    for first in range(0, LEN, block):
        keys = first + block
        falloff = decay_rows(doc_ids, log_gamma, first, block, keys)
        query_now, grad_now = query[:, :, first:keys], grad[:, :, first:keys]
        if waits[first // block] is not None:
            grad_now = tie(grad_now, waits[first // block])
        scores = einsum32("hdq,hdk->hqk", query_now, key[:, :, :keys]) * factor
        weights = (scores * falloff).astype(jnp.bfloat16)
        grad_weights = einsum32("hdq,hdk->hqk", grad_now, value[:, :, :keys])
        grad_scores = (grad_weights * falloff).astype(jnp.bfloat16)
        grad_query.append(einsum32("hdk,hqk->hdq", key[:, :, :keys], grad_scores) * factor)
        grad_key = grad_key.at[:, :, :keys].add(einsum32("hdq,hqk->hdk", query_now, grad_scores) * factor)
        grad_value = grad_value.at[:, :, :keys].add(einsum32("hdq,hqk->hdk", grad_now, weights))
    return jnp.concatenate(grad_query, axis=2), grad_key, grad_value


def newton_schulz_kernel(turns, step, in_ref, out_ref, cur_ref, low_ref, rest_ref, poly_ref, scale_ref):
    parts, size, cols = in_ref.shape
    width = parts * cols
    band = 256
    blocks = size // step

    def rows_of(index):
        return pl.ds(pl.multiple_of(index * step, step), step)

    def first_sum(index, total):
        rows = rows_of(index)
        for part in range(parts):
            block = in_ref[part, rows, :].astype(jnp.float32)
            total = total + jnp.sum(block * block)
        return total

    total = lax.fori_loop(0, blocks, first_sum, jnp.float32(0.0))
    scale_ref[...] = 1.0 / (jnp.sqrt(jnp.full(scale_ref.shape, total)) + 1e-07)

    @pl.loop(0, blocks)
    def _(index):
        rows = rows_of(index)
        scale = scale_ref[0, 0]
        for part in range(parts):
            block = in_ref[part, rows, :].astype(jnp.float32) * scale
            columns = pl.ds(part * cols, cols)
            cur_ref[rows, columns] = block
            low_ref[0, rows, columns] = block.astype(jnp.bfloat16)

    bands = [(first, min(256, size - first)) for first in range(0, size, 256)]

    def turn_body(turn, norm, last):
        here = lax.rem(turn, 2)
        there = 1 - here
        middle = norm * (1.0 / size)
        low = low_ref.at[here]
        for first, wide in bands:
            gram = dot(low[...], low[first : first + wide, :], 1, 1)
            place = lax.broadcasted_iota(jnp.int32, gram.shape, 0)
            eye = place == lax.broadcasted_iota(jnp.int32, gram.shape, 1) + first
            rest_ref[:, first : first + wide] = jnp.where(eye, gram - middle, gram).astype(jnp.bfloat16)
        for first, wide in bands:
            rest = rest_ref[:, first : first + wide]
            square = dot(rest_ref[...], rest, 1, 0)
            poly = (ns_second + 2.0 * ns_third * middle) * rest.astype(jnp.float32) + ns_third * square
            poly_ref[:, first : first + wide] = poly.astype(jnp.bfloat16)
        outer = ns_first + middle * (ns_second + ns_third * middle)

        total = jnp.zeros((1, band), jnp.float32)
        for first in range(0, width, band):
            columns = slice(first, first + band)
            fresh = outer * cur_ref[:, columns] + dot(poly_ref[...], low[:, columns], 1, 0)
            if last:
                out_ref[first // cols, :, first % cols : first % cols + band] = fresh.astype(jnp.bfloat16)
            else:
                cur_ref[:, columns] = fresh
                low_ref[there, :, columns] = fresh.astype(jnp.bfloat16)
                total = total + jnp.sum(fresh * fresh, axis=0, keepdims=True)
        return jnp.sum(total)

    norm = lax.fori_loop(0, turns - 1, lambda turn, norm: turn_body(turn, norm, False), jnp.float32(1.0))
    turn_body(turns - 1, norm, True)


def newton_schulz(block):
    parts, size, cols = block.shape
    width = parts * cols
    step = next(step for step in range(288, 0, -16) if size % step == 0)
    products = 2 * size * size * (2 * width + size) * NS_ITERS
    return pl.pallas_call(
        partial(newton_schulz_kernel, NS_ITERS, step),
        out_shape=jax.ShapeDtypeStruct(block.shape, jnp.bfloat16),
        in_specs=[pl.BlockSpec(memory_space=pltpu.VMEM)],
        out_specs=pl.BlockSpec(memory_space=pltpu.VMEM),
        scratch_shapes=[
            pltpu.VMEM((size, width), jnp.float32),
            pltpu.VMEM((2, size, width), jnp.bfloat16),
            pltpu.VMEM((size, size), jnp.bfloat16),
            pltpu.VMEM((size, size), jnp.bfloat16),
            pltpu.VMEM((8, 128), jnp.float32),
        ],
        compiler_params=pltpu.CompilerParams(vmem_limit_bytes=48 * 1024 * 1024),
        cost_estimate=pl.CostEstimate(flops=products, bytes_accessed=4 * size * width, transcendentals=0),
    )(block)


def orthogonalize(slabs, norm_terms):
    ranks = lax.axis_size("dp")
    widest = max(slab.shape[0] for slab in slabs)
    cols = slabs[0].shape[1]
    padded = [jnp.pad(slab.astype(jnp.bfloat16), ((0, widest - slab.shape[0]), (0, 0))) for slab in slabs]
    each = (len(slabs) + ranks - 1) // ranks
    padded += [jnp.zeros((widest, cols), jnp.bfloat16)] * (each * ranks - len(slabs))
    stacked = jnp.stack(padded)
    owned = lax.all_to_all(stacked.reshape(ranks, each, widest, cols), "dp", 0, 0, tiled=True)
    owned, norm_terms = tie((owned, norm_terms))
    done = []
    for index in range(each):
        mine = owned[:, index]
        if cols % 128:
            mine = jnp.moveaxis(mine, 0, 1).reshape(1, widest, ranks * cols)
        item = newton_schulz(mine)
        if cols % 128:
            item = jnp.moveaxis(item.reshape(widest, ranks, cols), 1, 0)
        done.append(item)
    ready = jnp.stack(done, axis=1)
    ready, norm_terms = tie((ready, norm_terms))
    returned = lax.all_to_all(ready, "dp", 0, 0, tiled=True).reshape(each * ranks, widest, cols)
    norm_sum = sum_norms(norm_terms)
    returned, norm_sum = tie((returned, norm_sum))
    return [returned[index, : slab.shape[0]] for index, slab in enumerate(slabs)], norm_sum


def rotated(value, axis, turn):
    count = lax.axis_size(axis)
    return lax.ppermute(value, axis, [(i, (i + turn) % count) for i in range(count)])


def gather_small(piece, axis):
    count = lax.axis_size(axis)
    index = lax.axis_index(axis)
    turned = tie([rotated(piece, axis, turn) for turn in range(1, count)])
    whole = jnp.zeros((count,) + piece.shape, piece.dtype)
    start = (0,) * piece.ndim
    for turn, item in enumerate([piece] + turned):
        whole = lax.dynamic_update_slice(whole, item[None], ((index - turn) % count,) + start)
    return whole


def sum_norms(terms):
    for axis in ("tensor", "dp"):
        count = lax.axis_size(axis)
        bit = 1
        while bit < count:
            terms = terms + lax.ppermute(terms, axis, [(i, i ^ bit) for i in range(count)])
            bit *= 2
    return terms


def per_device(
    tokens,
    cotangent,
    doc_lengths,
    key_weights,
    value_weights,
    out_weights,
    up_weights,
    down_weights,
    key_momentum,
    value_momentum,
    out_momentum,
    up_momentum,
    down_momentum,
    norm_params,
    norm_first,
    norm_second,
):
    tensor_count = lax.axis_size("tensor")
    tensor_index = lax.axis_index("tensor")
    heads = H // tensor_count
    width = tokens.shape[1]
    keys_local = key_weights.shape[2]
    values_local = value_weights.shape[2]
    hidden_local = up_weights.shape[2]
    value_total = values_local * tensor_count
    block = min(LEN, 512)
    ring = Ring()
    half = ring.half
    quarter = half // 4

    def low_t(matrix):
        return matrix.astype(jnp.bfloat16).T

    attend_lanes = gather_lanes(
        ring,
        jnp.concatenate(
            [low_t(key_weights[0]), low_t(key_weights[1]), low_t(value_weights[0]), low_t(value_weights[1])]
        ),
    )
    out_lanes = [Gather(ring, out_weights.astype(jnp.bfloat16), 1)]
    upper_lanes = gather_lanes(ring, jnp.concatenate([low_t(up_weights[0]), low_t(up_weights[1])]))
    down_lanes = [Gather(ring, down_weights.astype(jnp.bfloat16), -1)]
    tokens_all = gather_tokens(tokens)
    own_norms = norm_params.shape[0]
    filled_norms = TILE * ((own_norms + TILE - 1) // TILE)
    norm_piece = jnp.pad(norm_params, (0, filled_norms - own_norms)).reshape(filled_norms // 128, 128)
    norm_group = gather_small(norm_piece, "tensor")
    run(attend_lanes, 2 * quarter)
    gathered_norms = gather_small(tie(norm_group, reached(attend_lanes, quarter)), "dp")
    run(attend_lanes, quarter)
    gathered_norms = gathered_norms.reshape(-1, filled_norms)[:, :own_norms].reshape(-1)

    gain_one = gathered_norms[:width]
    gain_two = gathered_norms[width : 2 * width]
    group_gain = lax.dynamic_slice_in_dim(
        gathered_norms, 2 * width + tensor_index * values_local, values_local
    )[:, None]
    group_bias = lax.dynamic_slice_in_dim(
        gathered_norms, 2 * width + value_total + tensor_index * values_local, values_local
    )[:, None]
    lengths = tie(doc_lengths[0], reached(attend_lanes, quarter))
    starts_all = jnp.cumsum(lengths) - lengths
    positions = jnp.arange(LEN)
    doc_ids = jnp.sum((positions[:, None] >= starts_all[None, :]).astype(jnp.int32), axis=1) - 1

    inputs = tokens.astype(jnp.float32)
    scale_one = root_scale(inputs)
    normed_one = inputs * scale_one
    inputs_all = tokens_all.astype(jnp.float32)
    normed_all = (inputs_all * root_scale(inputs_all) * gain_one).astype(jnp.bfloat16)
    rows_total = normed_all.shape[0]
    grad_rows_two = gather_tokens(tie(cotangent, tokens_all))
    for turn in range(half - 3 * quarter):
        attend_lanes[0].step(normed_all if turn == 0 else None)
        attend_lanes[1].step()
    run(out_lanes, quarter)
    attend_full = assemble(attend_lanes)

    gate_row = 2 * keys_local + values_local
    attend = dot(attend_full[:gate_row], normed_all, 1, 1).astype(jnp.bfloat16)
    attend = tie(attend, reached(out_lanes, quarter))
    run(out_lanes, quarter, attend)
    query = attend[:keys_local].reshape(heads, KEY_HEAD_SIZE, rows_total)
    key = attend[keys_local : 2 * keys_local].reshape(heads, KEY_HEAD_SIZE, rows_total)
    value = attend[2 * keys_local :].reshape(heads, DV, rows_total)
    head_ids = (tensor_index * heads + jnp.arange(heads)).astype(jnp.float32)
    log_gamma = jnp.log(1.0 - jnp.exp2(-5.0 - head_ids))
    mixed_heads = retention_forward(query, key, value, doc_ids, log_gamma, block)
    mixed_heads = tie(mixed_heads, reached(out_lanes, 2 * quarter))
    run(out_lanes, half - 2 * quarter)
    out_full = assemble(out_lanes)
    run(upper_lanes, half)
    run(down_lanes, 2 * quarter)
    upper_full = assemble(upper_lanes)
    gate_pre = dot(attend_full[gate_row:], tie(normed_all, mixed_heads), 1, 1)
    centred = mixed_heads - jnp.mean(mixed_heads, axis=1, keepdims=True)
    group_scale = lax.rsqrt(jnp.mean(centred * centred, axis=1, keepdims=True) + group_floor)
    group_hat = centred * group_scale
    group_flat = group_hat.reshape(values_local, rows_total)
    group_out = group_flat * group_gain + group_bias
    gate_act, silu_pull = jax.vjp(jax.nn.silu, gate_pre)
    mixed_low = (gate_act * group_out).astype(jnp.bfloat16)
    mixed_low, grad_rows_two = tie((mixed_low, grad_rows_two), reached(out_lanes, half))
    branch_one = scatter_tokens(dot(mixed_low, out_full, 0, 0))
    middle = inputs + tie(branch_one, reached(upper_lanes[:1], 3 * quarter), reached(upper_lanes[1:], 2 * quarter))
    scale_two = root_scale(middle)
    normed_two = middle * scale_two
    second_all = gather_tokens((normed_two * gain_two).astype(jnp.bfloat16))
    run(down_lanes, half - 2 * quarter, second_all)
    second_all = tie(second_all, reached(down_lanes, 2 * quarter))
    down_full = assemble(down_lanes)
    hidden_gate = dot(upper_full[:hidden_local], second_all, 1, 1)
    second_late = tie(second_all, hidden_gate, reached(down_lanes, 3 * quarter))
    hidden_upper = dot(upper_full[hidden_local:], second_late, 1, 1)
    gelu_gate, gelu_pull = jax.vjp(partial(jax.nn.gelu, approximate=False), hidden_gate)
    hidden_low = (gelu_gate * hidden_upper).astype(jnp.bfloat16)

    grad_result = cotangent.astype(jnp.float32)
    rows_two_late = tie(grad_rows_two, hidden_low, reached(down_lanes, half))
    grad_down = dot(hidden_low, rows_two_late, 1, 0).astype(jnp.bfloat16)
    down_back = [Scatter(ring, grad_down, 0, hidden_local, -1)]
    run(down_back, half)
    grad_hidden = dot(down_full, tie(grad_rows_two, grad_down), 1, 1)
    grad_gate_mlp = gelu_pull(grad_hidden * hidden_upper)[0].astype(jnp.bfloat16)
    grad_upper_mlp = (grad_hidden * gelu_gate).astype(jnp.bfloat16)
    grad_hidden_low = jnp.concatenate([grad_gate_mlp, grad_upper_mlp])
    grad_hidden_low = tie(grad_hidden_low, loaded(down_back, quarter))
    grad_second = dot(grad_hidden_low, upper_full, 0, 0).astype(jnp.bfloat16)
    grad_second, grad_hidden_late = tie((grad_second, grad_hidden_low))
    grad_second_local = scatter_tokens(tie(grad_second, reached(down_back, 2 * quarter)))
    grad_hidden_late = tie(grad_hidden_late, loaded(down_back, 2 * quarter))
    grad_upper = dot(grad_hidden_late, second_all, 1, 0).astype(jnp.bfloat16)
    upper_back = scatter_lanes(ring, tie(grad_upper, reached(down_back, 3 * quarter)))
    run(upper_back, half)
    grad_second_local = tie(grad_second_local, reached(upper_back[:1], 2 * quarter), loaded(upper_back[1:], quarter))
    grad_gain_two = jnp.sum(grad_second_local * normed_two, axis=0)
    grad_middle = grad_result + norm_back(grad_second_local * gain_two, normed_two, scale_two)
    grad_rows_one = gather_tokens(grad_middle.astype(jnp.bfloat16))
    grad_rows_one = tie(grad_rows_one, loaded(upper_back, 3 * quarter))
    out_back = [Scatter(ring, dot(mixed_low, grad_rows_one, 1, 0).astype(jnp.bfloat16), 0, values_local, 1)]
    run(out_back, quarter)
    grad_mixed = dot(out_full, tie(grad_rows_one, loaded(out_back, 0)), 1, 1)
    grad_mixed = tie(grad_mixed, reached(out_back, quarter))
    grad_gate_low = silu_pull(grad_mixed * group_out)[0].astype(jnp.bfloat16)
    gate_back = [Scatter(ring, dot(grad_gate_low, normed_all, 1, 0).astype(jnp.bfloat16), 0, values_local, -1)]
    run(gate_back, quarter)
    run(out_back + gate_back, half - quarter)
    grad_group = grad_mixed * gate_act
    grad_group_gain = jnp.sum(grad_group * group_flat, axis=1)
    grad_group_bias = jnp.sum(grad_group, axis=1)
    grad_hat = (grad_group * group_gain).reshape(heads, DV, rows_total)
    grad_heads = group_scale * (
        grad_hat
        - jnp.mean(grad_hat, axis=1, keepdims=True)
        - group_hat * jnp.mean(grad_hat * group_hat, axis=1, keepdims=True)
    )
    grad_heads = tie(grad_heads, loaded(out_back, quarter), loaded(gate_back, 0))
    waits = [None, (reached(out_back, 2 * quarter), reached(gate_back, quarter))]
    grad_queries, grad_keys, grad_values = retention_backward(
        query, key, value, grad_heads.astype(jnp.bfloat16), doc_ids, log_gamma, block, waits
    )
    grad_attend_low = jnp.concatenate(
        [
            grad_queries.astype(jnp.bfloat16).reshape(keys_local, rows_total),
            grad_keys.astype(jnp.bfloat16).reshape(keys_local, rows_total),
            grad_values.astype(jnp.bfloat16).reshape(values_local, rows_total),
        ]
    )
    grad_attend_low = tie(grad_attend_low, reached(out_back, 3 * quarter), reached(gate_back, 2 * quarter))
    grad_attend = dot(grad_attend_low, normed_all, 1, 0).astype(jnp.bfloat16)
    attend_back = scatter_lanes(ring, grad_attend)
    run(attend_back, half)
    pieces = []
    for index in range(4):
        lane = attend_back[index % 2]
        rows = slice(index * rows_total // 4, (index + 1) * rows_total // 4)
        late, gate_late = tie((grad_attend_low[:, rows], grad_gate_low[:, rows]), loaded([lane], (1 + index // 2) * quarter))
        piece = dot(late, attend_full[:gate_row], 0, 0) + dot(gate_late, attend_full[gate_row:], 0, 0)
        pieces.append(piece.astype(jnp.bfloat16))
    grad_first = jnp.concatenate(pieces)
    grad_first_local = scatter_tokens(grad_first)
    branch_two = scatter_tokens(dot(tie(hidden_low, grad_first), down_full, 0, 0))
    result = middle + branch_two
    grad_gain_one = jnp.sum(grad_first_local * normed_one, axis=0)
    token_grad = grad_middle + norm_back(grad_first_local * gain_one, normed_one, scale_one)
    group_part = jnp.zeros((2, value_total), jnp.float32)
    group_part = lax.dynamic_update_slice_in_dim(
        group_part, jnp.stack([grad_group_gain, grad_group_bias]), tensor_index * values_local, 1
    )
    norm_terms = jnp.concatenate([grad_gain_one, grad_gain_two, group_part.reshape(-1)])
    norm_place = lax.axis_index("dp") * tensor_count + tensor_index
    grad_down_w = totals(down_back)
    grad_upper_w = totals(upper_back)
    grad_out_w = totals(out_back)
    grad_gate_w = totals(gate_back)
    grad_attend_w = totals(attend_back)

    fresh_query = momentum_decay * key_momentum[0] + grad_attend_w[:keys_local].T
    fresh_key = momentum_decay * key_momentum[1] + grad_attend_w[keys_local : 2 * keys_local].T
    fresh_value = momentum_decay * value_momentum[0] + grad_attend_w[2 * keys_local :].T
    fresh_gate = momentum_decay * value_momentum[1] + grad_gate_w.T
    fresh_out = momentum_decay * out_momentum + grad_out_w
    fresh_hidden = momentum_decay * up_momentum[0] + grad_upper_w[:hidden_local].T
    fresh_upper = momentum_decay * up_momentum[1] + grad_upper_w[hidden_local:].T
    fresh_down = momentum_decay * down_momentum + grad_down_w
    orth, norm_sum = orthogonalize(
        [
            fresh_down,
            fresh_hidden.T,
            fresh_upper.T,
            fresh_out,
            fresh_gate.T,
            fresh_value.T,
            fresh_query.T,
            fresh_key.T,
        ],
        norm_terms,
    )
    norm_grad = lax.dynamic_slice_in_dim(norm_sum, norm_place * own_norms, own_norms)
    orth = [item.astype(jnp.float32) for item in orth]
    keep_factor = 1.0 - muon_rate * weight_decay

    def rate(rows, cols):
        return muon_rate * math.sqrt(max(1.0, rows / cols))

    new_key_weights = key_weights * keep_factor - rate(width, keys_local) * jnp.stack([orth[6].T, orth[7].T])
    new_value_weights = value_weights * keep_factor - rate(width, values_local) * jnp.stack([orth[5].T, orth[4].T])
    new_upper_weights = up_weights * keep_factor - rate(width, hidden_local) * jnp.stack([orth[1].T, orth[2].T])
    new_out_weights = out_weights * keep_factor - rate(values_local, width) * orth[3]
    new_down_weights = down_weights * keep_factor - rate(hidden_local, width) * orth[0]
    new_norm_first = beta_first * norm_first + (1.0 - beta_first) * norm_grad
    new_norm_second = beta_second * norm_second + (1.0 - beta_second) * norm_grad * norm_grad
    fix_first = 1.0 - beta_first**STEP
    fix_second = 1.0 - beta_second**STEP
    new_norm_params = norm_params - adam_rate * (new_norm_first / fix_first) / (
        jnp.sqrt(new_norm_second / fix_second) + adam_eps
    )
    return (
        result.astype(jnp.bfloat16),
        token_grad,
        jnp.stack([fresh_query, fresh_key]),
        jnp.stack([fresh_value, fresh_gate]),
        fresh_out,
        jnp.stack([fresh_hidden, fresh_upper]),
        fresh_down,
        new_key_weights,
        new_value_weights,
        new_out_weights,
        new_upper_weights,
        new_down_weights,
        new_norm_first,
        new_norm_second,
        new_norm_params,
    )


def solution(mesh):
    tokens = P(("dp", "tensor"), None)
    wide = P(None, "dp", "tensor")
    tall = P("tensor", "dp")
    norms = P(("dp", "tensor"))
    return jax.shard_map(
        per_device,
        mesh=mesh,
        in_specs=(
            tokens, tokens, P("dp", None), wide, wide, tall, wide, tall,
            wide, wide, tall, wide, tall, norms, norms, norms,
        ),
        out_specs=(
            tokens, tokens, wide, wide, tall, wide, tall,
            wide, wide, tall, wide, tall, norms, norms, norms,
        ),
        check_vma=False,
    )
```

```python
from functools import partial
import math

import jax
import jax.numpy as jnp
from jax import lax
from jax.experimental import pallas as pl
from jax.experimental.pallas import tpu as pltpu
from jax.sharding import PartitionSpec as P

H = 8
KEY_HEAD_SIZE = 256
DV = 432
LEN = 1024
NS_ITERS = 5
STEP = 10


eps_norm = 1e-05
group_floor = 1.0
ns_first = 3.4445
ns_second = -4.775
ns_third = 2.0315
momentum_decay = 0.95
muon_rate = 0.5
weight_decay = 0.1
beta_first = 0.9
beta_second = 0.95
adam_rate = 0.8
adam_eps = 1e-08
TILE = 1024


def root_scale(values):
    return lax.rsqrt(jnp.mean(values * values, axis=-1, keepdims=True) + eps_norm)


def norm_back(grad_normed, normed, scaling):
    return scaling * (grad_normed - normed * jnp.mean(grad_normed * normed, axis=-1, keepdims=True))


def dot(left, right, left_dim, right_dim):
    return lax.dot_general(
        left, right, (((left_dim,), (right_dim,)), ((), ())), preferred_element_type=jnp.float32
    )


def gather_tokens(values):
    return lax.all_gather(values, "tensor", axis=0, tiled=True)


def scatter_tokens(values):
    return lax.psum_scatter(
        values.astype(jnp.bfloat16), "tensor", scatter_dimension=0, tiled=True
    ).astype(jnp.float32)


def ring_order(count):
    return list(range(0, count, 2)) + list(range(count - 1, 0, -2))


def ring_place(count):
    order = ring_order(count)
    return order, [(order[i], order[(i + 1) % count]) for i in range(count)]


def tie(value, *others):
    return lax.optimization_barrier((value, others))[0]


class Ring:
    def __init__(self):
        self.count = lax.axis_size("dp")
        order, self.right = ring_place(self.count)
        self.left = [(b, a) for a, b in self.right]
        self.half = self.count // 2
        place_of = [order.index(rank) for rank in range(self.count)]
        place = jnp.asarray(place_of, jnp.int32)[lax.axis_index("dp")]
        steps = jnp.arange(self.count, dtype=jnp.int32)
        self.rank_at = jnp.asarray(order, jnp.int32)[(place + steps) % self.count]
        self.sent = []
        self.added = None

    def rank(self, distance):
        return self.rank_at[distance % self.count]

    def exchange(self, blocks):
        if len(self.sent) > 2:
            blocks = tie(blocks, self.sent[-3])
        got = {}
        for side, block in blocks.items():
            got[side] = lax.ppermute(block, "dp", self.right if side > 0 else self.left)
        self.sent.append(got)
        return got


class Gather:
    def __init__(self, ring, shard, long_side):
        self.ring = ring
        self.shard = shard
        self.long_side = long_side
        self.rows, self.width = shard.shape
        self.blocks = [(shard, 0)]
        self.held = {1: shard, -1: shard}
        self.marks = []

    def step(self, after=None):
        at = len(self.marks) + 1
        sides = (1, -1) if at < self.ring.half else (self.long_side,)
        blocks = {side: self.held[side] for side in sides}
        if after is not None:
            blocks = tie(blocks, after)
        self.held = self.ring.exchange(blocks)
        self.blocks += [(self.held[side], -side * at) for side in sides]
        self.marks.append(self.held)


def run(lanes, rounds, after=None):
    for turn in range(rounds):
        for lane in lanes:
            lane.step(after if turn == 0 else None)


def reached(lanes, rounds):
    return [lane.marks[rounds - 1] for lane in lanes]


def loaded(lanes, rounds):
    return [lane.loads[rounds] for lane in lanes]


def nothing_kernel(out_ref):
    pass


def unwritten(shape, dtype):
    return pl.pallas_call(
        nothing_kernel,
        out_shape=jax.ShapeDtypeStruct(shape, dtype),
        out_specs=pl.BlockSpec(memory_space=pl.ANY),
    )()


def assemble(lanes):
    ring = lanes[0].ring
    width = lanes[0].width
    full = unwritten((sum(lane.rows for lane in lanes), width * ring.count), lanes[0].shard.dtype)
    placed, base = [], 0
    for lane in lanes:
        lane.blocks[0] = tie(lane.shard, lane.marks[0]), 0
        placed += [(index, base, block, distance) for index, (block, distance) in enumerate(lane.blocks)]
        base += lane.rows
    for _, row, block, distance in sorted(placed, key=lambda item: item[0]):
        full = lax.dynamic_update_slice(full, block, (row, ring.rank(distance) * width))
    return full


class Scatter:
    def __init__(self, ring, full, first, rows, long_side):
        self.ring = ring
        self.full = full
        self.first = first
        self.rows = rows
        self.long_side = long_side
        self.width = full.shape[1] // ring.count
        self.held = {}
        self.marks = []
        self.loads = []

    def piece(self, distance):
        column = self.ring.rank(distance) * self.width
        return lax.dynamic_slice(self.full, (self.first, column), (self.rows, self.width))

    def step(self, after=None):
        ring = self.ring
        at = ring.half - len(self.marks)
        came = self.held
        if came and ring.added is not None:
            came = tie(came, ring.added)
        sides = (1, -1) if at < ring.half else (self.long_side,)
        blocks = {}
        for side in sides:
            block = self.piece(side * at)
            if side in came:
                block = (block.astype(jnp.float32) + came[side].astype(jnp.float32)).astype(jnp.bfloat16)
            blocks[side] = block
        if came:
            ring.added = blocks
        self.loads.append(blocks)
        self.held = ring.exchange(blocks)
        self.marks.append(self.held)

    def total(self):
        own = self.piece(0).astype(jnp.float32)
        return own + self.held[1].astype(jnp.float32) + self.held[-1].astype(jnp.float32)


def halves(rows):
    cut = (rows // 2 + 15) // 16 * 16
    return [(0, cut, 1), (cut, rows - cut, -1)]


def gather_lanes(ring, shard):
    return [Gather(ring, shard[first : first + size], side) for first, size, side in halves(shard.shape[0])]


def scatter_lanes(ring, full):
    return [Scatter(ring, full, first, size, side) for first, size, side in halves(full.shape[0])]


def totals(lanes):
    return jnp.concatenate([lane.total() for lane in lanes])


def decay_rows(doc_ids, log_gamma, first, size, keys):
    query_pos = first + jnp.arange(size)
    key_pos = jnp.arange(keys)
    distance = query_pos[:, None] - key_pos[None, :]
    allowed = (doc_ids[first : first + size, None] == doc_ids[None, :keys]) & (distance >= 0)
    steps_back = jnp.maximum(distance, 0).astype(jnp.float32)
    falloff = jnp.exp(log_gamma[:, None, None] * steps_back[None])
    return jnp.where(allowed[None], falloff, 0.0)


def einsum32(spec, left, right):
    return jnp.einsum(spec, left, right, preferred_element_type=jnp.float32)


def retention_forward(query, key, value, doc_ids, log_gamma, block):
    factor = KEY_HEAD_SIZE ** (-0.5)
    pieces = []
    for first in range(0, LEN, block):
        keys = first + block
        falloff = decay_rows(doc_ids, log_gamma, first, block, keys)
        scores = einsum32("hdq,hdk->hqk", query[:, :, first:keys], key[:, :, :keys]) * factor
        weights = (scores * falloff).astype(jnp.bfloat16)
        pieces.append(einsum32("hdk,hqk->hdq", value[:, :, :keys], weights))
    return jnp.concatenate(pieces, axis=2)


def retention_backward(query, key, value, grad, doc_ids, log_gamma, block, waits):
    factor = KEY_HEAD_SIZE ** (-0.5)
    grad_query = []
    grad_key = jnp.zeros(key.shape, jnp.float32)
    grad_value = jnp.zeros(value.shape, jnp.float32)
    for first in range(0, LEN, block):
        keys = first + block
        falloff = decay_rows(doc_ids, log_gamma, first, block, keys)
        query_now, grad_now = query[:, :, first:keys], grad[:, :, first:keys]
        if waits[first // block] is not None:
            grad_now = tie(grad_now, waits[first // block])
        scores = einsum32("hdq,hdk->hqk", query_now, key[:, :, :keys]) * factor
        weights = (scores * falloff).astype(jnp.bfloat16)
        grad_weights = einsum32("hdq,hdk->hqk", grad_now, value[:, :, :keys])
        grad_scores = (grad_weights * falloff).astype(jnp.bfloat16)
        grad_query.append(einsum32("hdk,hqk->hdq", key[:, :, :keys], grad_scores) * factor)
        grad_key = grad_key.at[:, :, :keys].add(einsum32("hdq,hqk->hdk", query_now, grad_scores) * factor)
        grad_value = grad_value.at[:, :, :keys].add(einsum32("hdq,hqk->hdk", grad_now, weights))
    return jnp.concatenate(grad_query, axis=2), grad_key, grad_value


def newton_schulz_kernel(turns, parts, step, flag_ref, *refs):
    @pl.when(flag_ref[0] == 1)
    def _():
        newton_schulz_turns(turns, step, refs[:parts], refs[parts : 2 * parts], *refs[2 * parts :])


def newton_schulz_turns(turns, step, in_refs, out_refs, cur_ref, low_ref, rest_ref, poly_ref, scale_ref):
    size, band = in_refs[0].shape
    parts = len(in_refs)
    width = parts * band
    blocks = size // step

    def rows_of(index):
        return pl.ds(pl.multiple_of(index * step, step), step)

    def first_sum(index, total):
        rows = rows_of(index)
        for part in range(parts):
            block = in_refs[part][rows, :].astype(jnp.float32)
            total = total + jnp.sum(block * block)
        return total

    total = lax.fori_loop(0, blocks, first_sum, jnp.float32(0.0))
    scale_ref[...] = 1.0 / (jnp.sqrt(jnp.full(scale_ref.shape, total)) + 1e-07)

    @pl.loop(0, blocks)
    def _(index):
        rows = rows_of(index)
        scale = scale_ref[0, 0]
        for part in range(parts):
            block = in_refs[part][rows, :].astype(jnp.float32) * scale
            columns = slice(part * band, (part + 1) * band)
            cur_ref[rows, columns] = block
            low_ref[0, rows, columns] = block.astype(jnp.bfloat16)

    bands = [(first, min(256, size - first)) for first in range(0, size, 256)]

    def turn_body(turn, norm, last):
        here = lax.rem(turn, 2)
        there = 1 - here
        middle = norm * (1.0 / size)
        low = low_ref.at[here]
        for first, wide in bands:
            gram = dot(low[...], low[first : first + wide, :], 1, 1)
            place = lax.broadcasted_iota(jnp.int32, gram.shape, 0)
            eye = place == lax.broadcasted_iota(jnp.int32, gram.shape, 1) + first
            rest_ref[:, first : first + wide] = jnp.where(eye, gram - middle, gram).astype(jnp.bfloat16)
        for first, wide in bands:
            rest = rest_ref[:, first : first + wide]
            square = dot(rest_ref[...], rest, 1, 0)
            poly = (ns_second + 2.0 * ns_third * middle) * rest.astype(jnp.float32) + ns_third * square
            poly_ref[:, first : first + wide] = poly.astype(jnp.bfloat16)
        outer = ns_first + middle * (ns_second + ns_third * middle)

        total = jnp.zeros((1, band), jnp.float32)
        for first in range(0, width, band):
            columns = slice(first, first + band)
            fresh = outer * cur_ref[:, columns] + dot(poly_ref[...], low[:, columns], 1, 0)
            if last:
                out_refs[first // band][...] = fresh.astype(jnp.bfloat16)
            else:
                cur_ref[:, columns] = fresh
                low_ref[there, :, columns] = fresh.astype(jnp.bfloat16)
                total = total + jnp.sum(fresh * fresh, axis=0, keepdims=True)
        return jnp.sum(total)

    norm = lax.fori_loop(0, turns - 1, lambda turn, norm: turn_body(turn, norm, False), jnp.float32(1.0))
    turn_body(turns - 1, norm, True)


def newton_schulz(parts, mine):
    size, band = parts[0].shape
    count = len(parts)
    width = count * band
    step = next(step for step in range(288, 0, -16) if size % step == 0)
    products = 2 * size * size * (2 * width + size) * NS_ITERS
    whole = pl.BlockSpec(memory_space=pltpu.VMEM)
    return pl.pallas_call(
        partial(newton_schulz_kernel, NS_ITERS, count, step),
        out_shape=[jax.ShapeDtypeStruct((size, band), jnp.bfloat16)] * count,
        in_specs=[pl.BlockSpec(memory_space=pltpu.SMEM)] + [whole] * count,
        out_specs=[whole] * count,
        scratch_shapes=[
            pltpu.VMEM((size, width), jnp.float32),
            pltpu.VMEM((2, size, width), jnp.bfloat16),
            pltpu.VMEM((size, size), jnp.bfloat16),
            pltpu.VMEM((size, size), jnp.bfloat16),
            pltpu.VMEM((8, 128), jnp.float32),
        ],
        compiler_params=pltpu.CompilerParams(vmem_limit_bytes=48 * 1024 * 1024),
        cost_estimate=pl.CostEstimate(flops=products, bytes_accessed=4 * size * width, transcendentals=0),
    )(mine, *parts)


class Owners:
    def __init__(self, ranks):
        self.ranks = ranks
        self.count = lax.axis_size("dp")
        self.index = lax.axis_index("dp")
        slots = [ranks.index(rank) if rank in ranks else len(ranks) for rank in range(self.count)]
        steps = (self.index + jnp.arange(self.count)) % self.count
        self.slots = jnp.asarray(slots, jnp.int32)[steps]
        self.mine = (self.slots[0] < len(ranks)).astype(jnp.int32).reshape(1)

    def send(self, slabs):
        rows = max(slab.shape[0] for slab in slabs)
        stacked = jnp.stack([jnp.pad(slab, ((0, rows - slab.shape[0]), (0, 0))) for slab in slabs])
        last = len(self.ranks) - 1
        blocks = []
        for turn in range(self.count):
            block = lax.dynamic_index_in_dim(stacked, jnp.minimum(self.slots[turn], last), 0, False)
            if turn:
                pairs = [((rank - turn) % self.count, rank) for rank in self.ranks]
                block = lax.ppermute(block, "dp", pairs)
            blocks.append(block)
        return blocks

    def orthogonalize(self, blocks):
        rows, cols = blocks[0].shape
        each = max(1, 256 // cols)
        if each == 1:
            return newton_schulz(blocks, self.mine)
        parts = [jnp.concatenate(blocks[i : i + each], axis=1) for i in range(0, self.count, each)]
        done = newton_schulz(parts, self.mine)
        return [part[:, i * cols : (i + 1) * cols] for part in done for i in range(each)]

    def give_back(self, blocks, turns):
        came = []
        for turn in turns:
            block = blocks[turn]
            if turn:
                pairs = [(rank, (rank - turn) % self.count) for rank in self.ranks]
                block = lax.ppermute(block, "dp", pairs)
            came.append(block)
        return came

    def place(self, came):
        whole = unwritten((len(self.ranks) + 1,) + came[0].shape, came[0].dtype)
        for turn, block in enumerate(came):
            whole = lax.dynamic_update_slice(whole, block[None], (self.slots[turn], 0, 0))
        return whole


def rotated(value, axis, turn):
    count = lax.axis_size(axis)
    return lax.ppermute(value, axis, [(i, (i + turn) % count) for i in range(count)])


def gather_small(piece, axis):
    count = lax.axis_size(axis)
    index = lax.axis_index(axis)
    turned = tie([rotated(piece, axis, turn) for turn in range(1, count)])
    whole = jnp.zeros((count,) + piece.shape, piece.dtype)
    start = (0,) * piece.ndim
    for turn, item in enumerate([piece] + turned):
        whole = lax.dynamic_update_slice(whole, item[None], ((index - turn) % count,) + start)
    return whole


def sum_tensor(terms):
    count = lax.axis_size("tensor")
    bit = 1
    while bit < count:
        terms = terms + lax.ppermute(terms, "tensor", [(i, i ^ bit) for i in range(count)])
        bit *= 2
    return terms


def sum_dp(terms, own):
    count = lax.axis_size("dp")
    group = terms.shape[0] // count
    filled = TILE * ((group + TILE - 1) // TILE)
    rows = jnp.pad(terms.reshape(count, group), ((0, 0), (0, filled - group))).reshape(-1, 128)
    mine = lax.psum_scatter(rows, "dp", scatter_dimension=0, tiled=True).reshape(-1)
    return lax.dynamic_slice_in_dim(mine, lax.axis_index("tensor") * own, own)


def per_device(
    tokens,
    cotangent,
    doc_lengths,
    key_weights,
    value_weights,
    out_weights,
    up_weights,
    down_weights,
    key_momentum,
    value_momentum,
    out_momentum,
    up_momentum,
    down_momentum,
    norm_params,
    norm_first,
    norm_second,
):
    tensor_count = lax.axis_size("tensor")
    tensor_index = lax.axis_index("tensor")
    heads = H // tensor_count
    width = tokens.shape[1]
    keys_local = key_weights.shape[2]
    values_local = value_weights.shape[2]
    hidden_local = up_weights.shape[2]
    value_total = values_local * tensor_count
    block = min(LEN, 512)
    ring = Ring()
    half = ring.half
    quarter = half // 4

    def low_t(matrix):
        return matrix.astype(jnp.bfloat16).T

    attend_lanes = gather_lanes(
        ring,
        jnp.concatenate(
            [low_t(key_weights[0]), low_t(key_weights[1]), low_t(value_weights[0]), low_t(value_weights[1])]
        ),
    )
    out_lanes = [Gather(ring, out_weights.astype(jnp.bfloat16), 1)]
    upper_lanes = gather_lanes(ring, jnp.concatenate([low_t(up_weights[0]), low_t(up_weights[1])]))
    down_lanes = [Gather(ring, down_weights.astype(jnp.bfloat16), -1)]
    tokens_all = gather_tokens(tokens)
    own_norms = norm_params.shape[0]
    filled_norms = TILE * ((own_norms + TILE - 1) // TILE)
    norm_piece = jnp.pad(norm_params, (0, filled_norms - own_norms)).reshape(filled_norms // 128, 128)
    norm_group = gather_small(norm_piece, "tensor")
    run(attend_lanes, 2 * quarter)
    gathered_norms = gather_small(tie(norm_group, reached(attend_lanes[:1], 2 * quarter)), "dp")
    attend_lanes[0].step(gathered_norms)
    gathered_norms = gathered_norms.reshape(-1, filled_norms)[:, :own_norms].reshape(-1)

    gain_one = gathered_norms[:width]
    gain_two = gathered_norms[width : 2 * width]
    group_gain = lax.dynamic_slice_in_dim(
        gathered_norms, 2 * width + tensor_index * values_local, values_local
    )[:, None]
    group_bias = lax.dynamic_slice_in_dim(
        gathered_norms, 2 * width + value_total + tensor_index * values_local, values_local
    )[:, None]
    lengths = tie(doc_lengths[0], reached(attend_lanes, quarter))
    starts_all = jnp.cumsum(lengths) - lengths
    positions = jnp.arange(LEN)
    doc_ids = jnp.sum((positions[:, None] >= starts_all[None, :]).astype(jnp.int32), axis=1) - 1

    inputs = tokens.astype(jnp.float32)
    scale_one = root_scale(inputs)
    normed_one = inputs * scale_one
    inputs_all = tokens_all.astype(jnp.float32)
    normed_all = (inputs_all * root_scale(inputs_all) * gain_one).astype(jnp.bfloat16)
    rows_total = normed_all.shape[0]
    grad_rows_two = gather_tokens(tie(cotangent, tokens_all))
    attend_lanes[1].step(normed_all)
    run(attend_lanes, half - 2 * quarter - 1)
    run(out_lanes, quarter)
    attend_full = assemble(attend_lanes)

    gate_row = 2 * keys_local + values_local
    attend = dot(attend_full[:gate_row], normed_all, 1, 1).astype(jnp.bfloat16)
    attend = tie(attend, reached(out_lanes, quarter))
    run(out_lanes, quarter)
    query = attend[:keys_local].reshape(heads, KEY_HEAD_SIZE, rows_total)
    key = attend[keys_local : 2 * keys_local].reshape(heads, KEY_HEAD_SIZE, rows_total)
    value = attend[2 * keys_local :].reshape(heads, DV, rows_total)
    head_ids = (tensor_index * heads + jnp.arange(heads)).astype(jnp.float32)
    log_gamma = jnp.log(1.0 - jnp.exp2(-5.0 - head_ids))
    mixed_heads = retention_forward(query, key, value, doc_ids, log_gamma, block)
    mixed_heads = tie(mixed_heads, reached(out_lanes, 2 * quarter))
    run(out_lanes, half - 2 * quarter)
    out_full = assemble(out_lanes)
    run(upper_lanes, half)
    run(down_lanes, 2 * quarter)
    upper_full = assemble(upper_lanes)
    gate_pre = dot(attend_full[gate_row:], tie(normed_all, mixed_heads), 1, 1)
    centred = mixed_heads - jnp.mean(mixed_heads, axis=1, keepdims=True)
    group_scale = lax.rsqrt(jnp.mean(centred * centred, axis=1, keepdims=True) + group_floor)
    group_hat = centred * group_scale
    group_flat = group_hat.reshape(values_local, rows_total)
    group_out = group_flat * group_gain + group_bias
    gate_act, silu_pull = jax.vjp(jax.nn.silu, gate_pre)
    mixed_low = (gate_act * group_out).astype(jnp.bfloat16)
    mixed_low, grad_rows_two = tie((mixed_low, grad_rows_two), reached(out_lanes, half))
    branch_one = scatter_tokens(dot(mixed_low, out_full, 0, 0))
    middle = inputs + tie(branch_one, reached(upper_lanes[:1], 3 * quarter), reached(upper_lanes[1:], 2 * quarter))
    scale_two = root_scale(middle)
    normed_two = middle * scale_two
    second_all = gather_tokens((normed_two * gain_two).astype(jnp.bfloat16))
    run(down_lanes, half - 2 * quarter, second_all)
    second_all = tie(second_all, reached(down_lanes, 2 * quarter))
    down_full = assemble(down_lanes)
    hidden_gate = dot(upper_full[:hidden_local], second_all, 1, 1)
    second_late = tie(second_all, hidden_gate, reached(down_lanes, 3 * quarter))
    hidden_upper = dot(upper_full[hidden_local:], second_late, 1, 1)
    gelu_gate, gelu_pull = jax.vjp(partial(jax.nn.gelu, approximate=False), hidden_gate)
    hidden_low = (gelu_gate * hidden_upper).astype(jnp.bfloat16)

    grad_result = cotangent.astype(jnp.float32)
    rows_two_late = tie(grad_rows_two, hidden_low, reached(down_lanes, half))
    grad_down = dot(hidden_low, rows_two_late, 1, 0).astype(jnp.bfloat16)
    down_back = [Scatter(ring, grad_down, 0, hidden_local, -1)]
    run(down_back, half)
    grad_hidden = dot(down_full, tie(grad_rows_two, grad_down), 1, 1)
    grad_gate_mlp = gelu_pull(grad_hidden * hidden_upper)[0].astype(jnp.bfloat16)
    grad_upper_mlp = (grad_hidden * gelu_gate).astype(jnp.bfloat16)
    grad_hidden_low = jnp.concatenate([grad_gate_mlp, grad_upper_mlp])
    grad_hidden_low = tie(grad_hidden_low, loaded(down_back, quarter))
    grad_second = dot(grad_hidden_low, upper_full, 0, 0).astype(jnp.bfloat16)
    grad_second, grad_hidden_late = tie((grad_second, grad_hidden_low))
    grad_second_local = scatter_tokens(tie(grad_second, reached(down_back, 2 * quarter)))
    grad_hidden_late = tie(grad_hidden_late, loaded(down_back, 2 * quarter))
    grad_upper = dot(grad_hidden_late, second_all, 1, 0).astype(jnp.bfloat16)
    upper_back = scatter_lanes(ring, tie(grad_upper, reached(down_back, 3 * quarter)))
    run(upper_back, half)
    grad_second_local = tie(grad_second_local, reached(upper_back[:1], 2 * quarter), loaded(upper_back[1:], quarter))
    grad_gain_two = jnp.sum(grad_second_local * normed_two, axis=0)
    grad_middle = grad_result + norm_back(grad_second_local * gain_two, normed_two, scale_two)
    grad_rows_one = gather_tokens(grad_middle.astype(jnp.bfloat16))
    grad_rows_one = tie(grad_rows_one, loaded(upper_back, 3 * quarter))
    out_back = [Scatter(ring, dot(mixed_low, grad_rows_one, 1, 0).astype(jnp.bfloat16), 0, values_local, 1)]
    run(out_back, quarter)
    grad_mixed = dot(out_full, tie(grad_rows_one, loaded(out_back, 0)), 1, 1)
    grad_mixed = tie(grad_mixed, reached(out_back, quarter))
    grad_gate_low = silu_pull(grad_mixed * group_out)[0].astype(jnp.bfloat16)
    gate_back = [Scatter(ring, dot(grad_gate_low, normed_all, 1, 0).astype(jnp.bfloat16), 0, values_local, -1)]
    run(gate_back, quarter)
    run(out_back + gate_back, half - quarter)
    grad_group = grad_mixed * gate_act
    grad_group_gain = jnp.sum(grad_group * group_flat, axis=1)
    grad_group_bias = jnp.sum(grad_group, axis=1)
    grad_hat = (grad_group * group_gain).reshape(heads, DV, rows_total)
    grad_heads = group_scale * (
        grad_hat
        - jnp.mean(grad_hat, axis=1, keepdims=True)
        - group_hat * jnp.mean(grad_hat * group_hat, axis=1, keepdims=True)
    )
    grad_heads = tie(grad_heads, loaded(out_back, quarter), loaded(gate_back, 0))
    waits = [None, (reached(out_back, 2 * quarter), reached(gate_back, quarter))]
    grad_queries, grad_keys, grad_values = retention_backward(
        query, key, value, grad_heads.astype(jnp.bfloat16), doc_ids, log_gamma, block, waits
    )
    grad_attend_low = jnp.concatenate(
        [
            grad_queries.astype(jnp.bfloat16).reshape(keys_local, rows_total),
            grad_keys.astype(jnp.bfloat16).reshape(keys_local, rows_total),
            grad_values.astype(jnp.bfloat16).reshape(values_local, rows_total),
        ]
    )
    grad_attend_low = tie(grad_attend_low, reached(out_back, 3 * quarter), reached(gate_back, 2 * quarter))
    grad_attend = dot(grad_attend_low, normed_all, 1, 0).astype(jnp.bfloat16)
    attend_back = scatter_lanes(ring, grad_attend)
    run(attend_back, half)
    pieces = []
    for index in range(4):
        lane = attend_back[index % 2]
        rows = slice(index * rows_total // 4, (index + 1) * rows_total // 4)
        late, gate_late = tie((grad_attend_low[:, rows], grad_gate_low[:, rows]), loaded([lane], (1 + index // 2) * quarter))
        piece = dot(late, attend_full[:gate_row], 0, 0) + dot(gate_late, attend_full[gate_row:], 0, 0)
        pieces.append(piece.astype(jnp.bfloat16))
    grad_first = jnp.concatenate(pieces)
    grad_first_local = scatter_tokens(grad_first)
    branch_two = scatter_tokens(dot(tie(hidden_low, grad_first), down_full, 0, 0))
    result = middle + branch_two
    grad_gain_one = jnp.sum(grad_first_local * normed_one, axis=0)
    token_grad = grad_middle + norm_back(grad_first_local * gain_one, normed_one, scale_one)
    group_part = jnp.zeros((2, value_total), jnp.float32)
    group_part = lax.dynamic_update_slice_in_dim(
        group_part, jnp.stack([grad_group_gain, grad_group_bias]), tensor_index * values_local, 1
    )
    norm_terms = jnp.concatenate([grad_gain_one, grad_gain_two, group_part.reshape(-1)])
    grad_down_w = totals(down_back)
    grad_upper_w = totals(upper_back)
    grad_out_w = totals(out_back)
    grad_gate_w = totals(gate_back)
    grad_attend_w = totals(attend_back)

    fresh_query = momentum_decay * key_momentum[0] + grad_attend_w[:keys_local].T
    fresh_key = momentum_decay * key_momentum[1] + grad_attend_w[keys_local : 2 * keys_local].T
    fresh_value = momentum_decay * value_momentum[0] + grad_attend_w[2 * keys_local :].T
    fresh_gate = momentum_decay * value_momentum[1] + grad_gate_w.T
    fresh_out = momentum_decay * out_momentum + grad_out_w
    fresh_hidden = momentum_decay * up_momentum[0] + grad_upper_w[:hidden_local].T
    fresh_upper = momentum_decay * up_momentum[1] + grad_upper_w[hidden_local:].T
    fresh_down = momentum_decay * down_momentum + grad_down_w
    def low_rows(fresh):
        return fresh.astype(jnp.bfloat16)

    early = Owners([0, 3, 4, 7])
    late = Owners([1, 2, 5, 6])
    early_slabs = [low_rows(fresh_down), low_rows(fresh_hidden.T), low_rows(fresh_upper.T), low_rows(fresh_out)]
    late_slabs = [low_rows(fresh_gate.T), low_rows(fresh_value.T), low_rows(fresh_query.T), low_rows(fresh_key.T)]
    early_blocks = early.send(tie(early_slabs, loaded(attend_back, 3 * quarter)))
    late_slabs = tie(late_slabs, early_blocks[0])
    norm_terms = sum_tensor(norm_terms)
    late_blocks = late.send(late_slabs)
    early_blocks = tie(early_blocks, late_slabs, norm_terms)
    norm_grad = sum_dp(norm_terms, norm_params.shape[0])
    early_done = early.orthogonalize(early_blocks)
    late_blocks, early_done = tie((late_blocks, early_done))
    turns = list(range(early.count))
    early_came = early.give_back(early_done, turns[:6])
    late_done = late.orthogonalize(late_blocks)
    early_done, late_done = tie((early_done, late_done), early_came)
    early_came += early.give_back(early_done, turns[6:])
    late_came = late.give_back(late_done, turns[:5]) + late.give_back(tie(late_done, norm_grad), turns[5:])
    early_orth = early.place(early_came)
    late_orth = late.place(tie(late_came, early_came))
    early_orth = early_orth.astype(jnp.float32)
    late_orth = late_orth.astype(jnp.float32)
    keep_factor = 1.0 - muon_rate * weight_decay

    def rate(rows, cols):
        return muon_rate * math.sqrt(max(1.0, rows / cols))

    new_key_weights = key_weights * keep_factor - rate(width, keys_local) * jnp.swapaxes(
        late_orth[2:4, :keys_local], 1, 2
    )
    new_value_weights = value_weights * keep_factor - rate(width, values_local) * jnp.stack(
        [late_orth[1, :values_local].T, late_orth[0, :values_local].T]
    )
    new_upper_weights = up_weights * keep_factor - rate(width, hidden_local) * jnp.swapaxes(
        early_orth[1:3, :hidden_local], 1, 2
    )
    new_out_weights = out_weights * keep_factor - rate(values_local, width) * early_orth[3, :values_local]
    new_down_weights = down_weights * keep_factor - rate(hidden_local, width) * early_orth[0, :hidden_local]
    new_norm_first = beta_first * norm_first + (1.0 - beta_first) * norm_grad
    new_norm_second = beta_second * norm_second + (1.0 - beta_second) * norm_grad * norm_grad
    fix_first = 1.0 - beta_first**STEP
    fix_second = 1.0 - beta_second**STEP
    new_norm_params = norm_params - adam_rate * (new_norm_first / fix_first) / (
        jnp.sqrt(new_norm_second / fix_second) + adam_eps
    )
    return (
        result.astype(jnp.bfloat16),
        token_grad,
        jnp.stack([fresh_query, fresh_key]),
        jnp.stack([fresh_value, fresh_gate]),
        fresh_out,
        jnp.stack([fresh_hidden, fresh_upper]),
        fresh_down,
        new_key_weights,
        new_value_weights,
        new_out_weights,
        new_upper_weights,
        new_down_weights,
        new_norm_first,
        new_norm_second,
        new_norm_params,
    )


def solution(mesh):
    tokens = P(("dp", "tensor"), None)
    wide = P(None, "dp", "tensor")
    tall = P("tensor", "dp")
    norms = P(("dp", "tensor"))
    return jax.shard_map(
        per_device,
        mesh=mesh,
        in_specs=(
            tokens, tokens, P("dp", None), wide, wide, tall, wide, tall,
            wide, wide, tall, wide, tall, norms, norms, norms,
        ),
        out_specs=(
            tokens, tokens, wide, wide, tall, wide, tall,
            wide, wide, tall, wide, tall, norms, norms, norms,
        ),
        check_vma=False,
    )
```

```python
from functools import partial
import math

import jax
import jax.numpy as jnp
from jax import lax
from jax.experimental import pallas as pl
from jax.experimental.pallas import tpu as pltpu
from jax.sharding import PartitionSpec as P

H = 8
KEY_HEAD_SIZE = 256
DV = 432
LEN = 1024
NS_ITERS = 5
STEP = 10


eps_norm = 1e-05
group_floor = 1.0
ns_first = 3.4445
ns_second = -4.775
ns_third = 2.0315
momentum_decay = 0.95
muon_rate = 0.5
weight_decay = 0.1
beta_first = 0.9
beta_second = 0.95
adam_rate = 0.8
adam_eps = 1e-08
TILE = 1024


def root_scale(values):
    return lax.rsqrt(jnp.mean(values * values, axis=-1, keepdims=True) + eps_norm)


def norm_back(grad_normed, normed, scaling):
    return scaling * (grad_normed - normed * jnp.mean(grad_normed * normed, axis=-1, keepdims=True))


def dot(left, right, left_dim, right_dim):
    return lax.dot_general(
        left, right, (((left_dim,), (right_dim,)), ((), ())), preferred_element_type=jnp.float32
    )


def gather_tokens(values):
    return lax.all_gather(values, "tensor", axis=0, tiled=True)


def scatter_tokens(values):
    return lax.psum_scatter(
        values.astype(jnp.bfloat16), "tensor", scatter_dimension=0, tiled=True
    ).astype(jnp.float32)


def ring_order(count):
    return list(range(0, count, 2)) + list(range(count - 1, 0, -2))


def ring_place(count):
    order = ring_order(count)
    return order, [(order[i], order[(i + 1) % count]) for i in range(count)]


def tie(value, *others):
    return lax.optimization_barrier((value, others))[0]


class Ring:
    def __init__(self):
        self.count = lax.axis_size("dp")
        order, self.right = ring_place(self.count)
        self.left = [(b, a) for a, b in self.right]
        self.half = self.count // 2
        place_of = [order.index(rank) for rank in range(self.count)]
        place = jnp.asarray(place_of, jnp.int32)[lax.axis_index("dp")]
        steps = jnp.arange(self.count, dtype=jnp.int32)
        self.rank_at = jnp.asarray(order, jnp.int32)[(place + steps) % self.count]
        self.sent = []
        self.added = None

    def rank(self, distance):
        return self.rank_at[distance % self.count]

    def exchange(self, blocks):
        if len(self.sent) > 2:
            blocks = tie(blocks, self.sent[-3])
        got = {}
        for side, block in blocks.items():
            got[side] = lax.ppermute(block, "dp", self.right if side > 0 else self.left)
        self.sent.append(got)
        return got


class Gather:
    def __init__(self, ring, shard, long_side):
        self.ring = ring
        self.shard = shard
        self.long_side = long_side
        self.rows, self.width = shard.shape
        self.blocks = [(shard, 0)]
        self.held = {1: shard, -1: shard}
        self.marks = []

    def step(self, after=None):
        at = len(self.marks) + 1
        sides = (1, -1) if at < self.ring.half else (self.long_side,)
        blocks = {side: self.held[side] for side in sides}
        if after is not None:
            blocks = tie(blocks, after)
        self.held = self.ring.exchange(blocks)
        self.blocks += [(self.held[side], -side * at) for side in sides]
        self.marks.append(self.held)


def run(lanes, rounds, after=None):
    for turn in range(rounds):
        for lane in lanes:
            lane.step(after if turn == 0 else None)


def reached(lanes, rounds):
    return [lane.marks[rounds - 1] for lane in lanes]


def loaded(lanes, rounds):
    return [lane.loads[rounds] for lane in lanes]


def nothing_kernel(out_ref):
    pass


def unwritten(shape, dtype):
    return pl.pallas_call(
        nothing_kernel,
        out_shape=jax.ShapeDtypeStruct(shape, dtype),
        out_specs=pl.BlockSpec(memory_space=pl.ANY),
    )()


def assemble(lanes):
    ring = lanes[0].ring
    width = lanes[0].width
    full = unwritten((sum(lane.rows for lane in lanes), width * ring.count), lanes[0].shard.dtype)
    placed, base = [], 0
    for lane in lanes:
        lane.blocks[0] = tie(lane.shard, lane.marks[0]), 0
        placed += [(index, base, block, distance) for index, (block, distance) in enumerate(lane.blocks)]
        base += lane.rows
    for _, row, block, distance in sorted(placed, key=lambda item: item[0]):
        full = lax.dynamic_update_slice(full, block, (row, ring.rank(distance) * width))
    return full


class Scatter:
    def __init__(self, ring, full, first, rows, long_side):
        self.ring = ring
        self.full = full
        self.first = first
        self.rows = rows
        self.long_side = long_side
        self.width = full.shape[1] // ring.count
        self.held = {}
        self.marks = []
        self.loads = []

    def piece(self, distance):
        column = self.ring.rank(distance) * self.width
        return lax.dynamic_slice(self.full, (self.first, column), (self.rows, self.width))

    def step(self, after=None):
        ring = self.ring
        at = ring.half - len(self.marks)
        came = self.held
        if came and ring.added is not None:
            came = tie(came, ring.added)
        sides = (1, -1) if at < ring.half else (self.long_side,)
        blocks = {}
        for side in sides:
            block = self.piece(side * at)
            if side in came:
                block = (block.astype(jnp.float32) + came[side].astype(jnp.float32)).astype(jnp.bfloat16)
            blocks[side] = block
        if came:
            ring.added = blocks
        self.loads.append(blocks)
        self.held = ring.exchange(blocks)
        self.marks.append(self.held)

    def total(self):
        own = self.piece(0).astype(jnp.float32)
        return own + self.held[1].astype(jnp.float32) + self.held[-1].astype(jnp.float32)


def halves(rows):
    cut = (rows // 2 + 15) // 16 * 16
    return [(0, cut, 1), (cut, rows - cut, -1)]


def gather_lanes(ring, shard):
    return [Gather(ring, shard[first : first + size], side) for first, size, side in halves(shard.shape[0])]


def scatter_lanes(ring, full):
    return [Scatter(ring, full, first, size, side) for first, size, side in halves(full.shape[0])]


def totals(lanes):
    return jnp.concatenate([lane.total() for lane in lanes])


def decay_rows(doc_ids, log_gamma, first, size, keys):
    query_pos = first + jnp.arange(size)
    key_pos = jnp.arange(keys)
    distance = query_pos[:, None] - key_pos[None, :]
    allowed = (doc_ids[first : first + size, None] == doc_ids[None, :keys]) & (distance >= 0)
    steps_back = jnp.maximum(distance, 0).astype(jnp.float32)
    falloff = jnp.exp(log_gamma[:, None, None] * steps_back[None])
    return jnp.where(allowed[None], falloff, 0.0)


def einsum32(spec, left, right):
    return jnp.einsum(spec, left, right, preferred_element_type=jnp.float32)


def retention_forward(query, key, value, doc_ids, log_gamma, block):
    factor = KEY_HEAD_SIZE ** (-0.5)
    pieces = []
    for first in range(0, LEN, block):
        keys = first + block
        falloff = decay_rows(doc_ids, log_gamma, first, block, keys)
        scores = einsum32("hdq,hdk->hqk", query[:, :, first:keys], key[:, :, :keys]) * factor
        weights = (scores * falloff).astype(jnp.bfloat16)
        pieces.append(einsum32("hdk,hqk->hdq", value[:, :, :keys], weights))
    return jnp.concatenate(pieces, axis=2)


def retention_backward(query, key, value, grad, doc_ids, log_gamma, block, waits):
    factor = KEY_HEAD_SIZE ** (-0.5)
    grad_query = []
    grad_key = jnp.zeros(key.shape, jnp.float32)
    grad_value = jnp.zeros(value.shape, jnp.float32)
    for first in range(0, LEN, block):
        keys = first + block
        falloff = decay_rows(doc_ids, log_gamma, first, block, keys)
        query_now, grad_now = query[:, :, first:keys], grad[:, :, first:keys]
        if waits[first // block] is not None:
            grad_now = tie(grad_now, waits[first // block])
        scores = einsum32("hdq,hdk->hqk", query_now, key[:, :, :keys]) * factor
        weights = (scores * falloff).astype(jnp.bfloat16)
        grad_weights = einsum32("hdq,hdk->hqk", grad_now, value[:, :, :keys])
        grad_scores = (grad_weights * falloff).astype(jnp.bfloat16)
        grad_query.append(einsum32("hdk,hqk->hdq", key[:, :, :keys], grad_scores) * factor)
        grad_key = grad_key.at[:, :, :keys].add(einsum32("hdq,hqk->hdk", query_now, grad_scores) * factor)
        grad_value = grad_value.at[:, :, :keys].add(einsum32("hdq,hqk->hdk", grad_now, weights))
    return jnp.concatenate(grad_query, axis=2), grad_key, grad_value


def newton_schulz_kernel(turns, step, in_ref, out_ref, cur_ref, low_ref, rest_ref, poly_ref, scale_ref):
    parts, size, cols = in_ref.shape
    width = parts * cols
    band = 256
    blocks = size // step

    def rows_of(index):
        return pl.ds(pl.multiple_of(index * step, step), step)

    def first_sum(index, total):
        rows = rows_of(index)
        for part in range(parts):
            block = in_ref[part, rows, :].astype(jnp.float32)
            total = total + jnp.sum(block * block)
        return total

    total = lax.fori_loop(0, blocks, first_sum, jnp.float32(0.0))
    scale_ref[...] = 1.0 / (jnp.sqrt(jnp.full(scale_ref.shape, total)) + 1e-07)

    @pl.loop(0, blocks)
    def _(index):
        rows = rows_of(index)
        scale = scale_ref[0, 0]
        for part in range(parts):
            block = in_ref[part, rows, :].astype(jnp.float32) * scale
            columns = pl.ds(part * cols, cols)
            cur_ref[rows, columns] = block
            low_ref[0, rows, columns] = block.astype(jnp.bfloat16)

    bands = [(first, min(256, size - first)) for first in range(0, size, 256)]

    def turn_body(turn, norm, last):
        here = lax.rem(turn, 2)
        there = 1 - here
        middle = norm * (1.0 / size)
        low = low_ref.at[here]
        for first, wide in bands:
            gram = dot(low[...], low[first : first + wide, :], 1, 1)
            place = lax.broadcasted_iota(jnp.int32, gram.shape, 0)
            eye = place == lax.broadcasted_iota(jnp.int32, gram.shape, 1) + first
            rest_ref[:, first : first + wide] = jnp.where(eye, gram - middle, gram).astype(jnp.bfloat16)
        for first, wide in bands:
            rest = rest_ref[:, first : first + wide]
            square = dot(rest_ref[...], rest, 1, 0)
            poly = (ns_second + 2.0 * ns_third * middle) * rest.astype(jnp.float32) + ns_third * square
            poly_ref[:, first : first + wide] = poly.astype(jnp.bfloat16)
        outer = ns_first + middle * (ns_second + ns_third * middle)

        total = jnp.zeros((1, band), jnp.float32)
        for first in range(0, width, band):
            columns = slice(first, first + band)
            fresh = outer * cur_ref[:, columns] + dot(poly_ref[...], low[:, columns], 1, 0)
            if last:
                out_ref[first // cols, :, first % cols : first % cols + band] = fresh.astype(jnp.bfloat16)
            else:
                cur_ref[:, columns] = fresh
                low_ref[there, :, columns] = fresh.astype(jnp.bfloat16)
                total = total + jnp.sum(fresh * fresh, axis=0, keepdims=True)
        return jnp.sum(total)

    norm = lax.fori_loop(0, turns - 1, lambda turn, norm: turn_body(turn, norm, False), jnp.float32(1.0))
    turn_body(turns - 1, norm, True)


def newton_schulz(block):
    parts, size, cols = block.shape
    width = parts * cols
    step = next(step for step in range(288, 0, -16) if size % step == 0)
    products = 2 * size * size * (2 * width + size) * NS_ITERS
    return pl.pallas_call(
        partial(newton_schulz_kernel, NS_ITERS, step),
        out_shape=jax.ShapeDtypeStruct(block.shape, jnp.bfloat16),
        in_specs=[pl.BlockSpec(memory_space=pltpu.VMEM)],
        out_specs=pl.BlockSpec(memory_space=pltpu.VMEM),
        scratch_shapes=[
            pltpu.VMEM((size, width), jnp.float32),
            pltpu.VMEM((2, size, width), jnp.bfloat16),
            pltpu.VMEM((size, size), jnp.bfloat16),
            pltpu.VMEM((size, size), jnp.bfloat16),
            pltpu.VMEM((8, 128), jnp.float32),
        ],
        compiler_params=pltpu.CompilerParams(vmem_limit_bytes=48 * 1024 * 1024),
        cost_estimate=pl.CostEstimate(flops=products, bytes_accessed=4 * size * width, transcendentals=0),
    )(block)


def orthogonalize(slabs, norm_terms, own_norms):
    ranks = lax.axis_size("dp")
    widest = max(slab.shape[0] for slab in slabs)
    cols = slabs[0].shape[1]
    padded = [jnp.pad(slab.astype(jnp.bfloat16), ((0, widest - slab.shape[0]), (0, 0))) for slab in slabs]
    each = (len(slabs) + ranks - 1) // ranks
    padded += [jnp.zeros((widest, cols), jnp.bfloat16)] * (each * ranks - len(slabs))
    stacked = jnp.stack(padded)
    owned = lax.all_to_all(stacked.reshape(ranks, each, widest, cols), "dp", 0, 0, tiled=True)
    owned, norm_terms = tie((owned, sum_tensor(norm_terms)))
    norm_grad = sum_dp(norm_terms, own_norms)
    done = []
    for index in range(each):
        mine = owned[:, index]
        if cols % 128:
            mine = jnp.moveaxis(mine, 0, 1).reshape(1, widest, ranks * cols)
        item = newton_schulz(mine)
        if cols % 128:
            item = jnp.moveaxis(item.reshape(widest, ranks, cols), 1, 0)
        done.append(item)
    ready = jnp.stack(done, axis=1)
    ready = tie(ready, norm_grad)
    returned = lax.all_to_all(ready, "dp", 0, 0, tiled=True).reshape(each * ranks, widest, cols)
    return [returned[index, : slab.shape[0]] for index, slab in enumerate(slabs)], norm_grad


def gather_small(piece, axis):
    count = lax.axis_size(axis)
    index = lax.axis_index(axis)
    held = piece
    bit = 1
    while bit < count:
        came = lax.ppermute(held, axis, [(i, i ^ bit) for i in range(count)])
        mine = (index // bit) % 2
        start = (0,) * held.ndim
        both = jnp.zeros((2,) + held.shape, held.dtype)
        both = lax.dynamic_update_slice(both, held[None], (mine,) + start)
        held = lax.dynamic_update_slice(both, came[None], (1 - mine,) + start)
        bit *= 2
    return held.reshape((count,) + piece.shape), came


def sum_tensor(terms):
    count = lax.axis_size("tensor")
    bit = 1
    while bit < count:
        terms = terms + lax.ppermute(terms, "tensor", [(i, i ^ bit) for i in range(count)])
        bit *= 2
    return terms


def sum_dp(terms, own):
    count = lax.axis_size("dp")
    group = terms.shape[0] // count
    filled = TILE * ((group + TILE - 1) // TILE)
    rows = jnp.pad(terms.reshape(count, group), ((0, 0), (0, filled - group))).reshape(-1, 128)
    mine = lax.psum_scatter(rows, "dp", scatter_dimension=0, tiled=True).reshape(-1)
    return lax.dynamic_slice_in_dim(mine, lax.axis_index("tensor") * own, own)


def per_device(
    tokens,
    cotangent,
    doc_lengths,
    key_weights,
    value_weights,
    out_weights,
    up_weights,
    down_weights,
    key_momentum,
    value_momentum,
    out_momentum,
    up_momentum,
    down_momentum,
    norm_params,
    norm_first,
    norm_second,
):
    tensor_count = lax.axis_size("tensor")
    tensor_index = lax.axis_index("tensor")
    heads = H // tensor_count
    width = tokens.shape[1]
    keys_local = key_weights.shape[2]
    values_local = value_weights.shape[2]
    hidden_local = up_weights.shape[2]
    value_total = values_local * tensor_count
    block = min(LEN, 512)
    ring = Ring()
    half = ring.half
    quarter = half // 4

    def low_t(matrix):
        return matrix.astype(jnp.bfloat16).T

    attend_lanes = gather_lanes(
        ring,
        jnp.concatenate(
            [low_t(key_weights[0]), low_t(key_weights[1]), low_t(value_weights[0]), low_t(value_weights[1])]
        ),
    )
    out_lanes = [Gather(ring, out_weights.astype(jnp.bfloat16), 1)]
    upper_lanes = gather_lanes(ring, jnp.concatenate([low_t(up_weights[0]), low_t(up_weights[1])]))
    down_lanes = [Gather(ring, down_weights.astype(jnp.bfloat16), -1)]
    tokens_all = gather_tokens(tokens)
    own_norms = norm_params.shape[0]
    filled_norms = TILE * ((own_norms + TILE - 1) // TILE)
    norm_piece = jnp.pad(norm_params, (0, filled_norms - own_norms)).reshape(filled_norms // 128, 128)
    norm_group, _ = gather_small(norm_piece, "tensor")
    attend_lanes[0].step()
    attend_lanes[1].step()
    gathered_norms, last_norms = gather_small(tie(norm_group, reached(attend_lanes[:1], 1)), "dp")
    attend_lanes[0].step(last_norms)
    attend_lanes[1].step()
    gathered_norms = gathered_norms.reshape(-1, filled_norms)[:, :own_norms].reshape(-1)

    gain_one = gathered_norms[:width]
    gain_two = gathered_norms[width : 2 * width]
    group_gain = lax.dynamic_slice_in_dim(
        gathered_norms, 2 * width + tensor_index * values_local, values_local
    )[:, None]
    group_bias = lax.dynamic_slice_in_dim(
        gathered_norms, 2 * width + value_total + tensor_index * values_local, values_local
    )[:, None]
    lengths = tie(doc_lengths[0], reached(attend_lanes, 1))
    starts_all = jnp.cumsum(lengths) - lengths
    positions = jnp.arange(LEN)
    doc_ids = jnp.sum((positions[:, None] >= starts_all[None, :]).astype(jnp.int32), axis=1) - 1

    inputs = tokens.astype(jnp.float32)
    scale_one = root_scale(inputs)
    normed_one = inputs * scale_one
    inputs_all = tokens_all.astype(jnp.float32)
    normed_all = (inputs_all * root_scale(inputs_all) * gain_one).astype(jnp.bfloat16)
    rows_total = normed_all.shape[0]
    grad_rows_two = gather_tokens(tie(cotangent, tokens_all))
    attend_lanes[0].step(normed_all)
    attend_lanes[1].step()
    run(attend_lanes, half - 3)
    run(out_lanes, quarter)
    attend_full = assemble(attend_lanes)

    gate_row = 2 * keys_local + values_local
    attend = dot(attend_full[:gate_row], normed_all, 1, 1).astype(jnp.bfloat16)
    attend = tie(attend, reached(out_lanes, quarter))
    run(out_lanes, quarter, attend)
    upper_lanes[0].step()
    query = attend[:keys_local].reshape(heads, KEY_HEAD_SIZE, rows_total)
    key = attend[keys_local : 2 * keys_local].reshape(heads, KEY_HEAD_SIZE, rows_total)
    value = attend[2 * keys_local :].reshape(heads, DV, rows_total)
    head_ids = (tensor_index * heads + jnp.arange(heads)).astype(jnp.float32)
    log_gamma = jnp.log(1.0 - jnp.exp2(-5.0 - head_ids))
    mixed_heads = retention_forward(query, key, value, doc_ids, log_gamma, block)
    mixed_heads = tie(mixed_heads, reached(out_lanes, 2 * quarter))
    run(out_lanes, quarter)
    mixed_heads = tie(mixed_heads, reached(upper_lanes[:1], 1))
    upper_lanes[1].step()
    run(out_lanes, half - 3 * quarter)
    out_full = assemble(out_lanes)
    run(upper_lanes, half - 1)
    run(down_lanes, 2 * quarter)
    upper_full = assemble(upper_lanes)
    gate_pre = dot(attend_full[gate_row:], tie(normed_all, mixed_heads), 1, 1)
    centred = mixed_heads - jnp.mean(mixed_heads, axis=1, keepdims=True)
    group_scale = lax.rsqrt(jnp.mean(centred * centred, axis=1, keepdims=True) + group_floor)
    group_hat = centred * group_scale
    group_flat = group_hat.reshape(values_local, rows_total)
    group_out = group_flat * group_gain + group_bias
    gate_act, silu_pull = jax.vjp(jax.nn.silu, gate_pre)
    mixed_low = (gate_act * group_out).astype(jnp.bfloat16)
    mixed_low, grad_rows_two = tie((mixed_low, grad_rows_two), reached(out_lanes, half))
    branch_one = scatter_tokens(dot(mixed_low, out_full, 0, 0))
    middle = inputs + tie(branch_one, reached(upper_lanes[:1], 3 * quarter), reached(upper_lanes[1:], 2 * quarter))
    scale_two = root_scale(middle)
    normed_two = middle * scale_two
    second_all = gather_tokens((normed_two * gain_two).astype(jnp.bfloat16))
    run(down_lanes, half - 2 * quarter, second_all)
    second_all = tie(second_all, reached(down_lanes, 2 * quarter))
    down_full = assemble(down_lanes)
    hidden_gate = dot(upper_full[:hidden_local], second_all, 1, 1)
    second_late = tie(second_all, hidden_gate, reached(down_lanes, 3 * quarter))
    hidden_upper = dot(upper_full[hidden_local:], second_late, 1, 1)
    gelu_gate, gelu_pull = jax.vjp(partial(jax.nn.gelu, approximate=False), hidden_gate)
    hidden_low = (gelu_gate * hidden_upper).astype(jnp.bfloat16)

    grad_result = cotangent.astype(jnp.float32)
    rows_two_late = tie(grad_rows_two, hidden_low, reached(down_lanes, half))
    grad_down = dot(hidden_low, rows_two_late, 1, 0).astype(jnp.bfloat16)
    down_back = [Scatter(ring, grad_down, 0, hidden_local, -1)]
    run(down_back, half)
    grad_hidden = dot(down_full, tie(grad_rows_two, grad_down), 1, 1)
    grad_gate_mlp = gelu_pull(grad_hidden * hidden_upper)[0].astype(jnp.bfloat16)
    grad_upper_mlp = (grad_hidden * gelu_gate).astype(jnp.bfloat16)
    grad_hidden_low = jnp.concatenate([grad_gate_mlp, grad_upper_mlp])
    grad_hidden_low = tie(grad_hidden_low, loaded(down_back, quarter))
    grad_second = dot(grad_hidden_low, upper_full, 0, 0).astype(jnp.bfloat16)
    grad_second, grad_hidden_late = tie((grad_second, grad_hidden_low))
    grad_second_local = scatter_tokens(tie(grad_second, reached(down_back, 2 * quarter)))
    grad_hidden_late = tie(grad_hidden_late, loaded(down_back, 2 * quarter))
    grad_upper = dot(grad_hidden_late, second_all, 1, 0).astype(jnp.bfloat16)
    upper_back = scatter_lanes(ring, tie(grad_upper, reached(down_back, 3 * quarter)))
    run(upper_back, half)
    grad_second_local = tie(grad_second_local, reached(upper_back[:1], 2 * quarter), loaded(upper_back[1:], quarter))
    grad_gain_two = jnp.sum(grad_second_local * normed_two, axis=0)
    grad_middle = grad_result + norm_back(grad_second_local * gain_two, normed_two, scale_two)
    grad_rows_one = gather_tokens(grad_middle.astype(jnp.bfloat16))
    grad_rows_one = tie(grad_rows_one, loaded(upper_back, 3 * quarter))
    out_back = [Scatter(ring, dot(mixed_low, grad_rows_one, 1, 0).astype(jnp.bfloat16), 0, values_local, 1)]
    run(out_back, quarter)
    grad_mixed = dot(out_full, tie(grad_rows_one, loaded(out_back, 0)), 1, 1)
    grad_gate_low = silu_pull(grad_mixed * group_out)[0].astype(jnp.bfloat16)
    gate_back = [Scatter(ring, dot(grad_gate_low, normed_all, 1, 0).astype(jnp.bfloat16), 0, values_local, -1)]
    run(gate_back, quarter)
    run(out_back + gate_back, half - quarter)
    grad_group = grad_mixed * gate_act
    grad_group_gain = jnp.sum(grad_group * group_flat, axis=1)
    grad_group_bias = jnp.sum(grad_group, axis=1)
    grad_hat = (grad_group * group_gain).reshape(heads, DV, rows_total)
    grad_heads = group_scale * (
        grad_hat
        - jnp.mean(grad_hat, axis=1, keepdims=True)
        - group_hat * jnp.mean(grad_hat * group_hat, axis=1, keepdims=True)
    )
    grad_heads = tie(grad_heads, loaded(out_back, quarter), loaded(gate_back, 0))
    waits = [None, (loaded(out_back, 2 * quarter), loaded(gate_back, quarter))]
    grad_queries, grad_keys, grad_values = retention_backward(
        query, key, value, grad_heads.astype(jnp.bfloat16), doc_ids, log_gamma, block, waits
    )
    grad_attend_low = jnp.concatenate(
        [
            grad_queries.astype(jnp.bfloat16).reshape(keys_local, rows_total),
            grad_keys.astype(jnp.bfloat16).reshape(keys_local, rows_total),
            grad_values.astype(jnp.bfloat16).reshape(values_local, rows_total),
        ]
    )
    grad_attend_low = tie(grad_attend_low, loaded(out_back, 3 * quarter))
    grad_attend = dot(grad_attend_low, normed_all, 1, 0).astype(jnp.bfloat16)
    attend_back = scatter_lanes(ring, grad_attend)
    run(attend_back, half)
    pieces = []
    for index in range(4):
        lane = attend_back[index % 2]
        rows = slice(index * rows_total // 4, (index + 1) * rows_total // 4)
        late, gate_late = tie((grad_attend_low[:, rows], grad_gate_low[:, rows]), loaded([lane], (1 + index // 2) * quarter))
        piece = dot(late, attend_full[:gate_row], 0, 0) + dot(gate_late, attend_full[gate_row:], 0, 0)
        pieces.append(piece.astype(jnp.bfloat16))
    grad_first = jnp.concatenate(pieces)
    grad_first_local = scatter_tokens(grad_first)
    branch_two = scatter_tokens(dot(tie(hidden_low, grad_first), down_full, 0, 0))
    result = middle + branch_two
    grad_gain_one = jnp.sum(grad_first_local * normed_one, axis=0)
    token_grad = grad_middle + norm_back(grad_first_local * gain_one, normed_one, scale_one)
    group_part = jnp.zeros((2, value_total), jnp.float32)
    group_part = lax.dynamic_update_slice_in_dim(
        group_part, jnp.stack([grad_group_gain, grad_group_bias]), tensor_index * values_local, 1
    )
    norm_terms = jnp.concatenate([grad_gain_one, grad_gain_two, group_part.reshape(-1)])
    grad_down_w = totals(down_back)
    grad_upper_w = totals(upper_back)
    grad_out_w = totals(out_back)
    grad_gate_w = totals(gate_back)
    grad_attend_w = totals(attend_back)

    fresh_query = momentum_decay * key_momentum[0] + grad_attend_w[:keys_local].T
    fresh_key = momentum_decay * key_momentum[1] + grad_attend_w[keys_local : 2 * keys_local].T
    fresh_value = momentum_decay * value_momentum[0] + grad_attend_w[2 * keys_local :].T
    fresh_gate = momentum_decay * value_momentum[1] + grad_gate_w.T
    fresh_out = momentum_decay * out_momentum + grad_out_w
    fresh_hidden = momentum_decay * up_momentum[0] + grad_upper_w[:hidden_local].T
    fresh_upper = momentum_decay * up_momentum[1] + grad_upper_w[hidden_local:].T
    fresh_down = momentum_decay * down_momentum + grad_down_w
    orth, norm_grad = orthogonalize(
        [
            fresh_down,
            fresh_hidden.T,
            fresh_upper.T,
            fresh_out,
            fresh_gate.T,
            fresh_value.T,
            fresh_query.T,
            fresh_key.T,
        ],
        norm_terms,
        own_norms,
    )
    orth = [item.astype(jnp.float32) for item in orth]
    keep_factor = 1.0 - muon_rate * weight_decay

    def rate(rows, cols):
        return muon_rate * math.sqrt(max(1.0, rows / cols))

    new_key_weights = key_weights * keep_factor - rate(width, keys_local) * jnp.stack([orth[6].T, orth[7].T])
    new_value_weights = value_weights * keep_factor - rate(width, values_local) * jnp.stack([orth[5].T, orth[4].T])
    new_upper_weights = up_weights * keep_factor - rate(width, hidden_local) * jnp.stack([orth[1].T, orth[2].T])
    new_out_weights = out_weights * keep_factor - rate(values_local, width) * orth[3]
    new_down_weights = down_weights * keep_factor - rate(hidden_local, width) * orth[0]
    new_norm_first = beta_first * norm_first + (1.0 - beta_first) * norm_grad
    new_norm_second = beta_second * norm_second + (1.0 - beta_second) * norm_grad * norm_grad
    fix_first = 1.0 - beta_first**STEP
    fix_second = 1.0 - beta_second**STEP
    new_norm_params = norm_params - adam_rate * (new_norm_first / fix_first) / (
        jnp.sqrt(new_norm_second / fix_second) + adam_eps
    )
    return (
        result.astype(jnp.bfloat16),
        token_grad,
        jnp.stack([fresh_query, fresh_key]),
        jnp.stack([fresh_value, fresh_gate]),
        fresh_out,
        jnp.stack([fresh_hidden, fresh_upper]),
        fresh_down,
        new_key_weights,
        new_value_weights,
        new_out_weights,
        new_upper_weights,
        new_down_weights,
        new_norm_first,
        new_norm_second,
        new_norm_params,
    )


def solution(mesh):
    tokens = P(("dp", "tensor"), None)
    wide = P(None, "dp", "tensor")
    tall = P("tensor", "dp")
    norms = P(("dp", "tensor"))
    return jax.shard_map(
        per_device,
        mesh=mesh,
        in_specs=(
            tokens, tokens, P("dp", None), wide, wide, tall, wide, tall,
            wide, wide, tall, wide, tall, norms, norms, norms,
        ),
        out_specs=(
            tokens, tokens, wide, wide, tall, wide, tall,
            wide, wide, tall, wide, tall, norms, norms, norms,
        ),
        check_vma=False,
    )
```

```python
from functools import partial
import math

import jax
import jax.numpy as jnp
from jax import lax
from jax.experimental import pallas as pl
from jax.experimental.pallas import tpu as pltpu
from jax.sharding import PartitionSpec as P

H = 8
KEY_HEAD_SIZE = 256
DV = 432
LEN = 1024
NS_ITERS = 5
STEP = 10


eps_norm = 1e-05
group_floor = 1.0
ns_first = 3.4445
ns_second = -4.775
ns_third = 2.0315
momentum_decay = 0.95
muon_rate = 0.5
weight_decay = 0.1
beta_first = 0.9
beta_second = 0.95
adam_rate = 0.8
adam_eps = 1e-08
TILE = 1024


def root_scale(values):
    return lax.rsqrt(jnp.mean(values * values, axis=-1, keepdims=True) + eps_norm)


def norm_back(grad_normed, normed, scaling):
    return scaling * (grad_normed - normed * jnp.mean(grad_normed * normed, axis=-1, keepdims=True))


def dot(left, right, left_dim, right_dim):
    return lax.dot_general(
        left, right, (((left_dim,), (right_dim,)), ((), ())), preferred_element_type=jnp.float32
    )


def gather_tokens(values):
    return lax.all_gather(values, "tensor", axis=0, tiled=True)


def scatter_tokens(values):
    return lax.psum_scatter(
        values.astype(jnp.bfloat16), "tensor", scatter_dimension=0, tiled=True
    ).astype(jnp.float32)


def ring_order(count):
    return list(range(0, count, 2)) + list(range(count - 1, 0, -2))


def ring_place(count):
    order = ring_order(count)
    return order, [(order[i], order[(i + 1) % count]) for i in range(count)]


def tie(value, *others):
    return lax.optimization_barrier((value, others))[0]


class Ring:
    def __init__(self):
        self.count = lax.axis_size("dp")
        order, self.right = ring_place(self.count)
        self.left = [(b, a) for a, b in self.right]
        self.half = self.count // 2
        place_of = [order.index(rank) for rank in range(self.count)]
        place = jnp.asarray(place_of, jnp.int32)[lax.axis_index("dp")]
        steps = jnp.arange(self.count, dtype=jnp.int32)
        self.rank_at = jnp.asarray(order, jnp.int32)[(place + steps) % self.count]
        self.sent = []
        self.added = None

    def rank(self, distance):
        return self.rank_at[distance % self.count]

    def exchange(self, blocks):
        if len(self.sent) > 2:
            blocks = tie(blocks, self.sent[-3])
        got = {}
        for side, block in blocks.items():
            got[side] = lax.ppermute(block, "dp", self.right if side > 0 else self.left)
        self.sent.append(got)
        return got


class Gather:
    def __init__(self, ring, shard, long_side):
        self.ring = ring
        self.shard = shard
        self.long_side = long_side
        self.rows, self.width = shard.shape
        self.blocks = [(shard, 0)]
        self.held = {1: shard, -1: shard}
        self.marks = []

    def step(self, after=None):
        at = len(self.marks) + 1
        sides = (1, -1) if at < self.ring.half else (self.long_side,)
        blocks = {side: self.held[side] for side in sides}
        if after is not None:
            blocks = tie(blocks, after)
        self.held = self.ring.exchange(blocks)
        self.blocks += [(self.held[side], -side * at) for side in sides]
        self.marks.append(self.held)


def run(lanes, rounds, after=None):
    for turn in range(rounds):
        for lane in lanes:
            lane.step(after if turn == 0 else None)


def reached(lanes, rounds):
    return [lane.marks[rounds - 1] for lane in lanes]


def loaded(lanes, rounds):
    return [lane.loads[rounds] for lane in lanes]


def nothing_kernel(out_ref):
    pass


def unwritten(shape, dtype):
    return pl.pallas_call(
        nothing_kernel,
        out_shape=jax.ShapeDtypeStruct(shape, dtype),
        out_specs=pl.BlockSpec(memory_space=pl.ANY),
    )()


def assemble(lanes, delayed=False):
    ring = lanes[0].ring
    width = lanes[0].width
    full = unwritten((sum(lane.rows for lane in lanes), width * ring.count), lanes[0].shard.dtype)
    placed, base = [], 0
    for lane in lanes:
        for index in range(3 if delayed else 1):
            block, distance = lane.blocks[index]
            lane.blocks[index] = tie(block, lane.marks[1 if delayed else 0]), distance
        placed += [(index, base, block, distance) for index, (block, distance) in enumerate(lane.blocks)]
        base += lane.rows
    for _, row, block, distance in sorted(placed, key=lambda item: item[0]):
        full = lax.dynamic_update_slice(full, block, (row, ring.rank(distance) * width))
    return full


class Scatter:
    def __init__(self, ring, full, first, rows, long_side):
        self.ring = ring
        self.full = full
        self.first = first
        self.rows = rows
        self.long_side = long_side
        self.width = full.shape[1] // ring.count
        self.held = {}
        self.marks = []
        self.loads = []

    def piece(self, distance):
        column = self.ring.rank(distance) * self.width
        return lax.dynamic_slice(self.full, (self.first, column), (self.rows, self.width))

    def step(self, after=None):
        ring = self.ring
        at = ring.half - len(self.marks)
        came = self.held
        if came and ring.added is not None:
            came = tie(came, ring.added)
        sides = (1, -1) if at < ring.half else (self.long_side,)
        blocks = {}
        for side in sides:
            block = self.piece(side * at)
            if side in came:
                block = (block.astype(jnp.float32) + came[side].astype(jnp.float32)).astype(jnp.bfloat16)
            blocks[side] = block
        if came:
            ring.added = blocks
        self.loads.append(blocks)
        self.held = ring.exchange(blocks)
        self.marks.append(self.held)

    def total(self):
        own = self.piece(0).astype(jnp.float32)
        return own + self.held[1].astype(jnp.float32) + self.held[-1].astype(jnp.float32)


def halves(rows):
    cut = (rows // 2 + 15) // 16 * 16
    return [(0, cut, 1), (cut, rows - cut, -1)]


def gather_lanes(ring, shard):
    return [Gather(ring, shard[first : first + size], side) for first, size, side in halves(shard.shape[0])]


def scatter_lanes(ring, full):
    return [Scatter(ring, full, first, size, side) for first, size, side in halves(full.shape[0])]


def totals(lanes):
    return jnp.concatenate([lane.total() for lane in lanes])


def decay_rows(doc_ids, log_gamma, first, size, keys):
    query_pos = first + jnp.arange(size)
    key_pos = jnp.arange(keys)
    distance = query_pos[:, None] - key_pos[None, :]
    allowed = (doc_ids[first : first + size, None] == doc_ids[None, :keys]) & (distance >= 0)
    steps_back = jnp.maximum(distance, 0).astype(jnp.float32)
    falloff = jnp.exp(log_gamma[:, None, None] * steps_back[None])
    return jnp.where(allowed[None], falloff, 0.0)


def einsum32(spec, left, right):
    return jnp.einsum(spec, left, right, preferred_element_type=jnp.float32)


def retention_forward(query, key, value, doc_ids, log_gamma, block):
    factor = KEY_HEAD_SIZE ** (-0.5)
    pieces = []
    for first in range(0, LEN, block):
        keys = first + block
        falloff = decay_rows(doc_ids, log_gamma, first, block, keys)
        scores = einsum32("hdq,hdk->hqk", query[:, :, first:keys], key[:, :, :keys]) * factor
        weights = (scores * falloff).astype(jnp.bfloat16)
        pieces.append(einsum32("hdk,hqk->hdq", value[:, :, :keys], weights))
    return jnp.concatenate(pieces, axis=2)


def retention_backward(query, key, value, grad, doc_ids, log_gamma, block, waits):
    factor = KEY_HEAD_SIZE ** (-0.5)
    grad_query = []
    grad_key = jnp.zeros(key.shape, jnp.float32)
    grad_value = jnp.zeros(value.shape, jnp.float32)
    for first in range(0, LEN, block):
        keys = first + block
        falloff = decay_rows(doc_ids, log_gamma, first, block, keys)
        query_now, grad_now = query[:, :, first:keys], grad[:, :, first:keys]
        if waits[first // block] is not None:
            grad_now = tie(grad_now, waits[first // block])
        scores = einsum32("hdq,hdk->hqk", query_now, key[:, :, :keys]) * factor
        weights = (scores * falloff).astype(jnp.bfloat16)
        grad_weights = einsum32("hdq,hdk->hqk", grad_now, value[:, :, :keys])
        grad_scores = (grad_weights * falloff).astype(jnp.bfloat16)
        grad_query.append(einsum32("hdk,hqk->hdq", key[:, :, :keys], grad_scores) * factor)
        grad_key = grad_key.at[:, :, :keys].add(einsum32("hdq,hqk->hdk", query_now, grad_scores) * factor)
        grad_value = grad_value.at[:, :, :keys].add(einsum32("hdq,hqk->hdk", grad_now, weights))
    return jnp.concatenate(grad_query, axis=2), grad_key, grad_value


def mirror(ref, block, first, wide):
    ref[first:, first : first + wide] = block
    if block.shape[0] > wide:
        ref[first : first + wide, first + wide :] = block[wide:].T


def newton_schulz_kernel(turns, step, in_ref, out_ref, cur_ref, low_ref, rest_ref, poly_ref, scale_ref):
    parts, size, cols = in_ref.shape
    width = parts * cols
    band = 256
    blocks = size // step

    def rows_of(index):
        return pl.ds(pl.multiple_of(index * step, step), step)

    def first_sum(index, total):
        rows = rows_of(index)
        for part in range(parts):
            block = in_ref[part, rows, :].astype(jnp.float32)
            total = total + jnp.sum(block * block)
        return total

    total = lax.fori_loop(0, blocks, first_sum, jnp.float32(0.0))
    scale_ref[...] = 1.0 / (jnp.sqrt(jnp.full(scale_ref.shape, total)) + 1e-07)

    @pl.loop(0, blocks)
    def _(index):
        rows = rows_of(index)
        scale = scale_ref[0, 0]
        for part in range(parts):
            block = in_ref[part, rows, :].astype(jnp.float32) * scale
            columns = pl.ds(part * cols, cols)
            cur_ref[rows, columns] = block
            low_ref[0, rows, columns] = block.astype(jnp.bfloat16)

    bands = [(first, min(256, size - first)) for first in range(0, size, 256)]

    def turn_body(turn, norm, last):
        here = lax.rem(turn, 2)
        there = 1 - here
        middle = norm * (1.0 / size)
        low = low_ref.at[here]
        for first, wide in bands:
            gram = dot(low[first:, :], low[first : first + wide, :], 1, 1)
            place = lax.broadcasted_iota(jnp.int32, gram.shape, 0)
            eye = place == lax.broadcasted_iota(jnp.int32, gram.shape, 1)
            mirror(rest_ref, jnp.where(eye, gram - middle, gram).astype(jnp.bfloat16), first, wide)
        for first, wide in bands:
            square = dot(rest_ref[first:, :], rest_ref[:, first : first + wide], 1, 0)
            rest = rest_ref[first:, first : first + wide].astype(jnp.float32)
            poly = (ns_second + 2.0 * ns_third * middle) * rest + ns_third * square
            mirror(poly_ref, poly.astype(jnp.bfloat16), first, wide)
        outer = ns_first + middle * (ns_second + ns_third * middle)

        total = jnp.zeros((1, band), jnp.float32)
        for first in range(0, width, band):
            columns = slice(first, first + band)
            fresh = outer * cur_ref[:, columns] + dot(poly_ref[...], low[:, columns], 1, 0)
            if last:
                out_ref[first // cols, :, first % cols : first % cols + band] = fresh.astype(jnp.bfloat16)
            else:
                cur_ref[:, columns] = fresh
                low_ref[there, :, columns] = fresh.astype(jnp.bfloat16)
                total = total + jnp.sum(fresh * fresh, axis=0, keepdims=True)
        return jnp.sum(total)

    norm = lax.fori_loop(0, turns - 1, lambda turn, norm: turn_body(turn, norm, False), jnp.float32(1.0))
    turn_body(turns - 1, norm, True)


def newton_schulz(block):
    parts, size, cols = block.shape
    width = parts * cols
    step = next(step for step in range(288, 0, -16) if size % step == 0)
    products = 2 * size * size * (2 * width + size) * NS_ITERS
    return pl.pallas_call(
        partial(newton_schulz_kernel, NS_ITERS, step),
        out_shape=jax.ShapeDtypeStruct(block.shape, jnp.bfloat16),
        in_specs=[pl.BlockSpec(memory_space=pltpu.VMEM)],
        out_specs=pl.BlockSpec(memory_space=pltpu.VMEM),
        scratch_shapes=[
            pltpu.VMEM((size, width), jnp.float32),
            pltpu.VMEM((2, size, width), jnp.bfloat16),
            pltpu.VMEM((size, size), jnp.bfloat16),
            pltpu.VMEM((size, size), jnp.bfloat16),
            pltpu.VMEM((8, 128), jnp.float32),
        ],
        compiler_params=pltpu.CompilerParams(vmem_limit_bytes=48 * 1024 * 1024),
        cost_estimate=pl.CostEstimate(flops=products, bytes_accessed=4 * size * width, transcendentals=0),
    )(block)


def orthogonalize(slabs, norm_terms, own_norms):
    ranks = lax.axis_size("dp")
    widest = max(slab.shape[0] for slab in slabs)
    cols = slabs[0].shape[1]
    padded = [jnp.pad(slab.astype(jnp.bfloat16), ((0, widest - slab.shape[0]), (0, 0))) for slab in slabs]
    each = (len(slabs) + ranks - 1) // ranks
    padded += [jnp.zeros((widest, cols), jnp.bfloat16)] * (each * ranks - len(slabs))
    stacked = jnp.stack(padded)
    owned = lax.all_to_all(stacked.reshape(ranks, each, widest, cols), "dp", 0, 0, tiled=True)
    owned, norm_terms = tie((owned, sum_tensor(norm_terms)))
    norm_grad = sum_dp(norm_terms, own_norms)
    done = []
    for index in range(each):
        mine = owned[:, index]
        if cols % 128:
            mine = jnp.moveaxis(mine, 0, 1).reshape(1, widest, ranks * cols)
        item = newton_schulz(mine)
        if cols % 128:
            item = jnp.moveaxis(item.reshape(widest, ranks, cols), 1, 0)
        done.append(item)
    ready = jnp.stack(done, axis=1)
    ready = tie(ready, norm_grad)
    returned = lax.all_to_all(ready, "dp", 0, 0, tiled=True).reshape(each * ranks, widest, cols)
    return [returned[index, : slab.shape[0]] for index, slab in enumerate(slabs)], norm_grad


def gather_small(piece, axis):
    count = lax.axis_size(axis)
    index = lax.axis_index(axis)
    held = piece
    bit = 1
    while bit < count:
        came = lax.ppermute(held, axis, [(i, i ^ bit) for i in range(count)])
        mine = (index // bit) % 2
        start = (0,) * held.ndim
        both = jnp.zeros((2,) + held.shape, held.dtype)
        both = lax.dynamic_update_slice(both, held[None], (mine,) + start)
        held = lax.dynamic_update_slice(both, came[None], (1 - mine,) + start)
        bit *= 2
    return held.reshape((count,) + piece.shape), came


def sum_tensor(terms):
    count = lax.axis_size("tensor")
    bit = 1
    while bit < count:
        terms = terms + lax.ppermute(terms, "tensor", [(i, i ^ bit) for i in range(count)])
        bit *= 2
    return terms


def sum_dp(terms, own):
    count = lax.axis_size("dp")
    group = terms.shape[0] // count
    filled = TILE * ((group + TILE - 1) // TILE)
    rows = jnp.pad(terms.reshape(count, group), ((0, 0), (0, filled - group))).reshape(-1, 128)
    mine = lax.psum_scatter(rows, "dp", scatter_dimension=0, tiled=True).reshape(-1)
    return lax.dynamic_slice_in_dim(mine, lax.axis_index("tensor") * own, own)


def per_device(
    tokens,
    cotangent,
    doc_lengths,
    key_weights,
    value_weights,
    out_weights,
    up_weights,
    down_weights,
    key_momentum,
    value_momentum,
    out_momentum,
    up_momentum,
    down_momentum,
    norm_params,
    norm_first,
    norm_second,
):
    tensor_count = lax.axis_size("tensor")
    tensor_index = lax.axis_index("tensor")
    heads = H // tensor_count
    width = tokens.shape[1]
    keys_local = key_weights.shape[2]
    values_local = value_weights.shape[2]
    hidden_local = up_weights.shape[2]
    value_total = values_local * tensor_count
    block = min(LEN, 512)
    ring = Ring()
    half = ring.half
    quarter = half // 4

    def low_t(matrix):
        return matrix.astype(jnp.bfloat16).T

    attend_lanes = gather_lanes(
        ring,
        jnp.concatenate(
            [low_t(key_weights[0]), low_t(key_weights[1]), low_t(value_weights[0]), low_t(value_weights[1])]
        ),
    )
    out_lanes = [Gather(ring, out_weights.astype(jnp.bfloat16), 1)]
    upper_lanes = gather_lanes(ring, jnp.concatenate([low_t(up_weights[0]), low_t(up_weights[1])]))
    down_lanes = [Gather(ring, down_weights.astype(jnp.bfloat16), -1)]
    tokens_all = gather_tokens(tokens)
    own_norms = norm_params.shape[0]
    filled_norms = TILE * ((own_norms + TILE - 1) // TILE)
    norm_piece = jnp.pad(norm_params, (0, filled_norms - own_norms)).reshape(filled_norms // 128, 128)
    norm_group, _ = gather_small(norm_piece, "tensor")
    attend_lanes[0].step()
    attend_lanes[1].step()
    gathered_norms, last_norms = gather_small(tie(norm_group, reached(attend_lanes[:1], 1)), "dp")
    attend_lanes[0].step(last_norms)
    attend_lanes[1].step()
    gathered_norms = gathered_norms.reshape(-1, filled_norms)[:, :own_norms].reshape(-1)

    gain_one = gathered_norms[:width]
    gain_two = gathered_norms[width : 2 * width]
    group_gain = lax.dynamic_slice_in_dim(
        gathered_norms, 2 * width + tensor_index * values_local, values_local
    )[:, None]
    group_bias = lax.dynamic_slice_in_dim(
        gathered_norms, 2 * width + value_total + tensor_index * values_local, values_local
    )[:, None]
    lengths = tie(doc_lengths[0], reached(attend_lanes, 1))
    starts_all = jnp.cumsum(lengths) - lengths
    positions = jnp.arange(LEN)
    doc_ids = jnp.sum((positions[:, None] >= starts_all[None, :]).astype(jnp.int32), axis=1) - 1

    inputs = tokens.astype(jnp.float32)
    scale_one = root_scale(inputs)
    normed_one = inputs * scale_one
    inputs_all = tokens_all.astype(jnp.float32)
    normed_all = (inputs_all * root_scale(inputs_all) * gain_one).astype(jnp.bfloat16)
    rows_total = normed_all.shape[0]
    grad_rows_two = gather_tokens(tie(cotangent, tokens_all))
    attend_lanes[0].step(normed_all)
    attend_lanes[1].step()
    run(attend_lanes, half - 3)
    run(out_lanes, quarter)
    attend_full = assemble(attend_lanes, True)

    gate_row = 2 * keys_local + values_local
    attend = dot(attend_full[:gate_row], normed_all, 1, 1).astype(jnp.bfloat16)
    attend = tie(attend, reached(out_lanes, quarter))
    run(out_lanes, quarter, attend)
    upper_lanes[0].step()
    query = attend[:keys_local].reshape(heads, KEY_HEAD_SIZE, rows_total)
    key = attend[keys_local : 2 * keys_local].reshape(heads, KEY_HEAD_SIZE, rows_total)
    value = attend[2 * keys_local :].reshape(heads, DV, rows_total)
    head_ids = (tensor_index * heads + jnp.arange(heads)).astype(jnp.float32)
    log_gamma = jnp.log(1.0 - jnp.exp2(-5.0 - head_ids))
    mixed_heads = retention_forward(query, key, value, doc_ids, log_gamma, block)
    mixed_heads = tie(mixed_heads, reached(out_lanes, 2 * quarter))
    run(out_lanes, quarter)
    upper_lanes[1].step()
    run(out_lanes, half - 3 * quarter)
    out_full = assemble(out_lanes)
    run(upper_lanes, half - 1)
    run(down_lanes, 2 * quarter)
    upper_full = assemble(upper_lanes)
    gate_pre = dot(attend_full[gate_row:], tie(normed_all, mixed_heads), 1, 1)
    centred = mixed_heads - jnp.mean(mixed_heads, axis=1, keepdims=True)
    group_scale = lax.rsqrt(jnp.mean(centred * centred, axis=1, keepdims=True) + group_floor)
    group_hat = centred * group_scale
    group_flat = group_hat.reshape(values_local, rows_total)
    group_out = group_flat * group_gain + group_bias
    gate_act, silu_pull = jax.vjp(jax.nn.silu, gate_pre)
    mixed_low = (gate_act * group_out).astype(jnp.bfloat16)
    mixed_low, grad_rows_two = tie((mixed_low, grad_rows_two), reached(out_lanes, half), reached(upper_lanes[:1], 1))
    branch_one = scatter_tokens(dot(mixed_low, out_full, 0, 0))
    middle = inputs + tie(branch_one, reached(upper_lanes, half))
    scale_two = root_scale(middle)
    normed_two = middle * scale_two
    second_all = gather_tokens((normed_two * gain_two).astype(jnp.bfloat16))
    run(down_lanes, half - 2 * quarter, second_all)
    second_all = tie(second_all, reached(down_lanes, 2 * quarter))
    down_full = assemble(down_lanes)
    hidden_gate = dot(upper_full[:hidden_local], second_all, 1, 1)
    second_late = tie(second_all, hidden_gate, reached(down_lanes, 3 * quarter))
    hidden_upper = dot(upper_full[hidden_local:], second_late, 1, 1)
    gelu_gate, gelu_pull = jax.vjp(partial(jax.nn.gelu, approximate=False), hidden_gate)
    hidden_low = (gelu_gate * hidden_upper).astype(jnp.bfloat16)

    grad_result = cotangent.astype(jnp.float32)
    rows_two_late = tie(grad_rows_two, hidden_low, reached(down_lanes, half))
    grad_down = dot(hidden_low, rows_two_late, 1, 0).astype(jnp.bfloat16)
    down_back = [Scatter(ring, grad_down, 0, hidden_local, -1)]
    run(down_back, half)
    grad_hidden = dot(down_full, tie(grad_rows_two, grad_down), 1, 1)
    grad_gate_mlp = gelu_pull(grad_hidden * hidden_upper)[0].astype(jnp.bfloat16)
    grad_upper_mlp = (grad_hidden * gelu_gate).astype(jnp.bfloat16)
    grad_hidden_low = jnp.concatenate([grad_gate_mlp, grad_upper_mlp])
    grad_hidden_low = tie(grad_hidden_low, loaded(down_back, quarter))
    grad_second = dot(grad_hidden_low, upper_full, 0, 0).astype(jnp.bfloat16)
    grad_second, grad_hidden_late = tie((grad_second, grad_hidden_low))
    grad_second_local = scatter_tokens(tie(grad_second, reached(down_back, 2 * quarter)))
    grad_hidden_late = tie(grad_hidden_late, loaded(down_back, 2 * quarter))
    grad_upper = dot(grad_hidden_late, second_all, 1, 0).astype(jnp.bfloat16)
    upper_back = scatter_lanes(ring, tie(grad_upper, reached(down_back, 3 * quarter)))
    run(upper_back, half)
    grad_second_local = tie(grad_second_local, reached(upper_back[:1], 2 * quarter), loaded(upper_back[1:], quarter))
    grad_gain_two = jnp.sum(grad_second_local * normed_two, axis=0)
    grad_middle = grad_result + norm_back(grad_second_local * gain_two, normed_two, scale_two)
    grad_middle_low = grad_middle.astype(jnp.bfloat16)
    grad_rows_one = gather_tokens(grad_middle_low)
    branch_two = dot(tie(hidden_low, grad_middle_low), down_full, 0, 0).astype(jnp.bfloat16)
    grad_rows_one = tie(grad_rows_one, branch_two)
    result = middle + scatter_tokens(tie(branch_two, grad_rows_one))
    grad_rows_one = tie(grad_rows_one, loaded(upper_back, 3 * quarter))
    out_back = [Scatter(ring, dot(mixed_low, grad_rows_one, 1, 0).astype(jnp.bfloat16), 0, values_local, 1)]
    run(out_back, quarter)
    grad_mixed = dot(out_full, tie(grad_rows_one, loaded(out_back, 0)), 1, 1)
    grad_gate_low = silu_pull(grad_mixed * group_out)[0].astype(jnp.bfloat16)
    gate_back = [Scatter(ring, dot(grad_gate_low, normed_all, 1, 0).astype(jnp.bfloat16), 0, values_local, -1)]
    run(gate_back, quarter)
    run(out_back + gate_back, half - quarter)
    grad_group = grad_mixed * gate_act
    grad_group_gain = jnp.sum(grad_group * group_flat, axis=1)
    grad_group_bias = jnp.sum(grad_group, axis=1)
    grad_hat = (grad_group * group_gain).reshape(heads, DV, rows_total)
    grad_heads = group_scale * (
        grad_hat
        - jnp.mean(grad_hat, axis=1, keepdims=True)
        - group_hat * jnp.mean(grad_hat * group_hat, axis=1, keepdims=True)
    )
    grad_heads = tie(grad_heads, loaded(out_back, quarter), loaded(gate_back, 0))
    waits = [None, (loaded(out_back, 2 * quarter), loaded(gate_back, quarter))]
    grad_queries, grad_keys, grad_values = retention_backward(
        query, key, value, grad_heads.astype(jnp.bfloat16), doc_ids, log_gamma, block, waits
    )
    grad_attend_low = jnp.concatenate(
        [
            grad_queries.astype(jnp.bfloat16).reshape(keys_local, rows_total),
            grad_keys.astype(jnp.bfloat16).reshape(keys_local, rows_total),
            grad_values.astype(jnp.bfloat16).reshape(values_local, rows_total),
        ]
    )
    grad_attend_low = tie(grad_attend_low, loaded(out_back, 3 * quarter))
    grad_attend = dot(grad_attend_low, normed_all, 1, 0).astype(jnp.bfloat16)
    attend_back = scatter_lanes(ring, grad_attend)
    run(attend_back, half)
    pieces = []
    for index in range(4):
        rows = slice(index * rows_total // 4, (index + 1) * rows_total // 4)
        marker = loaded([attend_back[(0, 1, 0, 0)[index]]], (1, 1, 2, 2)[index] * quarter)
        late, gate_late = tie((grad_attend_low[:, rows], grad_gate_low[:, rows]), marker)
        piece = dot(late, attend_full[:gate_row], 0, 0) + dot(gate_late, attend_full[gate_row:], 0, 0)
        pieces.append(piece.astype(jnp.bfloat16))
    grad_first = jnp.concatenate(pieces)
    grad_first_local = scatter_tokens(grad_first)
    grad_gain_one = jnp.sum(grad_first_local * normed_one, axis=0)
    token_grad = grad_middle + norm_back(grad_first_local * gain_one, normed_one, scale_one)
    group_part = jnp.zeros((2, value_total), jnp.float32)
    group_part = lax.dynamic_update_slice_in_dim(
        group_part, jnp.stack([grad_group_gain, grad_group_bias]), tensor_index * values_local, 1
    )
    norm_terms = jnp.concatenate([grad_gain_one, grad_gain_two, group_part.reshape(-1)])
    grad_down_w = totals(down_back)
    grad_upper_w = totals(upper_back)
    grad_out_w = totals(out_back)
    grad_gate_w = totals(gate_back)
    grad_attend_w = totals(attend_back)

    fresh_query = momentum_decay * key_momentum[0] + grad_attend_w[:keys_local].T
    fresh_key = momentum_decay * key_momentum[1] + grad_attend_w[keys_local : 2 * keys_local].T
    fresh_value = momentum_decay * value_momentum[0] + grad_attend_w[2 * keys_local :].T
    fresh_gate = momentum_decay * value_momentum[1] + grad_gate_w.T
    fresh_out = momentum_decay * out_momentum + grad_out_w
    fresh_hidden = momentum_decay * up_momentum[0] + grad_upper_w[:hidden_local].T
    fresh_upper = momentum_decay * up_momentum[1] + grad_upper_w[hidden_local:].T
    fresh_down = momentum_decay * down_momentum + grad_down_w
    orth, norm_grad = orthogonalize(
        [
            fresh_down,
            fresh_hidden.T,
            fresh_upper.T,
            fresh_out,
            fresh_gate.T,
            fresh_value.T,
            fresh_query.T,
            fresh_key.T,
        ],
        norm_terms,
        own_norms,
    )
    orth = [item.astype(jnp.float32) for item in orth]
    keep_factor = 1.0 - muon_rate * weight_decay

    def rate(rows, cols):
        return muon_rate * math.sqrt(max(1.0, rows / cols))

    new_key_weights = key_weights * keep_factor - rate(width, keys_local) * jnp.stack([orth[6].T, orth[7].T])
    new_value_weights = value_weights * keep_factor - rate(width, values_local) * jnp.stack([orth[5].T, orth[4].T])
    new_upper_weights = up_weights * keep_factor - rate(width, hidden_local) * jnp.stack([orth[1].T, orth[2].T])
    new_out_weights = out_weights * keep_factor - rate(values_local, width) * orth[3]
    new_down_weights = down_weights * keep_factor - rate(hidden_local, width) * orth[0]
    new_norm_first = beta_first * norm_first + (1.0 - beta_first) * norm_grad
    new_norm_second = beta_second * norm_second + (1.0 - beta_second) * norm_grad * norm_grad
    fix_first = 1.0 - beta_first**STEP
    fix_second = 1.0 - beta_second**STEP
    new_norm_params = norm_params - adam_rate * (new_norm_first / fix_first) / (
        jnp.sqrt(new_norm_second / fix_second) + adam_eps
    )
    return (
        result.astype(jnp.bfloat16),
        token_grad,
        jnp.stack([fresh_query, fresh_key]),
        jnp.stack([fresh_value, fresh_gate]),
        fresh_out,
        jnp.stack([fresh_hidden, fresh_upper]),
        fresh_down,
        new_key_weights,
        new_value_weights,
        new_out_weights,
        new_upper_weights,
        new_down_weights,
        new_norm_first,
        new_norm_second,
        new_norm_params,
    )


def solution(mesh):
    tokens = P(("dp", "tensor"), None)
    wide = P(None, "dp", "tensor")
    tall = P("tensor", "dp")
    norms = P(("dp", "tensor"))
    return jax.shard_map(
        per_device,
        mesh=mesh,
        in_specs=(
            tokens, tokens, P("dp", None), wide, wide, tall, wide, tall,
            wide, wide, tall, wide, tall, norms, norms, norms,
        ),
        out_specs=(
            tokens, tokens, wide, wide, tall, wide, tall,
            wide, wide, tall, wide, tall, norms, norms, norms,
        ),
        check_vma=False,
    )
```

```python
from functools import partial
import math

import jax
import jax.numpy as jnp
from jax import lax
from jax.experimental import pallas as pl
from jax.experimental.pallas import tpu as pltpu
from jax.sharding import PartitionSpec as P

H = 8
KEY_HEAD_SIZE = 256
DV = 432
LEN = 1024
NS_ITERS = 5
STEP = 10


eps_norm = 1e-05
group_floor = 1.0
ns_first = 3.4445
ns_second = -4.775
ns_third = 2.0315
momentum_decay = 0.95
muon_rate = 0.5
weight_decay = 0.1
beta_first = 0.9
beta_second = 0.95
adam_rate = 0.8
adam_eps = 1e-08
TILE = 1024


def root_scale(values):
    return lax.rsqrt(jnp.mean(values * values, axis=-1, keepdims=True) + eps_norm)


def norm_back(grad_normed, normed, scaling):
    return scaling * (grad_normed - normed * jnp.mean(grad_normed * normed, axis=-1, keepdims=True))


def dot(left, right, left_dim, right_dim):
    return lax.dot_general(
        left, right, (((left_dim,), (right_dim,)), ((), ())), preferred_element_type=jnp.float32
    )


def gather_tokens(values):
    return lax.all_gather(values, "tensor", axis=0, tiled=True)


def scatter_tokens(values):
    return lax.psum_scatter(
        values.astype(jnp.bfloat16), "tensor", scatter_dimension=0, tiled=True
    ).astype(jnp.float32)


def ring_order(count):
    return list(range(0, count, 2)) + list(range(count - 1, 0, -2))


def ring_place(count):
    order = ring_order(count)
    return order, [(order[i], order[(i + 1) % count]) for i in range(count)]


def tie(value, *others):
    return lax.optimization_barrier((value, others))[0]


class Ring:
    def __init__(self):
        self.count = lax.axis_size("dp")
        order, self.right = ring_place(self.count)
        self.left = [(b, a) for a, b in self.right]
        self.half = self.count // 2
        place_of = [order.index(rank) for rank in range(self.count)]
        place = jnp.asarray(place_of, jnp.int32)[lax.axis_index("dp")]
        steps = jnp.arange(self.count, dtype=jnp.int32)
        self.rank_at = jnp.asarray(order, jnp.int32)[(place + steps) % self.count]
        self.sent = []
        self.added = None

    def rank(self, distance):
        return self.rank_at[distance % self.count]

    def exchange(self, blocks):
        if len(self.sent) > 2:
            blocks = tie(blocks, self.sent[-3])
        got = {}
        for side, block in blocks.items():
            got[side] = lax.ppermute(block, "dp", self.right if side > 0 else self.left)
        self.sent.append(got)
        return got


class Gather:
    def __init__(self, ring, shard, long_side):
        self.ring = ring
        self.shard = shard
        self.long_side = long_side
        self.rows, self.width = shard.shape
        self.blocks = [(shard, 0)]
        self.held = {1: shard, -1: shard}
        self.marks = []

    def step(self, after=None):
        at = len(self.marks) + 1
        sides = (1, -1) if at < self.ring.half else (self.long_side,)
        blocks = {side: self.held[side] for side in sides}
        if after is not None:
            blocks = tie(blocks, after)
        self.held = self.ring.exchange(blocks)
        self.blocks += [(self.held[side], -side * at) for side in sides]
        self.marks.append(self.held)


def run(lanes, rounds, after=None):
    for turn in range(rounds):
        for lane in lanes:
            lane.step(after if turn == 0 else None)


def reached(lanes, rounds):
    return [lane.marks[rounds - 1] for lane in lanes]


def loaded(lanes, rounds):
    return [lane.loads[rounds] for lane in lanes]


def nothing_kernel(out_ref):
    pass


def unwritten(shape, dtype):
    return pl.pallas_call(
        nothing_kernel,
        out_shape=jax.ShapeDtypeStruct(shape, dtype),
        out_specs=pl.BlockSpec(memory_space=pl.ANY),
    )()


def assemble(lanes, delayed=False):
    ring = lanes[0].ring
    width = lanes[0].width
    full = unwritten((sum(lane.rows for lane in lanes), width * ring.count), lanes[0].shard.dtype)
    placed, base = [], 0
    for lane in lanes:
        for index in range(3 if delayed else 1):
            block, distance = lane.blocks[index]
            lane.blocks[index] = tie(block, lane.marks[1 if delayed else 0]), distance
        placed += [(index, base, block, distance) for index, (block, distance) in enumerate(lane.blocks)]
        base += lane.rows
    for _, row, block, distance in sorted(placed, key=lambda item: item[0]):
        full = lax.dynamic_update_slice(full, block, (row, ring.rank(distance) * width))
    return full


class Scatter:
    def __init__(self, ring, full, first, rows, long_side):
        self.ring = ring
        self.full = full
        self.first = first
        self.rows = rows
        self.long_side = long_side
        self.width = full.shape[1] // ring.count
        self.held = {}
        self.marks = []
        self.loads = []

    def piece(self, distance):
        column = self.ring.rank(distance) * self.width
        return lax.dynamic_slice(self.full, (self.first, column), (self.rows, self.width))

    def step(self, after=None):
        ring = self.ring
        at = ring.half - len(self.marks)
        came = self.held
        if came and ring.added is not None:
            came = tie(came, ring.added)
        sides = (1, -1) if at < ring.half else (self.long_side,)
        blocks = {}
        for side in sides:
            block = self.piece(side * at)
            if side in came:
                block = (block.astype(jnp.float32) + came[side].astype(jnp.float32)).astype(jnp.bfloat16)
            blocks[side] = block
        if came:
            ring.added = blocks
        self.loads.append(blocks)
        self.held = ring.exchange(blocks)
        self.marks.append(self.held)

    def total(self):
        own = self.piece(0).astype(jnp.float32)
        return own + self.held[1].astype(jnp.float32) + self.held[-1].astype(jnp.float32)


def halves(rows):
    cut = (rows // 2 + 15) // 16 * 16
    return [(0, cut, 1), (cut, rows - cut, -1)]


def gather_lanes(ring, shard):
    return [Gather(ring, shard[first : first + size], side) for first, size, side in halves(shard.shape[0])]


def scatter_lanes(ring, full):
    return [Scatter(ring, full, first, size, side) for first, size, side in halves(full.shape[0])]


def totals(lanes):
    return jnp.concatenate([lane.total() for lane in lanes])


def decay_rows(doc_ids, log_gamma, first, size, keys):
    query_pos = first + jnp.arange(size)
    key_pos = jnp.arange(keys)
    distance = query_pos[:, None] - key_pos[None, :]
    allowed = (doc_ids[first : first + size, None] == doc_ids[None, :keys]) & (distance >= 0)
    steps_back = jnp.maximum(distance, 0).astype(jnp.float32)
    falloff = jnp.exp(log_gamma[:, None, None] * steps_back[None])
    return jnp.where(allowed[None], falloff, 0.0)


def einsum32(spec, left, right):
    return jnp.einsum(spec, left, right, preferred_element_type=jnp.float32)


def retention_forward(query, key, value, doc_ids, log_gamma, block):
    factor = KEY_HEAD_SIZE ** (-0.5)
    pieces = []
    for first in range(0, LEN, block):
        keys = first + block
        falloff = decay_rows(doc_ids, log_gamma, first, block, keys)
        scores = einsum32("hdq,hdk->hqk", query[:, :, first:keys], key[:, :, :keys]) * factor
        weights = (scores * falloff).astype(jnp.bfloat16)
        pieces.append(einsum32("hdk,hqk->hdq", value[:, :, :keys], weights))
    return jnp.concatenate(pieces, axis=2)


def retention_backward(query, key, value, grad, doc_ids, log_gamma, block, waits):
    factor = KEY_HEAD_SIZE ** (-0.5)
    grad_query = []
    grad_key = jnp.zeros(key.shape, jnp.float32)
    grad_value = jnp.zeros(value.shape, jnp.float32)
    for first in range(0, LEN, block):
        keys = first + block
        falloff = decay_rows(doc_ids, log_gamma, first, block, keys)
        query_now, grad_now = query[:, :, first:keys], grad[:, :, first:keys]
        if waits[first // block] is not None:
            grad_now = tie(grad_now, waits[first // block])
        scores = einsum32("hdq,hdk->hqk", query_now, key[:, :, :keys]) * factor
        weights = (scores * falloff).astype(jnp.bfloat16)
        grad_weights = einsum32("hdq,hdk->hqk", grad_now, value[:, :, :keys])
        grad_scores = (grad_weights * falloff).astype(jnp.bfloat16)
        grad_query.append(einsum32("hdk,hqk->hdq", key[:, :, :keys], grad_scores) * factor)
        grad_key = grad_key.at[:, :, :keys].add(einsum32("hdq,hqk->hdk", query_now, grad_scores) * factor)
        grad_value = grad_value.at[:, :, :keys].add(einsum32("hdq,hqk->hdk", grad_now, weights))
    return jnp.concatenate(grad_query, axis=2), grad_key, grad_value


def mirror(ref, block, first, wide):
    ref[first:, first : first + wide] = block
    if block.shape[0] > wide:
        ref[first : first + wide, first + wide :] = block[wide:].T


def newton_schulz_kernel(turns, step, in_ref, out_ref, cur_ref, low_ref, rest_ref, poly_ref, scale_ref):
    parts, size, cols = in_ref.shape
    width = parts * cols
    band = 256
    blocks = size // step

    def rows_of(index):
        return pl.ds(pl.multiple_of(index * step, step), step)

    def first_sum(index, total):
        rows = rows_of(index)
        for part in range(parts):
            block = in_ref[part, rows, :].astype(jnp.float32)
            total = total + jnp.sum(block * block)
        return total

    total = lax.fori_loop(0, blocks, first_sum, jnp.float32(0.0))
    scale_ref[...] = 1.0 / (jnp.sqrt(jnp.full(scale_ref.shape, total)) + 1e-07)

    @pl.loop(0, blocks)
    def _(index):
        rows = rows_of(index)
        scale = scale_ref[0, 0]
        for part in range(parts):
            block = in_ref[part, rows, :].astype(jnp.float32) * scale
            columns = pl.ds(part * cols, cols)
            cur_ref[rows, columns] = block
            low_ref[0, rows, columns] = block.astype(jnp.bfloat16)

    bands = [(first, min(256, size - first)) for first in range(0, size, 256)]

    def turn_body(turn, norm, last):
        here = lax.rem(turn, 2)
        there = 1 - here
        middle = norm * (1.0 / size)
        low = low_ref.at[here]
        for first, wide in bands:
            gram = dot(low[first:, :], low[first : first + wide, :], 1, 1)
            place = lax.broadcasted_iota(jnp.int32, gram.shape, 0)
            eye = place == lax.broadcasted_iota(jnp.int32, gram.shape, 1)
            mirror(rest_ref, jnp.where(eye, gram - middle, gram).astype(jnp.bfloat16), first, wide)
        for first, wide in bands:
            square = dot(rest_ref[first:, :], rest_ref[:, first : first + wide], 1, 0)
            rest = rest_ref[first:, first : first + wide].astype(jnp.float32)
            poly = (ns_second + 2.0 * ns_third * middle) * rest + ns_third * square
            mirror(poly_ref, poly.astype(jnp.bfloat16), first, wide)
        outer = ns_first + middle * (ns_second + ns_third * middle)

        total = jnp.zeros((1, band), jnp.float32)
        for first in range(0, width, band):
            columns = slice(first, first + band)
            fresh = outer * cur_ref[:, columns] + dot(poly_ref[...], low[:, columns], 1, 0)
            if last:
                out_ref[first // cols, :, first % cols : first % cols + band] = fresh.astype(jnp.bfloat16)
            else:
                cur_ref[:, columns] = fresh
                low_ref[there, :, columns] = fresh.astype(jnp.bfloat16)
                total = total + jnp.sum(fresh * fresh, axis=0, keepdims=True)
        return jnp.sum(total)

    norm = lax.fori_loop(0, turns - 1, lambda turn, norm: turn_body(turn, norm, False), jnp.float32(1.0))
    turn_body(turns - 1, norm, True)


def newton_schulz(block):
    parts, size, cols = block.shape
    width = parts * cols
    step = next(step for step in range(288, 0, -16) if size % step == 0)
    products = 2 * size * size * (2 * width + size) * NS_ITERS
    return pl.pallas_call(
        partial(newton_schulz_kernel, NS_ITERS, step),
        out_shape=jax.ShapeDtypeStruct(block.shape, jnp.bfloat16),
        in_specs=[pl.BlockSpec(memory_space=pltpu.VMEM)],
        out_specs=pl.BlockSpec(memory_space=pltpu.VMEM),
        scratch_shapes=[
            pltpu.VMEM((size, width), jnp.float32),
            pltpu.VMEM((2, size, width), jnp.bfloat16),
            pltpu.VMEM((size, size), jnp.bfloat16),
            pltpu.VMEM((size, size), jnp.bfloat16),
            pltpu.VMEM((8, 128), jnp.float32),
        ],
        compiler_params=pltpu.CompilerParams(vmem_limit_bytes=48 * 1024 * 1024),
        cost_estimate=pl.CostEstimate(flops=products, bytes_accessed=4 * size * width, transcendentals=0),
    )(block)


def orthogonalize(slabs, norm_terms, own_norms):
    ranks = lax.axis_size("dp")
    widest = max(slab.shape[0] for slab in slabs)
    cols = slabs[0].shape[1]
    padded = [jnp.pad(slab.astype(jnp.bfloat16), ((0, widest - slab.shape[0]), (0, 0))) for slab in slabs]
    each = (len(slabs) + ranks - 1) // ranks
    padded += [jnp.zeros((widest, cols), jnp.bfloat16)] * (each * ranks - len(slabs))
    stacked = jnp.stack(padded)
    owned = lax.all_to_all(stacked.reshape(ranks, each, widest, cols), "dp", 0, 0, tiled=True)
    owned, norm_terms = tie((owned, sum_tensor(norm_terms)))
    norm_grad = sum_dp(norm_terms, own_norms)
    done = []
    for index in range(each):
        mine = owned[:, index]
        if cols % 128:
            mine = jnp.moveaxis(mine, 0, 1).reshape(1, widest, ranks * cols)
        item = newton_schulz(mine)
        if cols % 128:
            item = jnp.moveaxis(item.reshape(widest, ranks, cols), 1, 0)
        done.append(item)
    ready = jnp.stack(done, axis=1)
    ready = tie(ready, norm_grad)
    returned = lax.all_to_all(ready, "dp", 0, 0, tiled=True).reshape(each * ranks, widest, cols)
    return [returned[index, : slab.shape[0]] for index, slab in enumerate(slabs)], norm_grad


def gather_small(piece, axis):
    count = lax.axis_size(axis)
    index = lax.axis_index(axis)
    held = piece
    bit = 1
    while bit < count:
        came = lax.ppermute(held, axis, [(i, i ^ bit) for i in range(count)])
        mine = (index // bit) % 2
        start = (0,) * held.ndim
        both = jnp.zeros((2,) + held.shape, held.dtype)
        both = lax.dynamic_update_slice(both, held[None], (mine,) + start)
        held = lax.dynamic_update_slice(both, came[None], (1 - mine,) + start)
        bit *= 2
    return held.reshape((count,) + piece.shape), came


def sum_tensor(terms):
    count = lax.axis_size("tensor")
    bit = 1
    while bit < count:
        terms = terms + lax.ppermute(terms, "tensor", [(i, i ^ bit) for i in range(count)])
        bit *= 2
    return terms


def sum_dp(terms, own):
    count = lax.axis_size("dp")
    group = terms.shape[0] // count
    filled = TILE * ((group + TILE - 1) // TILE)
    rows = jnp.pad(terms.reshape(count, group), ((0, 0), (0, filled - group))).reshape(-1, 128)
    mine = lax.psum_scatter(rows, "dp", scatter_dimension=0, tiled=True).reshape(-1)
    return lax.dynamic_slice_in_dim(mine, lax.axis_index("tensor") * own, own)


def per_device(
    tokens,
    cotangent,
    doc_lengths,
    key_weights,
    value_weights,
    out_weights,
    up_weights,
    down_weights,
    key_momentum,
    value_momentum,
    out_momentum,
    up_momentum,
    down_momentum,
    norm_params,
    norm_first,
    norm_second,
):
    tensor_count = lax.axis_size("tensor")
    tensor_index = lax.axis_index("tensor")
    heads = H // tensor_count
    width = tokens.shape[1]
    keys_local = key_weights.shape[2]
    values_local = value_weights.shape[2]
    hidden_local = up_weights.shape[2]
    value_total = values_local * tensor_count
    block = min(LEN, 512)
    ring = Ring()
    half = ring.half
    quarter = half // 4

    def low_t(matrix):
        return matrix.astype(jnp.bfloat16).T

    attend_lanes = gather_lanes(
        ring,
        jnp.concatenate(
            [low_t(key_weights[0]), low_t(key_weights[1]), low_t(value_weights[0]), low_t(value_weights[1])]
        ),
    )
    out_lanes = [Gather(ring, out_weights.astype(jnp.bfloat16), 1)]
    upper_lanes = gather_lanes(ring, jnp.concatenate([low_t(up_weights[0]), low_t(up_weights[1])]))
    down_lanes = [Gather(ring, down_weights.astype(jnp.bfloat16), -1)]
    tokens_all = gather_tokens(tokens)
    own_norms = norm_params.shape[0]
    filled_norms = TILE * ((own_norms + TILE - 1) // TILE)
    norm_piece = jnp.pad(norm_params, (0, filled_norms - own_norms)).reshape(filled_norms // 128, 128)
    norm_group, _ = gather_small(norm_piece, "tensor")
    attend_lanes[0].step()
    attend_lanes[1].step()
    gathered_norms, last_norms = gather_small(tie(norm_group, reached(attend_lanes[:1], 1)), "dp")
    attend_lanes[0].step()
    attend_lanes[1].step(last_norms)
    gathered_norms = gathered_norms.reshape(-1, filled_norms)[:, :own_norms].reshape(-1)

    gain_one = gathered_norms[:width]
    gain_two = gathered_norms[width : 2 * width]
    group_gain = lax.dynamic_slice_in_dim(
        gathered_norms, 2 * width + tensor_index * values_local, values_local
    )[:, None]
    group_bias = lax.dynamic_slice_in_dim(
        gathered_norms, 2 * width + value_total + tensor_index * values_local, values_local
    )[:, None]
    lengths = tie(doc_lengths[0], reached(attend_lanes, 1))
    starts_all = jnp.cumsum(lengths) - lengths
    positions = jnp.arange(LEN)
    doc_ids = jnp.sum((positions[:, None] >= starts_all[None, :]).astype(jnp.int32), axis=1) - 1

    inputs = tokens.astype(jnp.float32)
    scale_one = root_scale(inputs)
    normed_one = inputs * scale_one
    inputs_all = tokens_all.astype(jnp.float32)
    normed_all = (inputs_all * root_scale(inputs_all) * gain_one).astype(jnp.bfloat16)
    rows_total = normed_all.shape[0]
    grad_rows_two = gather_tokens(tie(cotangent, tokens_all))
    attend_lanes[0].step()
    attend_lanes[1].step(normed_all)
    run(attend_lanes, half - 3)
    run(out_lanes, quarter)
    attend_full = assemble(attend_lanes, True)

    gate_row = 2 * keys_local + values_local
    attend = dot(attend_full[:gate_row], normed_all, 1, 1).astype(jnp.bfloat16)
    attend = tie(attend, reached(out_lanes, quarter))
    run(out_lanes, quarter, attend)
    upper_lanes[0].step()
    query = attend[:keys_local].reshape(heads, KEY_HEAD_SIZE, rows_total)
    key = attend[keys_local : 2 * keys_local].reshape(heads, KEY_HEAD_SIZE, rows_total)
    value = attend[2 * keys_local :].reshape(heads, DV, rows_total)
    head_ids = (tensor_index * heads + jnp.arange(heads)).astype(jnp.float32)
    log_gamma = jnp.log(1.0 - jnp.exp2(-5.0 - head_ids))
    mixed_heads = retention_forward(query, key, value, doc_ids, log_gamma, block)
    mixed_heads = tie(mixed_heads, reached(out_lanes, 2 * quarter))
    run(out_lanes, quarter)
    upper_lanes[1].step()
    run(out_lanes, half - 3 * quarter)
    out_full = assemble(out_lanes)
    run(upper_lanes, half - 1)
    run(down_lanes, 2 * quarter)
    upper_full = assemble(upper_lanes)
    gate_pre = dot(attend_full[gate_row:], tie(normed_all, mixed_heads), 1, 1)
    centred = mixed_heads - jnp.mean(mixed_heads, axis=1, keepdims=True)
    group_scale = lax.rsqrt(jnp.mean(centred * centred, axis=1, keepdims=True) + group_floor)
    group_hat = centred * group_scale
    group_flat = group_hat.reshape(values_local, rows_total)
    group_out = group_flat * group_gain + group_bias
    gate_act, silu_pull = jax.vjp(jax.nn.silu, gate_pre)
    mixed_low = (gate_act * group_out).astype(jnp.bfloat16)
    mixed_low, grad_rows_two = tie((mixed_low, grad_rows_two), reached(out_lanes, half), reached(upper_lanes[:1], 1))
    branch_one = scatter_tokens(dot(mixed_low, out_full, 0, 0))
    middle = inputs + tie(branch_one, reached(upper_lanes, half))
    scale_two = root_scale(middle)
    normed_two = middle * scale_two
    second_all = gather_tokens((normed_two * gain_two).astype(jnp.bfloat16))
    run(down_lanes, half - 2 * quarter, second_all)
    second_all = tie(second_all, reached(down_lanes, 2 * quarter))
    down_full = assemble(down_lanes)
    hidden_gate = dot(upper_full[:hidden_local], second_all, 1, 1)
    second_late = tie(second_all, hidden_gate, reached(down_lanes, 3 * quarter))
    hidden_upper = dot(upper_full[hidden_local:], second_late, 1, 1)
    gelu_gate, gelu_pull = jax.vjp(partial(jax.nn.gelu, approximate=False), hidden_gate)
    hidden_low = (gelu_gate * hidden_upper).astype(jnp.bfloat16)

    grad_result = cotangent.astype(jnp.float32)
    rows_two_late = tie(grad_rows_two, hidden_low, reached(down_lanes, half))
    grad_down = dot(hidden_low, rows_two_late, 1, 0).astype(jnp.bfloat16)
    down_back = [Scatter(ring, grad_down, 0, hidden_local, -1)]
    run(down_back, half)
    grad_hidden = dot(down_full, tie(grad_rows_two, grad_down), 1, 1)
    grad_gate_mlp = gelu_pull(grad_hidden * hidden_upper)[0].astype(jnp.bfloat16)
    grad_upper_mlp = (grad_hidden * gelu_gate).astype(jnp.bfloat16)
    grad_hidden_low = jnp.concatenate([grad_gate_mlp, grad_upper_mlp])
    grad_hidden_low = tie(grad_hidden_low, loaded(down_back, quarter))
    grad_second = dot(grad_hidden_low, upper_full, 0, 0).astype(jnp.bfloat16)
    grad_second, grad_hidden_late = tie((grad_second, grad_hidden_low))
    grad_second_local = scatter_tokens(tie(grad_second, reached(down_back, 2 * quarter)))
    grad_hidden_late = tie(grad_hidden_late, loaded(down_back, 2 * quarter))
    grad_upper = dot(grad_hidden_late, second_all, 1, 0).astype(jnp.bfloat16)
    upper_back = scatter_lanes(ring, tie(grad_upper, reached(down_back, 3 * quarter)))
    run(upper_back, half)
    branch_two = dot(tie(hidden_low, grad_upper), down_full, 0, 0).astype(jnp.bfloat16)
    grad_second_local = tie(
        grad_second_local, reached(upper_back[:1], 2 * quarter), loaded(upper_back[1:], quarter), branch_two
    )
    grad_gain_two = jnp.sum(grad_second_local * normed_two, axis=0)
    grad_middle = grad_result + norm_back(grad_second_local * gain_two, normed_two, scale_two)
    grad_middle_low = grad_middle.astype(jnp.bfloat16)
    grad_rows_one = gather_tokens(grad_middle_low)
    branch_two = lax.psum_scatter(tie(branch_two, grad_rows_one), "tensor", scatter_dimension=0, tiled=True)
    result = middle + branch_two.astype(jnp.float32)
    grad_rows_one = tie(grad_rows_one, loaded(upper_back, 3 * quarter))
    out_back = [Scatter(ring, dot(mixed_low, grad_rows_one, 1, 0).astype(jnp.bfloat16), 0, values_local, 1)]
    run(out_back, quarter)
    grad_mixed = dot(out_full, tie(grad_rows_one, loaded(out_back, 0)), 1, 1)
    grad_gate_low = silu_pull(grad_mixed * group_out)[0].astype(jnp.bfloat16)
    gate_back = [Scatter(ring, dot(grad_gate_low, normed_all, 1, 0).astype(jnp.bfloat16), 0, values_local, -1)]
    run(gate_back, quarter)
    run(out_back + gate_back, half - quarter)
    grad_group = grad_mixed * gate_act
    grad_group_gain = jnp.sum(grad_group * group_flat, axis=1)
    grad_group_bias = jnp.sum(grad_group, axis=1)
    grad_hat = (grad_group * group_gain).reshape(heads, DV, rows_total)
    grad_heads = group_scale * (
        grad_hat
        - jnp.mean(grad_hat, axis=1, keepdims=True)
        - group_hat * jnp.mean(grad_hat * group_hat, axis=1, keepdims=True)
    )
    grad_heads = tie(grad_heads, loaded(out_back, quarter), loaded(gate_back, 0))
    waits = [None, (loaded(out_back, 2 * quarter), loaded(gate_back, quarter))]
    grad_queries, grad_keys, grad_values = retention_backward(
        query, key, value, grad_heads.astype(jnp.bfloat16), doc_ids, log_gamma, block, waits
    )
    grad_attend_low = jnp.concatenate(
        [
            grad_queries.astype(jnp.bfloat16).reshape(keys_local, rows_total),
            grad_keys.astype(jnp.bfloat16).reshape(keys_local, rows_total),
            grad_values.astype(jnp.bfloat16).reshape(values_local, rows_total),
        ]
    )
    grad_attend_low = tie(grad_attend_low, loaded(out_back, 3 * quarter))
    grad_attend = dot(grad_attend_low, normed_all, 1, 0).astype(jnp.bfloat16)
    attend_back = scatter_lanes(ring, grad_attend)
    run(attend_back, half)
    pieces = []
    for index in range(4):
        rows = slice(index * rows_total // 4, (index + 1) * rows_total // 4)
        if index < 3:
            marker = loaded([attend_back[min(index, 1)]], (1, 1, 2)[index] * quarter)
        else:
            marker = reached(attend_back[:1], half)
        late, gate_late = tie((grad_attend_low[:, rows], grad_gate_low[:, rows]), marker)
        piece = dot(late, attend_full[:gate_row], 0, 0) + dot(gate_late, attend_full[gate_row:], 0, 0)
        pieces.append(piece.astype(jnp.bfloat16))
    grad_first = jnp.concatenate(pieces)
    grad_first_local = scatter_tokens(tie(grad_first, branch_two))
    grad_gain_one = jnp.sum(grad_first_local * normed_one, axis=0)
    token_grad = grad_middle + norm_back(grad_first_local * gain_one, normed_one, scale_one)
    group_part = jnp.zeros((2, value_total), jnp.float32)
    group_part = lax.dynamic_update_slice_in_dim(
        group_part, jnp.stack([grad_group_gain, grad_group_bias]), tensor_index * values_local, 1
    )
    norm_terms = jnp.concatenate([grad_gain_one, grad_gain_two, group_part.reshape(-1)])
    grad_down_w = totals(down_back)
    grad_upper_w = totals(upper_back)
    grad_out_w = totals(out_back)
    grad_gate_w = totals(gate_back)
    grad_attend_w = totals(attend_back)

    fresh_query = momentum_decay * key_momentum[0] + grad_attend_w[:keys_local].T
    fresh_key = momentum_decay * key_momentum[1] + grad_attend_w[keys_local : 2 * keys_local].T
    fresh_value = momentum_decay * value_momentum[0] + grad_attend_w[2 * keys_local :].T
    fresh_gate = momentum_decay * value_momentum[1] + grad_gate_w.T
    fresh_out = momentum_decay * out_momentum + grad_out_w
    fresh_hidden = momentum_decay * up_momentum[0] + grad_upper_w[:hidden_local].T
    fresh_upper = momentum_decay * up_momentum[1] + grad_upper_w[hidden_local:].T
    fresh_down = momentum_decay * down_momentum + grad_down_w
    orth, norm_grad = orthogonalize(
        [
            fresh_down,
            fresh_hidden.T,
            fresh_upper.T,
            fresh_out,
            fresh_gate.T,
            fresh_value.T,
            fresh_query.T,
            fresh_key.T,
        ],
        norm_terms,
        own_norms,
    )
    orth = [item.astype(jnp.float32) for item in orth]
    keep_factor = 1.0 - muon_rate * weight_decay

    def rate(rows, cols):
        return muon_rate * math.sqrt(max(1.0, rows / cols))

    new_key_weights = key_weights * keep_factor - rate(width, keys_local) * jnp.stack([orth[6].T, orth[7].T])
    new_value_weights = value_weights * keep_factor - rate(width, values_local) * jnp.stack([orth[5].T, orth[4].T])
    new_upper_weights = up_weights * keep_factor - rate(width, hidden_local) * jnp.stack([orth[1].T, orth[2].T])
    new_out_weights = out_weights * keep_factor - rate(values_local, width) * orth[3]
    new_down_weights = down_weights * keep_factor - rate(hidden_local, width) * orth[0]
    new_norm_first = beta_first * norm_first + (1.0 - beta_first) * norm_grad
    new_norm_second = beta_second * norm_second + (1.0 - beta_second) * norm_grad * norm_grad
    fix_first = 1.0 - beta_first**STEP
    fix_second = 1.0 - beta_second**STEP
    new_norm_params = norm_params - adam_rate * (new_norm_first / fix_first) / (
        jnp.sqrt(new_norm_second / fix_second) + adam_eps
    )
    return (
        result.astype(jnp.bfloat16),
        token_grad,
        jnp.stack([fresh_query, fresh_key]),
        jnp.stack([fresh_value, fresh_gate]),
        fresh_out,
        jnp.stack([fresh_hidden, fresh_upper]),
        fresh_down,
        new_key_weights,
        new_value_weights,
        new_out_weights,
        new_upper_weights,
        new_down_weights,
        new_norm_first,
        new_norm_second,
        new_norm_params,
    )


def solution(mesh):
    tokens = P(("dp", "tensor"), None)
    wide = P(None, "dp", "tensor")
    tall = P("tensor", "dp")
    norms = P(("dp", "tensor"))
    return jax.shard_map(
        per_device,
        mesh=mesh,
        in_specs=(
            tokens, tokens, P("dp", None), wide, wide, tall, wide, tall,
            wide, wide, tall, wide, tall, norms, norms, norms,
        ),
        out_specs=(
            tokens, tokens, wide, wide, tall, wide, tall,
            wide, wide, tall, wide, tall, norms, norms, norms,
        ),
        check_vma=False,
    )
```

```python
from functools import partial
import math

import jax
import jax.numpy as jnp
from jax import lax
from jax.experimental import pallas as pl
from jax.experimental.pallas import tpu as pltpu
from jax.sharding import PartitionSpec as P

H = 8
KEY_HEAD_SIZE = 256
DV = 432
LEN = 1024
NS_ITERS = 5
STEP = 10


eps_norm = 1e-05
group_floor = 1.0
ns_first = 3.4445
ns_second = -4.775
ns_third = 2.0315
momentum_decay = 0.95
muon_rate = 0.5
weight_decay = 0.1
beta_first = 0.9
beta_second = 0.95
adam_rate = 0.8
adam_eps = 1e-08
TILE = 1024


def root_scale(values):
    return lax.rsqrt(jnp.mean(values * values, axis=-1, keepdims=True) + eps_norm)


def norm_back(grad_normed, normed, scaling):
    return scaling * (grad_normed - normed * jnp.mean(grad_normed * normed, axis=-1, keepdims=True))


def dot(left, right, left_dim, right_dim):
    return lax.dot_general(
        left, right, (((left_dim,), (right_dim,)), ((), ())), preferred_element_type=jnp.float32
    )


def gather_tokens(values):
    return lax.all_gather(values, "tensor", axis=0, tiled=True)


def scatter_tokens(values):
    return lax.psum_scatter(
        values.astype(jnp.bfloat16), "tensor", scatter_dimension=0, tiled=True
    ).astype(jnp.float32)


def ring_order(count):
    return list(range(0, count, 2)) + list(range(count - 1, 0, -2))


def ring_place(count):
    order = ring_order(count)
    return order, [(order[i], order[(i + 1) % count]) for i in range(count)]


def tie(value, *others):
    return lax.optimization_barrier((value, others))[0]


class Ring:
    def __init__(self):
        self.count = lax.axis_size("dp")
        order, self.right = ring_place(self.count)
        self.left = [(b, a) for a, b in self.right]
        self.half = self.count // 2
        place_of = [order.index(rank) for rank in range(self.count)]
        place = jnp.asarray(place_of, jnp.int32)[lax.axis_index("dp")]
        steps = jnp.arange(self.count, dtype=jnp.int32)
        self.rank_at = jnp.asarray(order, jnp.int32)[(place + steps) % self.count]
        self.sent = []
        self.added = None

    def rank(self, distance):
        return self.rank_at[distance % self.count]

    def exchange(self, blocks):
        if len(self.sent) > 2:
            blocks = tie(blocks, self.sent[-3])
        got = {}
        for side, block in blocks.items():
            got[side] = lax.ppermute(block, "dp", self.right if side > 0 else self.left)
        self.sent.append(got)
        return got


class Gather:
    def __init__(self, ring, shard, long_side):
        self.ring = ring
        self.shard = shard
        self.long_side = long_side
        self.rows, self.width = shard.shape
        self.blocks = [(shard, 0)]
        self.held = {1: shard, -1: shard}
        self.marks = []

    def step(self, after=None):
        at = len(self.marks) + 1
        sides = (1, -1) if at < self.ring.half else (self.long_side,)
        blocks = {side: self.held[side] for side in sides}
        if after is not None:
            blocks = tie(blocks, after)
        self.held = self.ring.exchange(blocks)
        self.blocks += [(self.held[side], -side * at) for side in sides]
        self.marks.append(self.held)


def run(lanes, rounds, after=None):
    for turn in range(rounds):
        for lane in lanes:
            lane.step(after if turn == 0 else None)


def reached(lanes, rounds):
    return [lane.marks[rounds - 1] for lane in lanes]


def loaded(lanes, rounds):
    return [lane.loads[rounds] for lane in lanes]


def nothing_kernel(out_ref):
    pass


def unwritten(shape, dtype):
    return pl.pallas_call(
        nothing_kernel,
        out_shape=jax.ShapeDtypeStruct(shape, dtype),
        out_specs=pl.BlockSpec(memory_space=pl.ANY),
    )()


def assemble(lanes):
    ring = lanes[0].ring
    width = lanes[0].width
    full = unwritten((sum(lane.rows for lane in lanes), width * ring.count), lanes[0].shard.dtype)
    placed, base = [], 0
    for lane in lanes:
        lane.blocks[0] = tie(lane.shard, lane.marks[0]), 0
        placed += [(index, base, block, distance) for index, (block, distance) in enumerate(lane.blocks)]
        base += lane.rows
    for _, row, block, distance in sorted(placed, key=lambda item: item[0]):
        full = lax.dynamic_update_slice(full, block, (row, ring.rank(distance) * width))
    return full


class Scatter:
    def __init__(self, ring, full, first, rows, long_side):
        self.ring = ring
        self.full = full
        self.first = first
        self.rows = rows
        self.long_side = long_side
        self.width = full.shape[1] // ring.count
        self.held = {}
        self.marks = []
        self.loads = []

    def piece(self, distance):
        column = self.ring.rank(distance) * self.width
        return lax.dynamic_slice(self.full, (self.first, column), (self.rows, self.width))

    def step(self, after=None):
        ring = self.ring
        at = ring.half - len(self.marks)
        came = self.held
        if came and ring.added is not None:
            came = tie(came, ring.added)
        sides = (1, -1) if at < ring.half else (self.long_side,)
        blocks = {}
        for side in sides:
            block = self.piece(side * at)
            if side in came:
                block = (block.astype(jnp.float32) + came[side].astype(jnp.float32)).astype(jnp.bfloat16)
            blocks[side] = block
        if came:
            ring.added = blocks
        self.loads.append(blocks)
        self.held = ring.exchange(blocks)
        self.marks.append(self.held)

    def total(self):
        own = self.piece(0).astype(jnp.float32)
        return own + self.held[1].astype(jnp.float32) + self.held[-1].astype(jnp.float32)


def halves(rows):
    cut = (rows // 2 + 15) // 16 * 16
    return [(0, cut, 1), (cut, rows - cut, -1)]


def gather_lanes(ring, shard):
    return [Gather(ring, shard[first : first + size], side) for first, size, side in halves(shard.shape[0])]


def scatter_lanes(ring, full):
    return [Scatter(ring, full, first, size, side) for first, size, side in halves(full.shape[0])]


def totals(lanes):
    return jnp.concatenate([lane.total() for lane in lanes])


def decay_rows(doc_ids, log_gamma, first, size, keys):
    query_pos = first + jnp.arange(size)
    key_pos = jnp.arange(keys)
    distance = query_pos[:, None] - key_pos[None, :]
    allowed = (doc_ids[first : first + size, None] == doc_ids[None, :keys]) & (distance >= 0)
    steps_back = jnp.maximum(distance, 0).astype(jnp.float32)
    falloff = jnp.exp(log_gamma[:, None, None] * steps_back[None])
    return jnp.where(allowed[None], falloff, 0.0)


def einsum32(spec, left, right):
    return jnp.einsum(spec, left, right, preferred_element_type=jnp.float32)


def retention_forward(query, key, value, doc_ids, log_gamma, block):
    factor = KEY_HEAD_SIZE ** (-0.5)
    pieces = []
    for first in range(0, LEN, block):
        keys = first + block
        falloff = decay_rows(doc_ids, log_gamma, first, block, keys)
        scores = einsum32("hdq,hdk->hqk", query[:, :, first:keys], key[:, :, :keys]) * factor
        weights = (scores * falloff).astype(jnp.bfloat16)
        pieces.append(einsum32("hdk,hqk->hdq", value[:, :, :keys], weights))
    return jnp.concatenate(pieces, axis=2)


def retention_backward(query, key, value, grad, doc_ids, log_gamma, block, waits):
    factor = KEY_HEAD_SIZE ** (-0.5)
    grad_query = []
    grad_key = jnp.zeros(key.shape, jnp.float32)
    grad_value = jnp.zeros(value.shape, jnp.float32)
    for first in range(0, LEN, block):
        keys = first + block
        falloff = decay_rows(doc_ids, log_gamma, first, block, keys)
        query_now, grad_now = query[:, :, first:keys], grad[:, :, first:keys]
        if waits[first // block] is not None:
            grad_now = tie(grad_now, waits[first // block])
        scores = einsum32("hdq,hdk->hqk", query_now, key[:, :, :keys]) * factor
        weights = (scores * falloff).astype(jnp.bfloat16)
        grad_weights = einsum32("hdq,hdk->hqk", grad_now, value[:, :, :keys])
        grad_scores = (grad_weights * falloff).astype(jnp.bfloat16)
        grad_query.append(einsum32("hdk,hqk->hdq", key[:, :, :keys], grad_scores) * factor)
        grad_key = grad_key.at[:, :, :keys].add(einsum32("hdq,hqk->hdk", query_now, grad_scores) * factor)
        grad_value = grad_value.at[:, :, :keys].add(einsum32("hdq,hqk->hdk", grad_now, weights))
    return jnp.concatenate(grad_query, axis=2), grad_key, grad_value


def mirror(ref, block, first, wide):
    ref[first:, first : first + wide] = block
    if block.shape[0] > wide:
        ref[first : first + wide, first + wide :] = block[wide:].T


def newton_schulz_kernel(turns, step, in_ref, out_ref, cur_ref, low_ref, rest_ref, poly_ref, scale_ref):
    parts, size, cols = in_ref.shape
    width = parts * cols
    band = 256
    blocks = size // step

    def rows_of(index):
        return pl.ds(pl.multiple_of(index * step, step), step)

    def first_sum(index, total):
        rows = rows_of(index)
        for part in range(parts):
            block = in_ref[part, rows, :].astype(jnp.float32)
            total = total + jnp.sum(block * block)
        return total

    total = lax.fori_loop(0, blocks, first_sum, jnp.float32(0.0))
    scale_ref[...] = 1.0 / (jnp.sqrt(jnp.full(scale_ref.shape, total)) + 1e-07)

    @pl.loop(0, blocks)
    def _(index):
        rows = rows_of(index)
        scale = scale_ref[0, 0]
        for part in range(parts):
            block = in_ref[part, rows, :].astype(jnp.float32) * scale
            columns = pl.ds(part * cols, cols)
            cur_ref[rows, columns] = block
            low_ref[0, rows, columns] = block.astype(jnp.bfloat16)

    bands = [(first, min(256, size - first)) for first in range(0, size, 256)]

    def turn_body(turn, norm, last):
        here = lax.rem(turn, 2)
        there = 1 - here
        middle = norm * (1.0 / size)
        low = low_ref.at[here]
        for first, wide in bands:
            gram = dot(low[first:, :], low[first : first + wide, :], 1, 1)
            place = lax.broadcasted_iota(jnp.int32, gram.shape, 0)
            eye = place == lax.broadcasted_iota(jnp.int32, gram.shape, 1)
            mirror(rest_ref, jnp.where(eye, gram - middle, gram).astype(jnp.bfloat16), first, wide)
        for first, wide in bands:
            square = dot(rest_ref[first:, :], rest_ref[:, first : first + wide], 1, 0)
            rest = rest_ref[first:, first : first + wide].astype(jnp.float32)
            poly = (ns_second + 2.0 * ns_third * middle) * rest + ns_third * square
            mirror(poly_ref, poly.astype(jnp.bfloat16), first, wide)
        outer = ns_first + middle * (ns_second + ns_third * middle)

        total = jnp.zeros((1, band), jnp.float32)
        for first in range(0, width, band):
            columns = slice(first, first + band)
            fresh = outer * cur_ref[:, columns] + dot(poly_ref[...], low[:, columns], 1, 0)
            if last:
                out_ref[first // cols, :, first % cols : first % cols + band] = fresh.astype(jnp.bfloat16)
            else:
                cur_ref[:, columns] = fresh
                low_ref[there, :, columns] = fresh.astype(jnp.bfloat16)
                total = total + jnp.sum(fresh * fresh, axis=0, keepdims=True)
        return jnp.sum(total)

    norm = lax.fori_loop(0, turns - 1, lambda turn, norm: turn_body(turn, norm, False), jnp.float32(1.0))
    turn_body(turns - 1, norm, True)


def newton_schulz(block):
    parts, size, cols = block.shape
    width = parts * cols
    step = next(step for step in range(288, 0, -16) if size % step == 0)
    products = 2 * size * size * (2 * width + size) * NS_ITERS
    return pl.pallas_call(
        partial(newton_schulz_kernel, NS_ITERS, step),
        out_shape=jax.ShapeDtypeStruct(block.shape, jnp.bfloat16),
        in_specs=[pl.BlockSpec(memory_space=pltpu.VMEM)],
        out_specs=pl.BlockSpec(memory_space=pltpu.VMEM),
        scratch_shapes=[
            pltpu.VMEM((size, width), jnp.float32),
            pltpu.VMEM((2, size, width), jnp.bfloat16),
            pltpu.VMEM((size, size), jnp.bfloat16),
            pltpu.VMEM((size, size), jnp.bfloat16),
            pltpu.VMEM((8, 128), jnp.float32),
        ],
        compiler_params=pltpu.CompilerParams(vmem_limit_bytes=48 * 1024 * 1024),
        cost_estimate=pl.CostEstimate(flops=products, bytes_accessed=4 * size * width, transcendentals=0),
    )(block)


def stack_slabs(slabs):
    ranks = lax.axis_size("dp")
    widest = max(slab.shape[0] for slab in slabs)
    cols = slabs[0].shape[1]
    padded = [jnp.pad(slab.astype(jnp.bfloat16), ((0, widest - slab.shape[0]), (0, 0))) for slab in slabs]
    each = (len(slabs) + ranks - 1) // ranks
    padded += [jnp.zeros((widest, cols), jnp.bfloat16)] * (each * ranks - len(slabs))
    return jnp.stack(padded).reshape(ranks, each, widest, cols)


def move_slots(stacked):
    return lax.all_to_all(stacked, "dp", 0, 0, tiled=True)


def orthogonalize(owned):
    ranks, each, widest, cols = owned.shape
    done = []
    for index in range(each):
        mine = owned[:, index]
        if cols % 128:
            mine = jnp.moveaxis(mine, 0, 1).reshape(1, widest, ranks * cols)
        item = newton_schulz(mine)
        if cols % 128:
            item = jnp.moveaxis(item.reshape(widest, ranks, cols), 1, 0)
        done.append(item)
    return jnp.stack(done, axis=1)


def gather_small(piece, axis):
    count = lax.axis_size(axis)
    index = lax.axis_index(axis)
    held = piece
    bit = 1
    while bit < count:
        came = lax.ppermute(held, axis, [(i, i ^ bit) for i in range(count)])
        mine = (index // bit) % 2
        start = (0,) * held.ndim
        both = jnp.zeros((2,) + held.shape, held.dtype)
        both = lax.dynamic_update_slice(both, held[None], (mine,) + start)
        held = lax.dynamic_update_slice(both, came[None], (1 - mine,) + start)
        bit *= 2
    return held.reshape((count,) + piece.shape), came


def sum_norms(terms):
    for axis in ("tensor", "dp"):
        count = lax.axis_size(axis)
        bit = 1
        while bit < count:
            terms = terms + lax.ppermute(terms, axis, [(i, i ^ bit) for i in range(count)])
            bit *= 2
    return terms


def per_device(
    tokens,
    cotangent,
    doc_lengths,
    key_weights,
    value_weights,
    out_weights,
    up_weights,
    down_weights,
    key_momentum,
    value_momentum,
    out_momentum,
    up_momentum,
    down_momentum,
    norm_params,
    norm_first,
    norm_second,
):
    tensor_count = lax.axis_size("tensor")
    tensor_index = lax.axis_index("tensor")
    heads = H // tensor_count
    width = tokens.shape[1]
    keys_local = key_weights.shape[2]
    values_local = value_weights.shape[2]
    hidden_local = up_weights.shape[2]
    value_total = values_local * tensor_count
    block = min(LEN, 512)
    ring = Ring()
    half = ring.half
    quarter = half // 4

    def low_t(matrix):
        return matrix.astype(jnp.bfloat16).T

    attend_lanes = gather_lanes(
        ring,
        jnp.concatenate(
            [low_t(key_weights[0]), low_t(key_weights[1]), low_t(value_weights[0]), low_t(value_weights[1])]
        ),
    )
    out_lanes = [Gather(ring, out_weights.astype(jnp.bfloat16), 1)]
    upper_lanes = gather_lanes(ring, jnp.concatenate([low_t(up_weights[0]), low_t(up_weights[1])]))
    down_lanes = [Gather(ring, down_weights.astype(jnp.bfloat16), -1)]
    tokens_all = gather_tokens(tokens)
    own_norms = norm_params.shape[0]
    filled_norms = TILE * ((own_norms + TILE - 1) // TILE)
    norm_piece = jnp.pad(norm_params, (0, filled_norms - own_norms)).reshape(filled_norms // 128, 128)
    norm_group, _ = gather_small(norm_piece, "tensor")
    attend_lanes[0].step()
    attend_lanes[1].step()
    gathered_norms, last_norms = gather_small(tie(norm_group, reached(attend_lanes[:1], 1)), "dp")
    attend_lanes[0].step(last_norms)
    attend_lanes[1].step()
    gathered_norms = gathered_norms.reshape(-1, filled_norms)[:, :own_norms].reshape(-1)

    gain_one = gathered_norms[:width]
    gain_two = gathered_norms[width : 2 * width]
    group_gain = lax.dynamic_slice_in_dim(
        gathered_norms, 2 * width + tensor_index * values_local, values_local
    )[:, None]
    group_bias = lax.dynamic_slice_in_dim(
        gathered_norms, 2 * width + value_total + tensor_index * values_local, values_local
    )[:, None]
    lengths = tie(doc_lengths[0], reached(attend_lanes, 1))
    starts_all = jnp.cumsum(lengths) - lengths
    positions = jnp.arange(LEN)
    doc_ids = jnp.sum((positions[:, None] >= starts_all[None, :]).astype(jnp.int32), axis=1) - 1

    inputs = tokens.astype(jnp.float32)
    scale_one = root_scale(inputs)
    normed_one = inputs * scale_one
    inputs_all = tokens_all.astype(jnp.float32)
    normed_all = (inputs_all * root_scale(inputs_all) * gain_one).astype(jnp.bfloat16)
    rows_total = normed_all.shape[0]
    grad_rows_two = gather_tokens(tie(cotangent, tokens_all))
    attend_lanes[0].step(normed_all)
    attend_lanes[1].step()
    run(attend_lanes, half - 3)
    run(out_lanes, quarter)
    attend_full = assemble(attend_lanes)

    gate_row = 2 * keys_local + values_local
    attend = dot(attend_full[:gate_row], normed_all, 1, 1).astype(jnp.bfloat16)
    attend = tie(attend, reached(out_lanes, quarter))
    run(out_lanes, quarter, attend)
    upper_lanes[0].step()
    query = attend[:keys_local].reshape(heads, KEY_HEAD_SIZE, rows_total)
    key = attend[keys_local : 2 * keys_local].reshape(heads, KEY_HEAD_SIZE, rows_total)
    value = attend[2 * keys_local :].reshape(heads, DV, rows_total)
    head_ids = (tensor_index * heads + jnp.arange(heads)).astype(jnp.float32)
    log_gamma = jnp.log(1.0 - jnp.exp2(-5.0 - head_ids))
    mixed_heads = retention_forward(query, key, value, doc_ids, log_gamma, block)
    mixed_heads = tie(mixed_heads, reached(out_lanes, 2 * quarter))
    run(out_lanes, quarter)
    upper_lanes[1].step()
    run(out_lanes, half - 3 * quarter)
    out_full = assemble(out_lanes)
    run(upper_lanes, half - 1)
    run(down_lanes, 2 * quarter)
    upper_full = assemble(upper_lanes)
    gate_pre = dot(attend_full[gate_row:], tie(normed_all, mixed_heads), 1, 1)
    centred = mixed_heads - jnp.mean(mixed_heads, axis=1, keepdims=True)
    group_scale = lax.rsqrt(jnp.mean(centred * centred, axis=1, keepdims=True) + group_floor)
    group_hat = centred * group_scale
    group_flat = group_hat.reshape(values_local, rows_total)
    group_out = group_flat * group_gain + group_bias
    gate_act, silu_pull = jax.vjp(jax.nn.silu, gate_pre)
    mixed_low = (gate_act * group_out).astype(jnp.bfloat16)
    mixed_low, grad_rows_two = tie((mixed_low, grad_rows_two), reached(out_lanes, half), reached(upper_lanes[:1], 1))
    branch_one = scatter_tokens(dot(mixed_low, out_full, 0, 0))
    middle = inputs + tie(branch_one, reached(upper_lanes, half))
    scale_two = root_scale(middle)
    normed_two = middle * scale_two
    second_all = gather_tokens((normed_two * gain_two).astype(jnp.bfloat16))
    run(down_lanes, half - 2 * quarter, second_all)
    second_all = tie(second_all, reached(down_lanes, 2 * quarter))
    down_full = assemble(down_lanes)
    hidden_gate = dot(upper_full[:hidden_local], second_all, 1, 1)
    second_late = tie(second_all, hidden_gate, reached(down_lanes, 3 * quarter))
    hidden_upper = dot(upper_full[hidden_local:], second_late, 1, 1)
    gelu_gate, gelu_pull = jax.vjp(partial(jax.nn.gelu, approximate=False), hidden_gate)
    hidden_low = (gelu_gate * hidden_upper).astype(jnp.bfloat16)

    grad_result = cotangent.astype(jnp.float32)
    rows_two_late = tie(grad_rows_two, hidden_low, reached(down_lanes, half))
    grad_down = dot(hidden_low, rows_two_late, 1, 0).astype(jnp.bfloat16)
    down_back = [Scatter(ring, grad_down, 0, hidden_local, -1)]
    run(down_back, half)
    grad_hidden = dot(down_full, tie(grad_rows_two, grad_down), 1, 1)
    grad_gate_mlp = gelu_pull(grad_hidden * hidden_upper)[0].astype(jnp.bfloat16)
    grad_upper_mlp = (grad_hidden * gelu_gate).astype(jnp.bfloat16)
    grad_hidden_low = jnp.concatenate([grad_gate_mlp, grad_upper_mlp])
    grad_hidden_low = tie(grad_hidden_low, loaded(down_back, quarter))
    grad_second = dot(grad_hidden_low, upper_full, 0, 0).astype(jnp.bfloat16)
    grad_second, grad_hidden_late = tie((grad_second, grad_hidden_low))
    grad_second_local = scatter_tokens(tie(grad_second, reached(down_back, 2 * quarter)))
    grad_hidden_late = tie(grad_hidden_late, loaded(down_back, 2 * quarter))
    grad_upper = dot(grad_hidden_late, second_all, 1, 0).astype(jnp.bfloat16)
    upper_back = scatter_lanes(ring, tie(grad_upper, reached(down_back, 3 * quarter)))
    run(upper_back, half)
    branch_two = dot(tie(hidden_low, grad_upper), down_full, 0, 0).astype(jnp.bfloat16)
    grad_second_local = tie(
        grad_second_local, reached(upper_back[:1], 2 * quarter), loaded(upper_back[1:], quarter), branch_two
    )
    grad_gain_two = jnp.sum(grad_second_local * normed_two, axis=0)
    grad_middle = grad_result + norm_back(grad_second_local * gain_two, normed_two, scale_two)
    grad_middle_low = grad_middle.astype(jnp.bfloat16)
    grad_rows_one = gather_tokens(grad_middle_low)
    branch_two = lax.psum_scatter(tie(branch_two, grad_rows_one), "tensor", scatter_dimension=0, tiled=True)
    result = middle + branch_two.astype(jnp.float32)
    grad_rows_one = tie(grad_rows_one, loaded(upper_back, 3 * quarter))
    out_back = [Scatter(ring, dot(mixed_low, grad_rows_one, 1, 0).astype(jnp.bfloat16), 0, values_local, 1)]
    run(out_back, quarter)
    grad_mixed = dot(out_full, tie(grad_rows_one, loaded(out_back, 0)), 1, 1)
    grad_gate_low = silu_pull(grad_mixed * group_out)[0].astype(jnp.bfloat16)
    gate_back = [Scatter(ring, dot(grad_gate_low, normed_all, 1, 0).astype(jnp.bfloat16), 0, values_local, -1)]
    run(gate_back, quarter)
    run(out_back + gate_back, half - quarter)
    grad_group = grad_mixed * gate_act
    grad_group_gain = jnp.sum(grad_group * group_flat, axis=1)
    grad_group_bias = jnp.sum(grad_group, axis=1)
    grad_hat = (grad_group * group_gain).reshape(heads, DV, rows_total)
    grad_heads = group_scale * (
        grad_hat
        - jnp.mean(grad_hat, axis=1, keepdims=True)
        - group_hat * jnp.mean(grad_hat * group_hat, axis=1, keepdims=True)
    )
    grad_heads = tie(grad_heads, loaded(out_back, quarter), loaded(gate_back, 0))
    waits = [None, (loaded(out_back, 2 * quarter), loaded(gate_back, quarter))]
    grad_queries, grad_keys, grad_values = retention_backward(
        query, key, value, grad_heads.astype(jnp.bfloat16), doc_ids, log_gamma, block, waits
    )
    grad_attend_low = jnp.concatenate(
        [
            grad_queries.astype(jnp.bfloat16).reshape(keys_local, rows_total),
            grad_keys.astype(jnp.bfloat16).reshape(keys_local, rows_total),
            grad_values.astype(jnp.bfloat16).reshape(values_local, rows_total),
        ]
    )
    grad_attend_low = tie(grad_attend_low, loaded(out_back, 3 * quarter))
    grad_attend = dot(grad_attend_low, normed_all, 1, 0).astype(jnp.bfloat16)
    attend_back = scatter_lanes(ring, grad_attend)
    run(attend_back, half)
    grad_down_w = totals(down_back)
    grad_upper_w = totals(upper_back)
    grad_out_w = totals(out_back)
    grad_gate_w = totals(gate_back)
    grad_attend_w = totals(attend_back)

    fresh_query = momentum_decay * key_momentum[0] + grad_attend_w[:keys_local].T
    fresh_key = momentum_decay * key_momentum[1] + grad_attend_w[keys_local : 2 * keys_local].T
    fresh_value = momentum_decay * value_momentum[0] + grad_attend_w[2 * keys_local :].T
    fresh_gate = momentum_decay * value_momentum[1] + grad_gate_w.T
    fresh_out = momentum_decay * out_momentum + grad_out_w
    fresh_hidden = momentum_decay * up_momentum[0] + grad_upper_w[:hidden_local].T
    fresh_upper = momentum_decay * up_momentum[1] + grad_upper_w[hidden_local:].T
    fresh_down = momentum_decay * down_momentum + grad_down_w
    slabs = [
        fresh_down,
        fresh_hidden.T,
        fresh_upper.T,
        fresh_out,
        fresh_gate.T,
        fresh_value.T,
        fresh_query.T,
        fresh_key.T,
    ]
    stacked = stack_slabs(slabs)
    attend_late, gate_late = tie((grad_attend_low, grad_gate_low), fresh_query, fresh_key, reached(attend_back, half))
    pieces = []
    for index in range(4):
        rows = slice(index * rows_total // 4, (index + 1) * rows_total // 4)
        piece = dot(attend_late[:, rows], attend_full[:gate_row], 0, 0)
        piece = piece + dot(gate_late[:, rows], attend_full[gate_row:], 0, 0)
        pieces.append(piece.astype(jnp.bfloat16))
    grad_first = tie(jnp.concatenate(pieces), branch_two)
    grad_first = lax.psum_scatter(grad_first, "tensor", scatter_dimension=0, tiled=True)
    owned = tie(move_slots(stacked), grad_first)
    ready = orthogonalize(owned)
    grad_first_local = tie(grad_first, ready).astype(jnp.float32)
    grad_gain_one = jnp.sum(grad_first_local * normed_one, axis=0)
    token_grad = grad_middle + norm_back(grad_first_local * gain_one, normed_one, scale_one)
    group_part = jnp.zeros((2, value_total), jnp.float32)
    group_part = lax.dynamic_update_slice_in_dim(
        group_part, jnp.stack([grad_group_gain, grad_group_bias]), tensor_index * values_local, 1
    )
    norm_sum = sum_norms(jnp.concatenate([grad_gain_one, grad_gain_two, group_part.reshape(-1)]))
    returned, norm_sum = tie((move_slots(ready), norm_sum))
    norm_place = lax.axis_index("dp") * tensor_count + tensor_index
    norm_grad = lax.dynamic_slice_in_dim(norm_sum, norm_place * own_norms, own_norms)
    returned = returned.reshape((-1,) + returned.shape[2:])
    orth = [returned[index, : slab.shape[0]].astype(jnp.float32) for index, slab in enumerate(slabs)]
    keep_factor = 1.0 - muon_rate * weight_decay

    def rate(rows, cols):
        return muon_rate * math.sqrt(max(1.0, rows / cols))

    new_key_weights = key_weights * keep_factor - rate(width, keys_local) * jnp.stack([orth[6].T, orth[7].T])
    new_value_weights = value_weights * keep_factor - rate(width, values_local) * jnp.stack([orth[5].T, orth[4].T])
    new_upper_weights = up_weights * keep_factor - rate(width, hidden_local) * jnp.stack([orth[1].T, orth[2].T])
    new_out_weights = out_weights * keep_factor - rate(values_local, width) * orth[3]
    new_down_weights = down_weights * keep_factor - rate(hidden_local, width) * orth[0]
    new_norm_first = beta_first * norm_first + (1.0 - beta_first) * norm_grad
    new_norm_second = beta_second * norm_second + (1.0 - beta_second) * norm_grad * norm_grad
    fix_first = 1.0 - beta_first**STEP
    fix_second = 1.0 - beta_second**STEP
    new_norm_params = norm_params - adam_rate * (new_norm_first / fix_first) / (
        jnp.sqrt(new_norm_second / fix_second) + adam_eps
    )
    return (
        result.astype(jnp.bfloat16),
        token_grad,
        jnp.stack([fresh_query, fresh_key]),
        jnp.stack([fresh_value, fresh_gate]),
        fresh_out,
        jnp.stack([fresh_hidden, fresh_upper]),
        fresh_down,
        new_key_weights,
        new_value_weights,
        new_out_weights,
        new_upper_weights,
        new_down_weights,
        new_norm_first,
        new_norm_second,
        new_norm_params,
    )


def solution(mesh):
    tokens = P(("dp", "tensor"), None)
    wide = P(None, "dp", "tensor")
    tall = P("tensor", "dp")
    norms = P(("dp", "tensor"))
    return jax.shard_map(
        per_device,
        mesh=mesh,
        in_specs=(
            tokens, tokens, P("dp", None), wide, wide, tall, wide, tall,
            wide, wide, tall, wide, tall, norms, norms, norms,
        ),
        out_specs=(
            tokens, tokens, wide, wide, tall, wide, tall,
            wide, wide, tall, wide, tall, norms, norms, norms,
        ),
        check_vma=False,
    )
```

```python
from functools import partial
import math

import jax
import jax.numpy as jnp
from jax import lax
from jax.experimental import pallas as pl
from jax.experimental.pallas import tpu as pltpu
from jax.sharding import PartitionSpec as P

H = 8
KEY_HEAD_SIZE = 256
DV = 432
LEN = 1024
NS_ITERS = 5
STEP = 10


eps_norm = 1e-05
group_floor = 1.0
ns_first = 3.4445
ns_second = -4.775
ns_third = 2.0315
momentum_decay = 0.95
muon_rate = 0.5
weight_decay = 0.1
beta_first = 0.9
beta_second = 0.95
adam_rate = 0.8
adam_eps = 1e-08
TILE = 1024


def root_scale(values):
    return lax.rsqrt(jnp.mean(values * values, axis=-1, keepdims=True) + eps_norm)


def norm_back(grad_normed, normed, scaling):
    return scaling * (grad_normed - normed * jnp.mean(grad_normed * normed, axis=-1, keepdims=True))


def dot(left, right, left_dim, right_dim):
    return lax.dot_general(
        left, right, (((left_dim,), (right_dim,)), ((), ())), preferred_element_type=jnp.float32
    )


def gather_tokens(values):
    return lax.all_gather(values, "tensor", axis=0, tiled=True)


def scatter_tokens(values):
    return lax.psum_scatter(
        values.astype(jnp.bfloat16), "tensor", scatter_dimension=0, tiled=True
    ).astype(jnp.float32)


def ring_order(count):
    return list(range(0, count, 2)) + list(range(count - 1, 0, -2))


def ring_place(count):
    order = ring_order(count)
    return order, [(order[i], order[(i + 1) % count]) for i in range(count)]


def tie(value, *others):
    return lax.optimization_barrier((value, others))[0]


class Ring:
    def __init__(self):
        self.count = lax.axis_size("dp")
        order, self.right = ring_place(self.count)
        self.left = [(b, a) for a, b in self.right]
        self.half = self.count // 2
        place_of = [order.index(rank) for rank in range(self.count)]
        place = jnp.asarray(place_of, jnp.int32)[lax.axis_index("dp")]
        steps = jnp.arange(self.count, dtype=jnp.int32)
        self.rank_at = jnp.asarray(order, jnp.int32)[(place + steps) % self.count]
        self.sent = []
        self.added = None

    def rank(self, distance):
        return self.rank_at[distance % self.count]

    def exchange(self, blocks):
        if len(self.sent) > 2:
            blocks = tie(blocks, self.sent[-3])
        got = {}
        for side, block in blocks.items():
            got[side] = lax.ppermute(block, "dp", self.right if side > 0 else self.left)
        self.sent.append(got)
        return got


class Gather:
    def __init__(self, ring, shard, long_side):
        self.ring = ring
        self.shard = shard
        self.long_side = long_side
        self.rows, self.width = shard.shape
        self.blocks = [(shard, 0)]
        self.held = {1: shard, -1: shard}
        self.marks = []

    def step(self, after=None):
        at = len(self.marks) + 1
        sides = (1, -1) if at < self.ring.half else (self.long_side,)
        blocks = {side: self.held[side] for side in sides}
        if after is not None:
            blocks = tie(blocks, after)
        self.held = self.ring.exchange(blocks)
        self.blocks += [(self.held[side], -side * at) for side in sides]
        self.marks.append(self.held)


def run(lanes, rounds):
    for _ in range(rounds):
        for lane in lanes:
            lane.step()


def reached(lanes, rounds):
    return [lane.marks[rounds - 1] for lane in lanes]


def loaded(lanes, rounds):
    return [lane.loads[rounds] for lane in lanes]


def nothing_kernel(out_ref):
    pass


def unwritten(shape, dtype):
    return pl.pallas_call(
        nothing_kernel,
        out_shape=jax.ShapeDtypeStruct(shape, dtype),
        out_specs=pl.BlockSpec(memory_space=pl.ANY),
    )()


def assemble(lanes):
    ring = lanes[0].ring
    width = lanes[0].width
    full = unwritten((sum(lane.rows for lane in lanes), width * ring.count), lanes[0].shard.dtype)
    placed, base = [], 0
    for lane in lanes:
        lane.blocks[0] = tie(lane.shard, lane.marks[0]), 0
        placed += [(index, base, block, distance) for index, (block, distance) in enumerate(lane.blocks)]
        base += lane.rows
    for _, row, block, distance in sorted(placed, key=lambda item: item[0]):
        full = lax.dynamic_update_slice(full, block, (row, ring.rank(distance) * width))
    return full


class Scatter:
    def __init__(self, ring, full, first, rows, long_side):
        self.ring = ring
        self.full = full
        self.first = first
        self.rows = rows
        self.long_side = long_side
        self.width = full.shape[1] // ring.count
        self.held = {}
        self.marks = []
        self.loads = []

    def piece(self, distance):
        column = self.ring.rank(distance) * self.width
        return lax.dynamic_slice(self.full, (self.first, column), (self.rows, self.width))

    def step(self, ready=None):
        ring = self.ring
        at = ring.half - len(self.marks)
        came = self.held
        if came and ring.added is not None:
            came = tie(came, ring.added)
        sides = (1, -1) if at < ring.half else (self.long_side,)
        blocks = {}
        for side in sides:
            block = self.piece(side * at)
            if side in came:
                block = (block.astype(jnp.float32) + came[side].astype(jnp.float32)).astype(jnp.bfloat16)
            blocks[side] = block
        if came:
            ring.added = blocks
        if ready is not None:
            blocks, ready = tie((blocks, ready))
        self.loads.append(blocks)
        self.held = ring.exchange(blocks)
        self.marks.append(self.held)
        return ready

    def total(self):
        own = self.piece(0).astype(jnp.float32)
        return own + self.held[1].astype(jnp.float32) + self.held[-1].astype(jnp.float32)


def halves(rows):
    cut = (rows // 2 + 15) // 16 * 16
    return [(0, cut, 1), (cut, rows - cut, -1)]


def gather_lanes(ring, shard):
    return [Gather(ring, shard[first : first + size], side) for first, size, side in halves(shard.shape[0])]


def scatter_lanes(ring, full):
    return [Scatter(ring, full, first, size, side) for first, size, side in halves(full.shape[0])]


def totals(lanes):
    return jnp.concatenate([lane.total() for lane in lanes])


def decay_rows(doc_ids, log_gamma, first, size, keys):
    query_pos = first + jnp.arange(size)
    key_pos = jnp.arange(keys)
    distance = query_pos[:, None] - key_pos[None, :]
    allowed = (doc_ids[first : first + size, None] == doc_ids[None, :keys]) & (distance >= 0)
    steps_back = jnp.maximum(distance, 0).astype(jnp.float32)
    falloff = jnp.exp(log_gamma[:, None, None] * steps_back[None])
    return jnp.where(allowed[None], falloff, 0.0)


def einsum32(spec, left, right):
    return jnp.einsum(spec, left, right, preferred_element_type=jnp.float32)


def retention_forward(query, key, value, doc_ids, log_gamma, block):
    factor = KEY_HEAD_SIZE ** (-0.5)
    pieces = []
    for first in range(0, LEN, block):
        keys = first + block
        falloff = decay_rows(doc_ids, log_gamma, first, block, keys)
        scores = einsum32("hdq,hdk->hqk", query[:, :, first:keys], key[:, :, :keys]) * factor
        weights = (scores * falloff).astype(jnp.bfloat16)
        pieces.append(einsum32("hdk,hqk->hdq", value[:, :, :keys], weights))
    return jnp.concatenate(pieces, axis=2)


def retention_backward(query, key, value, grad, doc_ids, log_gamma, block, waits):
    factor = KEY_HEAD_SIZE ** (-0.5)
    grad_query = []
    grad_key = jnp.zeros(key.shape, jnp.float32)
    grad_value = jnp.zeros(value.shape, jnp.float32)
    for first in range(0, LEN, block):
        keys = first + block
        falloff = decay_rows(doc_ids, log_gamma, first, block, keys)
        query_now, grad_now = query[:, :, first:keys], grad[:, :, first:keys]
        if waits[first // block] is not None:
            grad_now = tie(grad_now, waits[first // block])
        scores = einsum32("hdq,hdk->hqk", query_now, key[:, :, :keys]) * factor
        weights = (scores * falloff).astype(jnp.bfloat16)
        grad_weights = einsum32("hdq,hdk->hqk", grad_now, value[:, :, :keys])
        grad_scores = (grad_weights * falloff).astype(jnp.bfloat16)
        grad_query.append(einsum32("hdk,hqk->hdq", key[:, :, :keys], grad_scores) * factor)
        grad_key = grad_key.at[:, :, :keys].add(einsum32("hdq,hqk->hdk", query_now, grad_scores) * factor)
        grad_value = grad_value.at[:, :, :keys].add(einsum32("hdq,hqk->hdk", grad_now, weights))
    return jnp.concatenate(grad_query, axis=2), grad_key, grad_value


def mirror(ref, block, first, wide):
    ref[first:, first : first + wide] = block
    if block.shape[0] > wide:
        ref[first : first + wide, first + wide :] = block[wide:].T


def newton_schulz_kernel(turns, step, in_ref, out_ref, cur_ref, low_ref, rest_ref, poly_ref, scale_ref):
    parts, size, cols = in_ref.shape
    width = parts * cols
    band = 256
    blocks = size // step

    def rows_of(index):
        return pl.ds(pl.multiple_of(index * step, step), step)

    def first_sum(index, total):
        rows = rows_of(index)
        for part in range(parts):
            block = in_ref[part, rows, :].astype(jnp.float32)
            total = total + jnp.sum(block * block)
        return total

    total = lax.fori_loop(0, blocks, first_sum, jnp.float32(0.0))
    scale_ref[...] = 1.0 / (jnp.sqrt(jnp.full(scale_ref.shape, total)) + 1e-07)

    @pl.loop(0, blocks)
    def _(index):
        rows = rows_of(index)
        scale = scale_ref[0, 0]
        for part in range(parts):
            block = in_ref[part, rows, :].astype(jnp.float32) * scale
            columns = pl.ds(part * cols, cols)
            cur_ref[rows, columns] = block
            low_ref[0, rows, columns] = block.astype(jnp.bfloat16)

    bands = [(first, min(256, size - first)) for first in range(0, size, 256)]

    def turn_body(turn, norm, last):
        here = lax.rem(turn, 2)
        there = 1 - here
        middle = norm * (1.0 / size)
        low = low_ref.at[here]
        for first, wide in bands:
            gram = dot(low[first:, :], low[first : first + wide, :], 1, 1)
            place = lax.broadcasted_iota(jnp.int32, gram.shape, 0)
            eye = place == lax.broadcasted_iota(jnp.int32, gram.shape, 1)
            mirror(rest_ref, jnp.where(eye, gram - middle, gram).astype(jnp.bfloat16), first, wide)
        for first, wide in bands:
            square = dot(rest_ref[first:, :], rest_ref[:, first : first + wide], 1, 0)
            rest = rest_ref[first:, first : first + wide].astype(jnp.float32)
            poly = (ns_second + 2.0 * ns_third * middle) * rest + ns_third * square
            mirror(poly_ref, poly.astype(jnp.bfloat16), first, wide)
        outer = ns_first + middle * (ns_second + ns_third * middle)

        total = jnp.zeros((1, band), jnp.float32)
        for first in range(0, width, band):
            columns = slice(first, first + band)
            fresh = outer * cur_ref[:, columns] + dot(poly_ref[...], low[:, columns], 1, 0)
            if last:
                out_ref[first // cols, :, first % cols : first % cols + band] = fresh.astype(jnp.bfloat16)
            else:
                cur_ref[:, columns] = fresh
                low_ref[there, :, columns] = fresh.astype(jnp.bfloat16)
                total = total + jnp.sum(fresh * fresh, axis=0, keepdims=True)
        return jnp.sum(total)

    norm = lax.fori_loop(0, turns - 1, lambda turn, norm: turn_body(turn, norm, False), jnp.float32(1.0))
    turn_body(turns - 1, norm, True)


def newton_schulz(block):
    parts, size, cols = block.shape
    width = parts * cols
    step = next(step for step in range(288, 0, -16) if size % step == 0)
    products = 2 * size * size * (2 * width + size) * NS_ITERS
    return pl.pallas_call(
        partial(newton_schulz_kernel, NS_ITERS, step),
        out_shape=jax.ShapeDtypeStruct(block.shape, jnp.bfloat16),
        in_specs=[pl.BlockSpec(memory_space=pltpu.VMEM)],
        out_specs=pl.BlockSpec(memory_space=pltpu.VMEM),
        scratch_shapes=[
            pltpu.VMEM((size, width), jnp.float32),
            pltpu.VMEM((2, size, width), jnp.bfloat16),
            pltpu.VMEM((size, size), jnp.bfloat16),
            pltpu.VMEM((size, size), jnp.bfloat16),
            pltpu.VMEM((8, 128), jnp.float32),
        ],
        compiler_params=pltpu.CompilerParams(vmem_limit_bytes=48 * 1024 * 1024),
        cost_estimate=pl.CostEstimate(flops=products, bytes_accessed=4 * size * width, transcendentals=0),
    )(block)


def slots_for(count, rows, cols):
    ranks = lax.axis_size("dp")
    total = ranks * ((count + ranks - 1) // ranks)
    if total > count:
        return jnp.zeros((total, rows, cols), jnp.bfloat16)
    return unwritten((total, rows, cols), jnp.bfloat16)


def fill_slots(slots, first, slabs):
    for index, slab in enumerate(slabs):
        low = jnp.pad(slab.astype(jnp.bfloat16), ((0, slots.shape[1] - slab.shape[0]), (0, 0)))
        slots = lax.dynamic_update_slice(slots, low[None], (first + index, 0, 0))
    return slots


def move_slots(stacked):
    return lax.all_to_all(stacked, "dp", 0, 0, tiled=True)


def orthogonalize(owned):
    ranks, each, widest, cols = owned.shape
    done = []
    for index in range(each):
        mine = owned[:, index]
        if cols % 128:
            mine = jnp.moveaxis(mine, 0, 1).reshape(1, widest, ranks * cols)
        item = newton_schulz(mine)
        if cols % 128:
            item = jnp.moveaxis(item.reshape(widest, ranks, cols), 1, 0)
        done.append(item)
    return jnp.stack(done, axis=1)


def gather_small(piece, axis):
    count = lax.axis_size(axis)
    index = lax.axis_index(axis)
    held = piece
    bit = 1
    while bit < count:
        came = lax.ppermute(held, axis, [(i, i ^ bit) for i in range(count)])
        mine = (index // bit) % 2
        start = (0,) * held.ndim
        both = jnp.zeros((2,) + held.shape, held.dtype)
        both = lax.dynamic_update_slice(both, held[None], (mine,) + start)
        held = lax.dynamic_update_slice(both, came[None], (1 - mine,) + start)
        bit *= 2
    return held.reshape((count,) + piece.shape), came


def sum_norms(terms):
    for axis in ("tensor", "dp"):
        count = lax.axis_size(axis)
        bit = 1
        while bit < count:
            terms = terms + lax.ppermute(terms, axis, [(i, i ^ bit) for i in range(count)])
            bit *= 2
    return terms


def per_device(
    tokens,
    cotangent,
    doc_lengths,
    key_weights,
    value_weights,
    out_weights,
    up_weights,
    down_weights,
    key_momentum,
    value_momentum,
    out_momentum,
    up_momentum,
    down_momentum,
    norm_params,
    norm_first,
    norm_second,
):
    tensor_count = lax.axis_size("tensor")
    tensor_index = lax.axis_index("tensor")
    heads = H // tensor_count
    width = tokens.shape[1]
    keys_local = key_weights.shape[2]
    values_local = value_weights.shape[2]
    hidden_local = up_weights.shape[2]
    value_total = values_local * tensor_count
    block = min(LEN, 512)
    ring = Ring()
    half = ring.half
    quarter = half // 4

    def low_t(matrix):
        return matrix.astype(jnp.bfloat16).T

    attend_lanes = gather_lanes(
        ring,
        jnp.concatenate(
            [low_t(key_weights[0]), low_t(key_weights[1]), low_t(value_weights[0]), low_t(value_weights[1])]
        ),
    )
    out_lanes = [Gather(ring, out_weights.astype(jnp.bfloat16), 1)]
    upper_lanes = gather_lanes(ring, jnp.concatenate([low_t(up_weights[0]), low_t(up_weights[1])]))
    down_lanes = [Gather(ring, down_weights.astype(jnp.bfloat16), -1)]
    tokens_all = gather_tokens(tokens)
    own_norms = norm_params.shape[0]
    filled_norms = TILE * ((own_norms + TILE - 1) // TILE)
    norm_piece = jnp.pad(norm_params, (0, filled_norms - own_norms)).reshape(filled_norms // 128, 128)
    norm_group, _ = gather_small(norm_piece, "tensor")
    attend_lanes[0].step()
    attend_lanes[1].step()
    gathered_norms, last_norms = gather_small(tie(norm_group, reached(attend_lanes[:1], 1)), "dp")
    attend_lanes[0].step(last_norms)
    attend_lanes[1].step()
    gathered_norms = gathered_norms.reshape(-1, filled_norms)[:, :own_norms].reshape(-1)

    gain_one = gathered_norms[:width]
    gain_two = gathered_norms[width : 2 * width]
    group_gain = lax.dynamic_slice_in_dim(
        gathered_norms, 2 * width + tensor_index * values_local, values_local
    )[:, None]
    group_bias = lax.dynamic_slice_in_dim(
        gathered_norms, 2 * width + value_total + tensor_index * values_local, values_local
    )[:, None]
    lengths = tie(doc_lengths[0], reached(attend_lanes, 1))
    starts_all = jnp.cumsum(lengths) - lengths
    positions = jnp.arange(LEN)
    doc_ids = jnp.sum((positions[:, None] >= starts_all[None, :]).astype(jnp.int32), axis=1) - 1

    inputs = tokens.astype(jnp.float32)
    scale_one = root_scale(inputs)
    normed_one = inputs * scale_one
    inputs_all = tokens_all.astype(jnp.float32)
    normed_all = (inputs_all * root_scale(inputs_all) * gain_one).astype(jnp.bfloat16)
    rows_total = normed_all.shape[0]
    grad_rows_two = gather_tokens(tie(cotangent, tokens_all))
    attend_lanes[0].step(normed_all)
    attend_lanes[1].step()
    run(attend_lanes, half - 3)
    run(out_lanes, quarter)
    attend_full = assemble(attend_lanes)

    gate_row = 2 * keys_local + values_local
    attend = dot(attend_full[:gate_row], normed_all, 1, 1).astype(jnp.bfloat16)
    attend = tie(attend, reached(out_lanes, quarter))
    out_lanes[0].step(attend)
    run(out_lanes, quarter - 1)
    upper_lanes[0].step()
    query = attend[:keys_local].reshape(heads, KEY_HEAD_SIZE, rows_total)
    key = attend[keys_local : 2 * keys_local].reshape(heads, KEY_HEAD_SIZE, rows_total)
    value = attend[2 * keys_local :].reshape(heads, DV, rows_total)
    head_ids = (tensor_index * heads + jnp.arange(heads)).astype(jnp.float32)
    log_gamma = jnp.log(1.0 - jnp.exp2(-5.0 - head_ids))
    mixed_heads = retention_forward(query, key, value, doc_ids, log_gamma, block)
    mixed_heads = tie(mixed_heads, reached(out_lanes, 2 * quarter))
    run(out_lanes, quarter)
    upper_lanes[1].step()
    run(out_lanes, half - 3 * quarter)
    out_full = assemble(out_lanes)
    run(upper_lanes, half - 1)
    run(down_lanes, 2 * quarter)
    upper_full = assemble(upper_lanes)
    gate_pre = dot(attend_full[gate_row:], tie(normed_all, mixed_heads), 1, 1)
    centred = mixed_heads - jnp.mean(mixed_heads, axis=1, keepdims=True)
    group_scale = lax.rsqrt(jnp.mean(centred * centred, axis=1, keepdims=True) + group_floor)
    group_hat = centred * group_scale
    group_flat = group_hat.reshape(values_local, rows_total)
    group_out = group_flat * group_gain + group_bias
    gate_act, silu_pull = jax.vjp(jax.nn.silu, gate_pre)
    mixed_low = (gate_act * group_out).astype(jnp.bfloat16)
    mixed_low, grad_rows_two = tie((mixed_low, grad_rows_two), reached(out_lanes, half), reached(upper_lanes[:1], 1))
    branch_one = scatter_tokens(dot(mixed_low, out_full, 0, 0))
    middle = inputs + tie(branch_one, reached(upper_lanes, half))
    scale_two = root_scale(middle)
    normed_two = middle * scale_two
    second_all = gather_tokens((normed_two * gain_two).astype(jnp.bfloat16))
    down_lanes[0].step(second_all)
    run(down_lanes, half - 2 * quarter - 1)
    second_all = tie(second_all, reached(down_lanes, 2 * quarter))
    down_full = assemble(down_lanes)
    hidden_gate = dot(upper_full[:hidden_local], second_all, 1, 1)
    second_late = tie(second_all, hidden_gate, reached(down_lanes, 3 * quarter))
    hidden_upper = dot(upper_full[hidden_local:], second_late, 1, 1)
    gelu_gate, gelu_pull = jax.vjp(partial(jax.nn.gelu, approximate=False), hidden_gate)
    hidden_low = (gelu_gate * hidden_upper).astype(jnp.bfloat16)

    grad_result = cotangent.astype(jnp.float32)
    rows_two_late = tie(grad_rows_two, hidden_low, reached(down_lanes, half))
    grad_down = dot(hidden_low, rows_two_late, 1, 0).astype(jnp.bfloat16)
    down_back = [Scatter(ring, grad_down, 0, hidden_local, -1)]
    run(down_back, half)
    grad_hidden = dot(down_full, tie(grad_rows_two, grad_down), 1, 1)
    grad_gate_mlp = gelu_pull(grad_hidden * hidden_upper)[0].astype(jnp.bfloat16)
    grad_upper_mlp = (grad_hidden * gelu_gate).astype(jnp.bfloat16)
    grad_hidden_low = jnp.concatenate([grad_gate_mlp, grad_upper_mlp])
    grad_hidden_low = tie(grad_hidden_low, loaded(down_back, quarter))
    grad_second = dot(grad_hidden_low, upper_full, 0, 0).astype(jnp.bfloat16)
    grad_second, grad_hidden_late = tie((grad_second, grad_hidden_low))
    grad_second_local = scatter_tokens(tie(grad_second, reached(down_back, 2 * quarter)))
    grad_hidden_late = tie(grad_hidden_late, loaded(down_back, 2 * quarter))
    grad_upper = dot(grad_hidden_late, second_all, 1, 0).astype(jnp.bfloat16)
    upper_back = scatter_lanes(ring, tie(grad_upper, reached(down_back, 3 * quarter)))
    run(upper_back, half)
    branch_two = dot(tie(hidden_low, grad_upper), down_full, 0, 0).astype(jnp.bfloat16)
    grad_second_local = tie(
        grad_second_local, reached(upper_back[:1], 2 * quarter), loaded(upper_back[1:], quarter), branch_two
    )
    grad_gain_two = jnp.sum(grad_second_local * normed_two, axis=0)
    grad_middle = grad_result + norm_back(grad_second_local * gain_two, normed_two, scale_two)
    grad_middle_low = grad_middle.astype(jnp.bfloat16)
    grad_rows_one = gather_tokens(grad_middle_low)
    branch_two = lax.psum_scatter(tie(branch_two, grad_rows_one), "tensor", scatter_dimension=0, tiled=True)
    result = middle + branch_two.astype(jnp.float32)
    grad_rows_one = tie(grad_rows_one, loaded(upper_back, 3 * quarter))
    out_back = [Scatter(ring, dot(mixed_low, grad_rows_one, 1, 0).astype(jnp.bfloat16), 0, values_local, 1)]
    run(out_back, quarter)
    grad_mixed = dot(out_full, tie(grad_rows_one, loaded(out_back, 0)), 1, 1)
    grad_gate_low = silu_pull(grad_mixed * group_out)[0].astype(jnp.bfloat16)
    gate_back = [Scatter(ring, dot(grad_gate_low, normed_all, 1, 0).astype(jnp.bfloat16), 0, values_local, -1)]
    run(gate_back, quarter)
    run(out_back + gate_back, half - quarter)
    grad_group = grad_mixed * gate_act
    grad_group_gain = jnp.sum(grad_group * group_flat, axis=1)
    grad_group_bias = jnp.sum(grad_group, axis=1)
    grad_hat = (grad_group * group_gain).reshape(heads, DV, rows_total)
    grad_heads = group_scale * (
        grad_hat
        - jnp.mean(grad_hat, axis=1, keepdims=True)
        - group_hat * jnp.mean(grad_hat * group_hat, axis=1, keepdims=True)
    )
    grad_heads = tie(grad_heads, loaded(out_back, quarter), loaded(gate_back, 0))
    waits = [None, (loaded(out_back, 2 * quarter), loaded(gate_back, quarter))]
    grad_queries, grad_keys, grad_values = retention_backward(
        query, key, value, grad_heads.astype(jnp.bfloat16), doc_ids, log_gamma, block, waits
    )
    grad_attend_low = jnp.concatenate(
        [
            grad_queries.astype(jnp.bfloat16).reshape(keys_local, rows_total),
            grad_keys.astype(jnp.bfloat16).reshape(keys_local, rows_total),
            grad_values.astype(jnp.bfloat16).reshape(values_local, rows_total),
        ]
    )
    grad_attend_low = tie(grad_attend_low, loaded(out_back, 3 * quarter))
    grad_attend = dot(grad_attend_low, normed_all, 1, 0).astype(jnp.bfloat16)
    attend_back = scatter_lanes(ring, grad_attend)
    run(attend_back, half - 1)
    grad_down_w = totals(down_back)
    grad_upper_w = totals(upper_back)
    grad_out_w = totals(out_back)
    grad_gate_w = totals(gate_back)
    fresh_gate = momentum_decay * value_momentum[1] + grad_gate_w.T
    fresh_out = momentum_decay * out_momentum + grad_out_w
    fresh_hidden = momentum_decay * up_momentum[0] + grad_upper_w[:hidden_local].T
    fresh_upper = momentum_decay * up_momentum[1] + grad_upper_w[hidden_local:].T
    fresh_down = momentum_decay * down_momentum + grad_down_w
    early_slabs = [fresh_down, fresh_hidden.T, fresh_upper.T, fresh_out, fresh_gate.T]
    slots = slots_for(8, max(keys_local, values_local, hidden_local), fresh_down.shape[1])
    slots = fill_slots(slots, 0, early_slabs)
    attend_back[0].step()
    slots = attend_back[1].step(slots)
    grad_attend_w = totals(attend_back)
    fresh_query = momentum_decay * key_momentum[0] + grad_attend_w[:keys_local].T
    fresh_key = momentum_decay * key_momentum[1] + grad_attend_w[keys_local : 2 * keys_local].T
    fresh_value = momentum_decay * value_momentum[0] + grad_attend_w[2 * keys_local :].T
    late_slabs = [fresh_value.T, fresh_query.T, fresh_key.T]
    slabs = early_slabs + late_slabs
    slots = fill_slots(slots, len(early_slabs), late_slabs)
    slots, attend_late, gate_late = tie((slots, grad_attend_low, grad_gate_low))
    ranks = lax.axis_size("dp")
    stacked = slots.reshape((ranks, slots.shape[0] // ranks) + slots.shape[1:])
    pieces = []
    for index in range(4):
        rows = slice(index * rows_total // 4, (index + 1) * rows_total // 4)
        piece = dot(attend_late[:, rows], attend_full[:gate_row], 0, 0)
        piece = piece + dot(gate_late[:, rows], attend_full[gate_row:], 0, 0)
        pieces.append(piece.astype(jnp.bfloat16))
    owned, grad_first = tie((move_slots(stacked), jnp.concatenate(pieces)))
    grad_first = tie(grad_first, branch_two)
    grad_first = lax.psum_scatter(grad_first, "tensor", scatter_dimension=0, tiled=True)
    ready = orthogonalize(owned)
    grad_first_local = tie(grad_first, ready).astype(jnp.float32)
    grad_gain_one = jnp.sum(grad_first_local * normed_one, axis=0)
    token_grad = grad_middle + norm_back(grad_first_local * gain_one, normed_one, scale_one)
    group_part = jnp.zeros((2, value_total), jnp.float32)
    group_part = lax.dynamic_update_slice_in_dim(
        group_part, jnp.stack([grad_group_gain, grad_group_bias]), tensor_index * values_local, 1
    )
    norm_sum = sum_norms(jnp.concatenate([grad_gain_one, grad_gain_two, group_part.reshape(-1)]))
    returned, norm_sum = tie((move_slots(ready), norm_sum))
    norm_place = lax.axis_index("dp") * tensor_count + tensor_index
    norm_grad = lax.dynamic_slice_in_dim(norm_sum, norm_place * own_norms, own_norms)
    returned = returned.reshape((-1,) + returned.shape[2:])
    orth = [returned[index, : slab.shape[0]].astype(jnp.float32) for index, slab in enumerate(slabs)]
    keep_factor = 1.0 - muon_rate * weight_decay

    def rate(rows, cols):
        return muon_rate * math.sqrt(max(1.0, rows / cols))

    new_key_weights = key_weights * keep_factor - rate(width, keys_local) * jnp.stack([orth[6].T, orth[7].T])
    new_value_weights = value_weights * keep_factor - rate(width, values_local) * jnp.stack([orth[5].T, orth[4].T])
    new_upper_weights = up_weights * keep_factor - rate(width, hidden_local) * jnp.stack([orth[1].T, orth[2].T])
    new_out_weights = out_weights * keep_factor - rate(values_local, width) * orth[3]
    new_down_weights = down_weights * keep_factor - rate(hidden_local, width) * orth[0]
    new_norm_first = beta_first * norm_first + (1.0 - beta_first) * norm_grad
    new_norm_second = beta_second * norm_second + (1.0 - beta_second) * norm_grad * norm_grad
    fix_first = 1.0 - beta_first**STEP
    fix_second = 1.0 - beta_second**STEP
    new_norm_params = norm_params - adam_rate * (new_norm_first / fix_first) / (
        jnp.sqrt(new_norm_second / fix_second) + adam_eps
    )
    return (
        result.astype(jnp.bfloat16),
        token_grad,
        jnp.stack([fresh_query, fresh_key]),
        jnp.stack([fresh_value, fresh_gate]),
        fresh_out,
        jnp.stack([fresh_hidden, fresh_upper]),
        fresh_down,
        new_key_weights,
        new_value_weights,
        new_out_weights,
        new_upper_weights,
        new_down_weights,
        new_norm_first,
        new_norm_second,
        new_norm_params,
    )


def solution(mesh):
    tokens = P(("dp", "tensor"), None)
    wide = P(None, "dp", "tensor")
    tall = P("tensor", "dp")
    norms = P(("dp", "tensor"))
    return jax.shard_map(
        per_device,
        mesh=mesh,
        in_specs=(
            tokens, tokens, P("dp", None), wide, wide, tall, wide, tall,
            wide, wide, tall, wide, tall, norms, norms, norms,
        ),
        out_specs=(
            tokens, tokens, wide, wide, tall, wide, tall,
            wide, wide, tall, wide, tall, norms, norms, norms,
        ),
        check_vma=False,
    )
```
